128 devices in a mesh: img: 16 (over z, y), tile: 8 (over x, core).
Axes of the slice: x: 4, y: 4, z: 4, core: 2. Of those that a mesh axis runs over, the one named last changes fastest.
Arguments:
- spins: float32 [16, 3, 16, 256, 256], P('img', None, None, 'tile'), may hold values from -4.5 to 4.5
- aniso: float32 [16, 256, 256], P(None, 'tile'), may hold values from 0.2 to 2
Outputs:
- path: float32 [16, 3, 16, 256, 256], P('img', None, None, 'tile')
The draws below stay inside these ranges and needn't reach their ends.
All inputs are finite; a program needn't handle non-finite values.
Results may differ from the reference program's by a relative error of at most 0.0003.
Values sent between devices are 32-bit elements; how exact they have to be, the bound alone decides.
No kernel may reach another device: no remote copies, remote signals or barrier semaphores. Data moves between devices by JAX's collectives and lax.ppermute only.
A program may use at most 128 MiB of HBM per device.

```python
import math
import jax
import jax.numpy as jnp
from jax import lax

NY = 256
NZ = 16
OUTER = 2
INNER = 3
IMAGES = 16
NX = 256


def draw_spins(key, part):
    noise_key = jax.random.fold_in(key, 11)
    frac_img = jnp.arange(IMAGES, dtype=jnp.float32) / (IMAGES - 1)
    frac_cell = jnp.arange(NX, dtype=jnp.float32) / (NX - 1)
    angles = jnp.pi * frac_img
    select = jnp.arange(3)
    base_dir = jnp.where(select[None, :] == 0, jnp.sin(angles)[:, None], jnp.where(select[None, :] == 2, jnp.cos(angles)[:, None], 0.0))
    base_dir = base_dir[:, :, None, None, None]
    amplitude = 0.15 * (3.0 ** frac_img)[:, None, None, None, None] * (3.0 ** frac_cell)[None, None, None, :, None]
    shape = (IMAGES, 3, NZ, NX, NY)
    noise = jnp.clip(jax.random.normal(noise_key, shape, jnp.float32), -2.5, 2.5)
    return (base_dir + amplitude * noise).astype(jnp.float32)


def shard_levels(rng, extent, split, low, top_value):
    factor_of, own = 1.0, jax.random.fold_in(rng, 6)
    for position, parts in split:
        heights = jnp.exp(jax.random.uniform(jax.random.fold_in(own, position), (parts,), jnp.float32, low / len(split), top_value / len(split)))
        factor_of = factor_of * jnp.repeat(heights, extent[position] // parts).reshape([-1 if axis == position else 1 for axis in range(len(extent))])
    return factor_of


def setup_inputs(seed: int = 0) -> dict:
    splits = jax.random.split(jax.random.key(seed), 3)
    return {
        "spins": draw_spins(jax.random.fold_in(splits[2], 71), 0),
        "aniso": jnp.clip(jnp.exp(math.log(2.0) - 2.3025851 * jax.random.uniform(splits[1], (NZ, NX, NY), jnp.float32) ** shard_levels(splits[1], (NZ, NX, NY), ((1, 8),), -0.2, 0.2)), 0.2, 2.0),
    }


exchange_coef = 1.0
cubic_coef = 0.5
spring_coef = 20.0
step_scale = 0.25
epsilon = 1e-06

def laplace(field):
    widths = [(0, 0)] * (field.ndim - 4) + [(0, 0), (1, 1), (0, 0), (1, 1)]
    padded = jnp.pad(field, widths)
    centre = padded[..., 1:-1, 1:-1, 1:-1]
    beside_all = padded[..., 2:, 1:-1, 1:-1] + padded[..., :-2, 1:-1, 1:-1]
    beside_all = beside_all + padded[..., 1:-1, 2:, 1:-1] + padded[..., 1:-1, :-2, 1:-1]
    beside_all = beside_all + padded[..., 1:-1, 1:-1, 2:] + padded[..., 1:-1, 1:-1, :-2]
    return beside_all - 6.0 * centre

def axis_select():
    return (jnp.arange(3) == 2).astype(jnp.float32)[:, None, None, None]

def force_field(middle_ext, coefs):
    middle = middle_ext[..., 1:-1, :]
    square_norm = lax.optimization_barrier(jnp.sum(middle * middle, axis=-4, keepdims=True))
    return exchange_coef * laplace(middle_ext) + coefs * middle * axis_select() - cubic_coef * (square_norm - 1.0) * middle

def hessian_point(middle, vector, coefs):
    square_norm = lax.optimization_barrier(jnp.sum(middle * middle, axis=-4, keepdims=True))
    projected = lax.optimization_barrier(jnp.sum(middle * vector, axis=-4, keepdims=True))
    return coefs * vector * axis_select() - cubic_coef * ((square_norm - 1.0) * vector + 2.0 * middle * projected)

def pad_x(field):
    widths = [(0, 0)] * (field.ndim - 2) + [(1, 1), (0, 0)]
    return jnp.pad(field, widths)

def reference(spins, aniso):
    images = spins.shape[0]
    cell_count = float(spins.size)
    image_index = jnp.arange(images, dtype=jnp.int32)
    segment_live = (image_index < images - 1).astype(jnp.float32)
    interior = ((image_index > 0) & (image_index < images - 1)).astype(jnp.float32)
    target = image_index.astype(jnp.float32) / (images - 1)
    current = spins
    for outer_step in range(OUTER):
        after_img = jnp.concatenate([current[1:], jnp.zeros_like(current[:1])])
        before_img = jnp.concatenate([jnp.zeros_like(current[:1]), current[:-1]])

        def segment_stats(couple):
            own_img, next_img = couple
            middle = 0.5 * (own_img + next_img)
            drive_own = force_field(pad_x(middle), aniso)
            difference = next_img - own_img
            return (jnp.sum(difference * difference), jnp.sum(drive_own * drive_own))
        diff_sq, drive_sq = lax.map(segment_stats, (current, after_img))
        seg_len = segment_live * jnp.sqrt(diff_sq + epsilon)
        drive_len = segment_live * jnp.sqrt(drive_sq + epsilon)
        path_len = jnp.sum(seg_len)
        time_step = path_len / jnp.sum(drive_len)
        arc_share = jnp.concatenate([jnp.zeros((1,), jnp.float32), jnp.cumsum(seg_len)[:-1]]) / path_len
        spring_pull = spring_coef * (arc_share - target) * (images - 1) / (2.0 * path_len)

        def gradient(bundle):
            before_k, own_img, after_k, pull_k, inner_k = bundle
            middle_a = 0.5 * (before_k + own_img)
            middle_b = 0.5 * (own_img + after_k)
            res_a = (own_img - before_k) / time_step - force_field(pad_x(middle_a), aniso)
            res_b = (after_k - own_img) / time_step - force_field(pad_x(middle_b), aniso)
            adjoint = exchange_coef * laplace(pad_x(res_a + res_b))
            adjoint = adjoint + hessian_point(middle_a, res_a, aniso) + hessian_point(middle_b, res_b, aniso)
            result = res_a - res_b - 0.5 * time_step * adjoint + pull_k * (after_k - before_k)
            return result * inner_k
        for inner_step in range(INNER):
            gradients = lax.map(gradient, (before_img, current, after_img, spring_pull, interior))
            grad_scale = jnp.sqrt(jnp.sum(gradients * gradients) / cell_count + epsilon)
            current = current - step_scale * gradients / grad_scale
    return current
```

```python
import jax
import jax.numpy as jnp
from jax import lax
from jax.sharding import Mesh
from jax.sharding import PartitionSpec as P

OUTER = 2
INNER = 3
IMG = ("img_0", "img_1")
TILE = ("tile_0", "tile_1")
IMG_TILE = ("img_0", "img_1", "tile_0", "tile_1")


exchange_coef = 1.0
cubic_coef = 0.5
spring_coef = 20.0
step_scale = 0.25
epsilon = 1e-06


def padded_2(cells, sides, width):
    for axis, dim in sides:
        count = lax.axis_size(axis)
        ends = count - 1
        head = lax.slice_in_dim(cells, 0, width, axis=dim)
        tail = lax.slice_in_dim(cells, cells.shape[dim] - width, cells.shape[dim], axis=dim)
        cells = jnp.concatenate(
            [
                lax.ppermute(tail, axis, [(i, (i + 1) % count) for i in range(ends)]),
                cells,
                lax.ppermute(head, axis, [((i + 1) % count, i) for i in range(ends)]),
            ],
            axis=dim,
        )
    return cells


def from_everyone(values):
    peers = lax.axis_size(IMG_TILE)
    return lax.all_to_all(
        jnp.broadcast_to(values[None], (peers, *values.shape)), IMG_TILE, 0, 0, tiled=True
    )


def laplace(field):
    widths = [(0, 0)] * (field.ndim - 4) + [(0, 0), (1, 1), (0, 0), (1, 1)]
    padded = jnp.pad(field, widths)
    centre = padded[..., 1:-1, 1:-1, 1:-1]
    beside_all = padded[..., 2:, 1:-1, 1:-1] + padded[..., :-2, 1:-1, 1:-1]
    beside_all = beside_all + padded[..., 1:-1, 2:, 1:-1] + padded[..., 1:-1, :-2, 1:-1]
    beside_all = beside_all + padded[..., 1:-1, 1:-1, 2:] + padded[..., 1:-1, 1:-1, :-2]
    return beside_all - 6.0 * centre


def axis_select():
    return (jnp.arange(3) == 2).astype(jnp.float32)[:, None, None, None]


def force_field(middle_ext, coefs):
    middle = middle_ext[..., 1:-1, :]
    square_norm = jnp.sum(middle * middle, axis=-4, keepdims=True)
    return (
        exchange_coef * laplace(middle_ext)
        + coefs * middle * axis_select()
        - cubic_coef * (square_norm - 1.0) * middle
    )


def hessian_point(middle, vector, coefs):
    square_norm = jnp.sum(middle * middle, axis=-4, keepdims=True)
    projected = jnp.sum(middle * vector, axis=-4, keepdims=True)
    return coefs * vector * axis_select() - cubic_coef * (
        (square_norm - 1.0) * vector + 2.0 * middle * projected
    )


def body(spins, aniso):
    local_images = spins.shape[0]
    width_x = spins.shape[3]
    img_count = lax.axis_size(IMG)
    tile_count = lax.axis_size(TILE)
    images = local_images * img_count
    cell_count = float(
        images * spins.shape[1] * spins.shape[2] * width_x * tile_count * spins.shape[4]
    )
    first_image = lax.axis_index(IMG) * local_images
    image_index = first_image + jnp.arange(local_images, dtype=jnp.int32)
    interior = ((image_index > 0) & (image_index < images - 1)).astype(jnp.float32)
    target = image_index.astype(jnp.float32) / (images - 1)
    rim_depth = 1
    cycle_mask = 1.0
    current = spins
    for outer_step in range(OUTER):
        repeated = current
        framed_all = padded_2(repeated, ((IMG, 0), (TILE, 3)), rim_depth)
        before_img = framed_all[:-2]
        own_framed = framed_all[1:-1]
        after_img = framed_all[2:]
        difference = (after_img - own_framed)[..., rim_depth : rim_depth + width_x, :]
        middle_seg = 0.5 * (own_framed + after_img)
        drive_own = force_field(middle_seg, aniso)
        diff_sq = jnp.sum(difference * difference, axis=(1, 2, 3, 4))
        drive_sq = jnp.sum(drive_own * drive_own, axis=(1, 2, 3, 4))
        shares = from_everyone(jnp.concatenate([diff_sq, drive_sq]))
        shares = shares.reshape(img_count, tile_count, 2, local_images).sum(axis=1)
        shares = jnp.moveaxis(shares, 1, 0).reshape(2, images)
        every_image = jnp.arange(images)
        lengths = jnp.sqrt(shares + epsilon) * (every_image < images - 1)
        seg_len = lengths[0]
        path_len, drive_total = jnp.sum(seg_len), jnp.sum(lengths[1])
        before_arc = jnp.sum(
            jnp.where(every_image[None, :] < image_index[:, None], seg_len[None, :], 0.0), axis=1
        )
        time_step = path_len / drive_total
        spring_pull = (
            spring_coef * (before_arc / path_len - target) * (images - 1) / (2.0 * path_len)
        )
        spring_pull = spring_pull[:, None, None, None, None]
        interior_mask = interior[:, None, None, None, None]
        before_core = before_img[..., 1:-1, :]
        after_core = after_img[..., 1:-1, :]
        before_own = before_img[..., rim_depth : rim_depth + width_x, :]
        after_own = after_img[..., rim_depth : rim_depth + width_x, :]
        for inner_step in range(INNER):
            if inner_step == 0:
                own_ext = own_framed
            else:
                own_ext = padded_2(current, ((TILE, 3),), rim_depth)
            own_core = own_ext[..., 1:-1, :]
            middle_a = 0.5 * (before_img + own_ext)
            middle_b = 0.5 * (own_ext + after_img)
            res_a = (
                (own_core - before_core) / time_step - force_field(middle_a, aniso)
            ) * cycle_mask
            res_b = (
                (after_core - own_core) / time_step - force_field(middle_b, aniso)
            ) * cycle_mask
            res_sum = res_a + res_b
            adjoint_lap = laplace(padded_2(res_sum, ((TILE, 3),), 1))
            middle_a_own = middle_a[..., rim_depth : rim_depth + width_x, :]
            middle_b_own = middle_b[..., rim_depth : rim_depth + width_x, :]
            adjoint = exchange_coef * adjoint_lap
            adjoint = (
                adjoint
                + hessian_point(middle_a_own, res_a, aniso)
                + hessian_point(middle_b_own, res_b, aniso)
            )
            gradients = (
                res_a - res_b - 0.5 * time_step * adjoint + spring_pull * (after_own - before_own)
            )
            gradients = gradients * interior_mask
            grad_total = jnp.sum(from_everyone(jnp.sum(gradients * gradients)[None]))
            grad_scale = jnp.sqrt(grad_total / cell_count + epsilon)
            current = current - step_scale * gradients / grad_scale
    return current


def solution(mesh):
    split = Mesh(mesh.devices.reshape(4, 4, 4, 2), ("img_0", "img_1", "tile_0", "tile_1"))
    return jax.shard_map(
        body,
        mesh=split,
        in_specs=(P(IMG, None, None, TILE, None), P(None, TILE, None)),
        out_specs=P(IMG, None, None, TILE, None),
        check_vma=False,
    )
```

```python
import jax
import jax.numpy as jnp
from jax import lax
from jax.experimental import pallas as pl
from jax.experimental.pallas import tpu as pltpu
from jax.sharding import Mesh
from jax.sharding import PartitionSpec as P

OUTER = 2
INNER = 3
IMG = ("img_0", "img_1")
TILE = ("tile_0", "tile_1")
IMG_TILE = ("img_0", "img_1", "tile_0", "tile_1")

spring_coef = 20.0
step_scale = 0.25
epsilon = 1e-06

HALO = 2 * INNER
PRODUCTS = 12
VMEM_LIMIT = 48 * 1024 * 1024


def shifted(cells, axis, total):
    where = lax.broadcasted_iota(jnp.int32, cells.shape, axis)
    size = cells.shape[axis]
    total = total + jnp.where(where == 0, 0.0, pltpu.roll(cells, 1, axis))
    return total + jnp.where(where == size - 1, 0.0, pltpu.roll(cells, size - 1, axis))


def laplace(cells, beside):
    return [
        shifted(cell, 1, shifted(cell, 0, total - 6.0 * cell))
        for cell, total in zip(cells, beside)
    ]


def dot(left, right):
    return left[0] * right[0] + left[1] * right[1] + left[2] * right[2]


def row(ref, at):
    return [ref[comp, at] for comp in range(3)]


def put(ref, at, cells):
    for comp in range(3):
        ref[comp, at] = cells[comp]


def plus(left, right):
    return [one + other for one, other in zip(left, right)]


def scaled(factors, cells):
    return [factor * cell for factor, cell in zip(factors, cells)]


def stiffness(square, coefs):
    plain = 0.5 - 0.125 * square
    return [plain, plain, plain + coefs]


def folded(cells):
    cells = cells[:8] + cells[8:]
    return cells[:, :128] + cells[:, 128:]


def loop(low, high, body, carry=0):
    return lax.fori_loop(low, high, body, carry)


def clear_outside(tile, last_tile, refs, own):
    rows = refs[0].shape[1]

    @pl.when(tile == 0)
    def _():
        for ref in refs:
            ref[:, 0:HALO] = jnp.zeros((3, HALO) + ref.shape[2:], jnp.float32)

    @pl.when(tile == last_tile)
    def _():
        for ref in refs:
            ref[:, HALO + own :] = jnp.zeros((3, rows - HALO - own) + ref.shape[2:], jnp.float32)


def drives(phi_ref, a_ref, b_ref, coef_ref, fa_ref, fb_ref, low, high):
    def body(at, carry):
        phi, a, b = row(phi_ref, at), row(a_ref, at), row(b_ref, at)
        m, n = plus(phi, a), plus(phi, b)
        side = plus(row(phi_ref, at - 1), row(phi_ref, at + 1))
        side_m = plus(side, plus(row(a_ref, at - 1), row(a_ref, at + 1)))
        side_n = plus(side, plus(row(b_ref, at - 1), row(b_ref, at + 1)))
        coefs = coef_ref[at]
        put(fa_ref, at, plus(laplace(m, side_m), scaled(stiffness(dot(m, m), coefs), m)))
        put(fb_ref, at, plus(laplace(n, side_n), scaled(stiffness(dot(n, n), coefs), n)))
        return carry

    loop(low, high, body)


def parts(phi, a, b, coefs, fa_ref, fb_ref, at):
    m, n = plus(phi, a), plus(phi, b)
    square_m, square_n = dot(m, m), dot(n, n)
    square_phi = dot(phi, phi)
    fa, fb = row(fa_ref, at), row(fb_ref, at)
    side = plus(row(fa_ref, at - 1), row(fa_ref, at + 1))
    side = plus(side, plus(row(fb_ref, at - 1), row(fb_ref, at + 1)))
    adjoint = laplace(plus(fa, fb), side)
    stiff_m, stiff_n = stiffness(square_m, coefs), stiffness(square_n, coefs)
    turn_m, turn_n = 0.25 * dot(m, fa), 0.25 * dot(n, fb)
    rise_m, rise_n = square_phi - dot(a, a), dot(b, b) - square_phi
    return m, n, square_m - square_n, fa, fb, adjoint, stiff_m, stiff_n, turn_m, turn_n, rise_m, rise_n


def first_kernel(
    place_ref, own_edge, own_mid, a_edge, a_mid, b_edge, b_mid, up_ref, down_ref, coef_ref,
    phi_ref, a_ref, b_ref, q_ref, r_ref, sums_ref, fa_ref, fb_ref, acc_ref
):
    own = own_edge.shape[1] + own_mid.shape[1]
    rows = own + 2 * HALO
    last_tile = place_ref[2] - 1
    tile = place_ref[1]
    for which, (ref, edge, mid) in enumerate(
        ((a_ref, a_edge, a_mid), (phi_ref, own_edge, own_mid), (b_ref, b_edge, b_mid))
    ):
        ref[:, 0:HALO] = up_ref[which]
        ref[:, HALO : 2 * HALO] = edge[:, 0:HALO]
        ref[:, 2 * HALO : own] = mid[...]
        ref[:, own : own + HALO] = edge[:, HALO:]
        ref[:, own + HALO :] = down_ref[which]
    drives(phi_ref, a_ref, b_ref, coef_ref, fa_ref, fb_ref, 1, rows - 1)
    clear_outside(tile, last_tile, (fa_ref, fb_ref), own)
    acc_ref[...] = jnp.zeros_like(acc_ref)

    def fields(at):
        phi, a, b = row(phi_ref, at), row(a_ref, at), row(b_ref, at)
        coefs = coef_ref[at]
        m, n, gap, fa, fb, adjoint, stiff_m, stiff_n, turn_m, turn_n, rise_m, rise_n = parts(
            phi, a, b, coefs, fa_ref, fb_ref, at
        )
        gap, rise_m, rise_n = 0.125 * gap, 0.125 * rise_m, 0.125 * rise_n
        flat, bent = [], []
        for c in range(3):
            flat.append(phi[c] * gap + m[c] * rise_m + n[c] * rise_n)
            bent.append(
                0.25
                * (
                    adjoint[c]
                    + (stiff_m[c] * fa[c] + stiff_n[c] * fb[c])
                    - (m[c] * turn_m + n[c] * turn_n)
                )
            )
        put(q_ref, at, flat)
        put(r_ref, at, bent)
        return phi, a, b, fb, flat, bent

    def rim(at, carry):
        fields(at)
        return carry

    def inside(at, carry):
        phi, a, b, fb, flat, bent = fields(at)
        ahead = [one - other for one, other in zip(b, phi)]
        pull = [one - other for one, other in zip(b, a)]
        curve = [2.0 * one - (two + other) for one, two, other in zip(phi, a, b)]
        pairs = (
            (curve, curve), (curve, flat), (curve, bent), (curve, pull),
            (flat, flat), (flat, bent), (flat, pull),
            (bent, bent), (bent, pull), (pull, pull),
            (ahead, ahead), (fb, fb),
        )
        for which, (left, right) in enumerate(pairs):
            acc_ref[which] += folded(dot(left, right))
        return carry

    loop(2, HALO, rim)
    loop(HALO, HALO + own, inside)
    loop(HALO + own, rows - 2, rim)
    clear_outside(tile, last_tile, (q_ref, r_ref), own)
    lane = lax.broadcasted_iota(jnp.int32, (1, 128), 1)
    sums = jnp.zeros((1, 128), jnp.float32)
    for which in range(PRODUCTS):
        sums = jnp.where(lane == which, jnp.sum(acc_ref[which]), sums)
    sums_ref[...] = jnp.broadcast_to(sums, sums_ref.shape)


def path_scalars(place_ref, all_ref, tiles, cells):
    devices = all_ref.shape[0]
    images = devices // tiles
    table = jnp.sum(all_ref[...].reshape(images, tiles, 128), axis=1)
    lane = lax.broadcasted_iota(jnp.int32, (images, 128), 1)
    image = lax.broadcasted_iota(jnp.int32, (images, 128), 0)
    one = image[:, :1]

    def column(which):
        return jnp.sum(jnp.where(lane == which, table, 0.0), axis=1, keepdims=True)

    live = one < images - 1
    seg = jnp.where(live, jnp.sqrt(column(10) + epsilon), 0.0)
    drv = jnp.where(live, jnp.sqrt(0.25 * column(11) + epsilon), 0.0)
    path_len = jnp.sum(seg, axis=0, keepdims=True)
    tau = path_len / jnp.sum(drv, axis=0, keepdims=True)
    before = jnp.sum(jnp.where(image < lane, seg, 0.0), axis=0, keepdims=True)
    before = jnp.sum(jnp.where(image == lane, before, 0.0), axis=1, keepdims=True)
    target = one.astype(jnp.float32) / (images - 1)
    pull = spring_coef * (before / path_len - target) * (images - 1) / (2.0 * path_len)
    inv = 1.0 / tau
    norm = inv * (inv * column(0) + 2.0 * (column(1) + tau * column(2) + pull * column(3)))
    norm += column(4) + 2.0 * (tau * column(5) + pull * column(6))
    norm += tau * (tau * column(7) + 2.0 * pull * column(8)) + pull * pull * column(9)
    inner = (one > 0) & (one < images - 1)
    total = jnp.sum(jnp.where(inner, norm, 0.0), axis=0, keepdims=True)
    step = step_scale / jnp.sqrt(total / cells + epsilon)
    mine = jnp.sum(jnp.where(one == place_ref[0], pull, 0.0), axis=0, keepdims=True)
    return tau[0, 0], mine[0, 0], step[0, 0]


def gradients(phi_ref, a_ref, b_ref, coef_ref, fa_ref, fb_ref, g_ref, acc_ref, tau, pull, out):
    inv = 1.0 / tau
    turned = 0.25 * tau

    def grad(at):
        phi, a, b = row(phi_ref, at), row(a_ref, at), row(b_ref, at)
        m, n, gap, fa, fb, adjoint, stiff_m, stiff_n, turn_m, turn_n, rise_m, rise_n = parts(
            phi, a, b, coef_ref[at], fa_ref, fb_ref, at
        )
        gap = 0.125 * gap + 2.0 * inv
        lean_m = 0.125 * rise_m - turned * turn_m
        lean_n = 0.125 * rise_n - turned * turn_n
        return [
            phi[c] * gap
            + (m[c] * lean_m + n[c] * lean_n)
            + turned * (adjoint[c] + (stiff_m[c] * fa[c] + stiff_n[c] * fb[c]))
            + ((pull - inv) * b[c] - (pull + inv) * a[c])
            for c in range(3)
        ]

    def rim(at, carry):
        put(g_ref, at - out, grad(at))
        return carry

    def inside(at, carry):
        cells = grad(at)
        put(g_ref, at - out, cells)
        acc_ref[...] += folded(dot(cells, cells))
        return carry

    return rim, inside


def interior(place_ref):
    return jnp.where((place_ref[0] > 0) & (place_ref[0] < place_ref[3] - 1), 1.0, 0.0)


def second_kernel(
    tiles, cells, place_ref, all_ref, p_ref, a_ref, b_ref, q_ref, r_ref, coef_ref,
    phi_ref, g_ref, scal_ref, sums_ref, fa_ref, fb_ref, acc_ref
):
    rows = p_ref.shape[1]
    own = rows - 2 * HALO
    tile, last_tile = place_ref[1], place_ref[2] - 1
    tau, pull, step = path_scalars(place_ref, all_ref, tiles, cells)
    live = interior(place_ref)
    step = step * live
    inv = 1.0 / tau
    scal_ref[0] = tau
    scal_ref[1] = pull
    keep, from_a, from_b = 1.0 - 2.0 * step * inv, step * (inv + pull), step * (inv - pull)
    bend = step * tau

    def update(at, carry):
        p, a, b, q, r = (row(ref, at) for ref in (p_ref, a_ref, b_ref, q_ref, r_ref))
        put(
            phi_ref,
            at,
            [
                (keep * p[c] + from_a * a[c]) + (from_b * b[c] - step * q[c]) - bend * r[c]
                for c in range(3)
            ],
        )
        return carry

    loop(2, rows - 2, update)
    drives(phi_ref, a_ref, b_ref, coef_ref, fa_ref, fb_ref, 3, rows - 3)
    clear_outside(tile, last_tile, (fa_ref, fb_ref), own)
    acc_ref[...] = jnp.zeros_like(acc_ref)
    rim, inside = gradients(
        phi_ref, a_ref, b_ref, coef_ref, fa_ref, fb_ref, g_ref, acc_ref, tau, pull, 0
    )
    loop(4, HALO, rim)
    loop(HALO, HALO + own, inside)
    loop(HALO + own, rows - 4, rim)
    clear_outside(tile, last_tile, (g_ref,), own)
    sums = jnp.sum(acc_ref[...], axis=0, keepdims=True) * live
    sums_ref[...] = jnp.broadcast_to(sums, sums_ref.shape)


def step_of(all_ref, cells):
    return step_scale / jnp.sqrt(jnp.sum(all_ref[...]) / cells + epsilon)


def third_kernel(
    cells, place_ref, scal_ref, all_ref, p_ref, h_ref, a_ref, b_ref, coef_ref,
    phi_ref, g_ref, sums_ref, fa_ref, fb_ref, acc_ref
):
    rows = p_ref.shape[1]
    own = rows - 2 * HALO
    tile, last_tile = place_ref[1], place_ref[2] - 1
    live = interior(place_ref)
    tau, pull = scal_ref[0], scal_ref[1]
    step = step_of(all_ref, cells) * live

    def update(at, carry):
        p, h = row(p_ref, at), row(h_ref, at)
        put(phi_ref, at, [p[c] - step * h[c] for c in range(3)])
        return carry

    loop(4, rows - 4, update)
    drives(phi_ref, a_ref, b_ref, coef_ref, fa_ref, fb_ref, 5, rows - 5)
    clear_outside(tile, last_tile, (fa_ref, fb_ref), own)
    acc_ref[...] = jnp.zeros_like(acc_ref)
    _, inside = gradients(
        phi_ref, a_ref, b_ref, coef_ref, fa_ref, fb_ref, g_ref, acc_ref, tau, pull, HALO
    )
    loop(HALO, HALO + own, inside)
    sums = jnp.sum(acc_ref[...], axis=0, keepdims=True) * live
    sums_ref[...] = jnp.broadcast_to(sums, sums_ref.shape)


def last_kernel(cells, place_ref, all_ref, p_ref, g_ref, edge_ref, mid_ref):
    own = g_ref.shape[1]
    step = step_of(all_ref, cells) * interior(place_ref)

    def moved(at):
        p, g = row(p_ref, at + HALO), row(g_ref, at)
        return [p[c] - step * g[c] for c in range(3)]

    def top(at, carry):
        put(edge_ref, at, moved(at))
        return carry

    def middle(at, carry):
        put(mid_ref, at - HALO, moved(at))
        return carry

    def bottom(at, carry):
        put(edge_ref, at - (own - 2 * HALO), moved(at))
        return carry

    loop(0, HALO, top)
    loop(HALO, own - HALO, middle)
    loop(own - HALO, own, bottom)


def f32(*shape):
    return jax.ShapeDtypeStruct(shape, jnp.float32)


def call(kernel, operands, outs, scratch, scalars=1, small_out=()):
    smem = pl.BlockSpec(memory_space=pltpu.SMEM)
    vmem = pl.BlockSpec(memory_space=pltpu.VMEM)
    return pl.pallas_call(
        kernel,
        out_shape=outs,
        in_specs=[smem if i < scalars else vmem for i in range(len(operands))],
        out_specs=[smem if i in small_out else vmem for i in range(len(outs))],
        scratch_shapes=[pltpu.VMEM(shape, jnp.float32) for shape in scratch],
        compiler_params=pltpu.CompilerParams(vmem_limit_bytes=VMEM_LIMIT),
    )(*operands)


def beside(cells, axis, forward):
    count = lax.axis_size(axis)
    pairs = [(i, i + 1) if forward else (i + 1, i) for i in range(count - 1)]
    return lax.ppermute(cells, axis, pairs)


def from_everyone(rows):
    return lax.all_to_all(rows, IMG_TILE, 0, 0, tiled=True)


def body(spins, aniso):
    _, comps, depth, own, width = spins.shape
    images, tiles = lax.axis_size(IMG), lax.axis_size(TILE)
    devices = images * tiles
    cells = float(images * comps * depth * own * tiles * width)
    rows = own + 2 * HALO
    place = jnp.stack(
        [lax.axis_index(IMG), lax.axis_index(TILE), jnp.int32(tiles), jnp.int32(images)]
    ).astype(jnp.int32)
    start = jnp.swapaxes(spins[0], 1, 2)
    coefs = jnp.swapaxes(aniso, 0, 1)
    coefs = jnp.concatenate(
        [beside(coefs[own - HALO :], TILE, True), coefs, beside(coefs[:HALO], TILE, False)]
    )
    edge = jnp.concatenate([start[:, :HALO], start[:, own - HALO :]], axis=1)
    mid = start[:, HALO : own - HALO]
    ext = (3, rows, depth, width)
    whole = f32(*ext)
    table = f32(devices, 128)
    for _ in range(OUTER):
        a_edge, b_edge = beside(edge, IMG, True), beside(edge, IMG, False)
        trio = jnp.stack([a_edge, edge, b_edge])
        up = beside(trio[:, :, HALO:], TILE, True)
        down = beside(trio[:, :, :HALO], TILE, False)
        a_mid, b_mid = beside(mid, IMG, True), beside(mid, IMG, False)
        phi, a, b, q, r, sums = call(
            first_kernel,
            [place, edge, mid, a_edge, a_mid, b_edge, b_mid, up, down, coefs],
            [whole, whole, whole, whole, whole, table],
            [ext, ext, (PRODUCTS, 8, 128)],
        )
        phi, g, scal, sums = call(
            lambda *refs: second_kernel(tiles, cells, *refs),
            [place, from_everyone(sums), phi, a, b, q, r, coefs],
            [whole, whole, f32(2), table],
            [ext, ext, (8, 128)],
            small_out=(2,),
        )
        phi, g, sums = call(
            lambda *refs: third_kernel(cells, *refs),
            [place, scal, from_everyone(sums), phi, g, a, b, coefs],
            [whole, f32(3, own, depth, width), table],
            [ext, ext, (8, 128)],
            scalars=2,
        )
        edge, mid = call(
            lambda *refs: last_kernel(cells, *refs),
            [place, from_everyone(sums), phi, g],
            [f32(3, 2 * HALO, depth, width), f32(3, own - 2 * HALO, depth, width)],
            [],
        )
    final = jnp.concatenate([edge[:, :HALO], mid, edge[:, HALO:]], axis=1)
    return jnp.swapaxes(final, 1, 2)[None]


def solution(mesh):
    split = Mesh(mesh.devices.reshape(4, 4, 4, 2), IMG_TILE)
    return jax.shard_map(
        body,
        mesh=split,
        in_specs=(P(IMG, None, None, TILE, None), P(None, TILE, None)),
        out_specs=P(IMG, None, None, TILE, None),
        check_vma=False,
    )
```

```python
import jax
import jax.numpy as jnp
from jax import lax
from jax.experimental import pallas as pl
from jax.experimental.pallas import tpu as pltpu
from jax.sharding import Mesh
from jax.sharding import PartitionSpec as P

OUTER = 2
INNER = 3
IMG = ("img_0", "img_1")
TILE = ("tile_0", "tile_1")
IMG_TILE = ("img_0", "img_1", "tile_0", "tile_1")

spring_coef = 20.0
step_scale = 0.25
epsilon = 1e-06

HALO = 2 * INNER
PRODUCTS = 11
SUBLANES = 2
LANES = 2
TILES = range(SUBLANES * LANES)
VMEM_LIMIT = 24 * 1024 * 1024


def tile_of(ref, comp, at, place):
    z, y = divmod(place, LANES)
    return ref[comp, at, z * 8 : z * 8 + 8, y * 128 : y * 128 + 128]


def put(ref, comp, at, place, cells):
    z, y = divmod(place, LANES)
    ref[comp, at, z * 8 : z * 8 + 8, y * 128 : y * 128 + 128] = cells


def flat_of(ref, at, place):
    z, y = divmod(place, LANES)
    return ref[at, z * 8 : z * 8 + 8, y * 128 : y * 128 + 128]


def put_flat(ref, at, place, cells):
    z, y = divmod(place, LANES)
    ref[at, z * 8 : z * 8 + 8, y * 128 : y * 128 + 128] = cells


def vector(ref, at, place):
    return [tile_of(ref, comp, at, place) for comp in range(3)]


def around(line, axis):
    size = line[0].shape[axis]
    where = lax.broadcasted_iota(jnp.int32, line[0].shape, axis)
    first, last = where == 0, where == size - 1
    later = [pltpu.roll(cells, 1, axis) for cells in line]
    earlier = [pltpu.roll(cells, size - 1, axis) for cells in line]
    later, earlier = [0.0, *later], [*earlier, 0.0]
    return [
        jnp.where(first, later[i], later[i + 1]) + jnp.where(last, earlier[i + 1], earlier[i])
        for i in range(len(line))
    ]


def laplace(ref, comp, at):
    cells = [tile_of(ref, comp, at, place) for place in TILES]
    total = [
        (tile_of(ref, comp, at - 1, place) + tile_of(ref, comp, at + 1, place)) - 6.0 * cells[place]
        for place in TILES
    ]
    for z in range(SUBLANES):
        picked = range(z * LANES, z * LANES + LANES)
        for place, side in zip(picked, around([cells[i] for i in picked], 1)):
            total[place] = total[place] + side
    for y in range(LANES):
        picked = range(y, SUBLANES * LANES, LANES)
        for place, side in zip(picked, around([cells[i] for i in picked], 0)):
            total[place] = total[place] + side
    return cells, total


def dot(left, right):
    return left[0] * right[0] + left[1] * right[1] + left[2] * right[2]


def stiffness(square, coefs):
    plain = 0.5 - 0.125 * square
    return [plain, plain, plain + coefs]


def loop(low, high, body, carry=0):
    return lax.fori_loop(low, high, body, carry, unroll=4)


def clear_outside(tile, last_tile, refs, own):
    rows = refs[0].shape[1]

    @pl.when(tile == 0)
    def _():
        for ref in refs:
            ref[:, 0:HALO] = jnp.zeros((3, HALO) + ref.shape[2:], jnp.float32)

    @pl.when(tile == last_tile)
    def _():
        for ref in refs:
            ref[:, HALO + own :] = jnp.zeros((3, rows - HALO - own) + ref.shape[2:], jnp.float32)


def drives(m_ref, n_ref, coef_ref, fa_ref, fb_ref, fs_ref, sm_ref, sn_ref, low, high):
    def body(at, carry):
        for which, (ref, out, squares) in enumerate(
            ((m_ref, fa_ref, sm_ref), (n_ref, fb_ref, sn_ref))
        ):
            stiff = []
            for place in TILES:
                cells = vector(ref, at, place)
                square = dot(cells, cells)
                put_flat(squares, at, place, square)
                stiff.append(stiffness(square, flat_of(coef_ref, at, place)))
            for comp in range(3):
                cells, bent = laplace(ref, comp, at)
                for place in TILES:
                    drive = bent[place] + stiff[place][comp] * cells[place]
                    put(out, comp, at, place, drive)
                    if which:
                        drive = drive + tile_of(fa_ref, comp, at, place)
                        put(fs_ref, comp, at, place, drive)
        return carry

    loop(low, high, body)


def assemble(phi_ref, m_ref, n_ref, own, at, to, pieces):
    own_ref, a_ref, b_ref = pieces
    for comp in range(3):
        for place in TILES:
            phi = tile_of(own_ref, comp, at, place)
            put(phi_ref, comp, to, place, phi)
            put(m_ref, comp, to, place, phi + tile_of(a_ref, comp, at, place))
            put(n_ref, comp, to, place, phi + tile_of(b_ref, comp, at, place))


def first_kernel(
    place_ref, own_edge, own_mid, a_edge, a_mid, b_edge, b_mid, up_ref, down_ref, coef_ref,
    phi_ref, m_ref, n_ref, q_ref, r_ref, sums_ref, fa_ref, fb_ref, fs_ref, sm_ref, sn_ref
):
    own = own_edge.shape[1] + own_mid.shape[1]
    rows = own + 2 * HALO
    tile, last_tile = place_ref[1], place_ref[2] - 1
    edges, mids = (own_edge, a_edge, b_edge), (own_mid, a_mid, b_mid)
    ups, downs = ([ref.at[which] for which in (1, 0, 2)] for ref in (up_ref, down_ref))
    for pieces, low, high, shift in (
        (ups, 0, HALO, 0),
        (edges, 0, HALO, HALO),
        (mids, 0, own - 2 * HALO, 2 * HALO),
        (edges, HALO, 2 * HALO, own - HALO),
        (downs, 0, HALO, own + HALO),
    ):

        def join(at, carry, pieces=pieces, shift=shift):
            assemble(phi_ref, m_ref, n_ref, own, at, at + shift, pieces)
            return carry

        loop(low, high, join)
    drives(m_ref, n_ref, coef_ref, fa_ref, fb_ref, fs_ref, sm_ref, sn_ref, 1, rows - 1)
    clear_outside(tile, last_tile, (fa_ref, fb_ref, fs_ref), own)

    def fields(at, sums):
        adjoint = [laplace(fs_ref, comp, at)[1] for comp in range(3)]
        for place in TILES:
            phi, m, n = (vector(ref, at, place) for ref in (phi_ref, m_ref, n_ref))
            fa, fb = vector(fa_ref, at, place), vector(fb_ref, at, place)
            square_m, square_n = flat_of(sm_ref, at, place), flat_of(sn_ref, at, place)
            coefs = flat_of(coef_ref, at, place)
            stiff_m, stiff_n = stiffness(square_m, coefs), stiffness(square_n, coefs)
            turn_m, turn_n = 0.25 * dot(m, fa), 0.25 * dot(n, fb)
            gap = 0.125 * (square_m - square_n)
            rise_m = 0.25 * dot(m, phi) - 0.125 * square_m
            rise_n = 0.125 * square_n - 0.25 * dot(n, phi)
            flat, bent = [], []
            for c in range(3):
                flat.append(phi[c] * gap + m[c] * rise_m + n[c] * rise_n)
                bent.append(
                    0.25
                    * (
                        adjoint[c][place]
                        + (stiff_m[c] * fa[c] + stiff_n[c] * fb[c])
                        - (m[c] * turn_m + n[c] * turn_n)
                    )
                )
                put(q_ref, c, at, place, flat[c])
                put(r_ref, c, at, place, bent[c])
            if sums:
                behind = [2.0 * one - other for one, other in zip(phi, m)]
                ahead = [other - 2.0 * one for one, other in zip(phi, n)]
                pairs = (
                    (behind, behind), (behind, ahead), (ahead, ahead),
                    (flat, behind), (flat, ahead), (bent, behind), (bent, ahead),
                    (flat, flat), (flat, bent), (bent, bent), (fb, fb),
                )
                sums = [total + dot(left, right) for total, (left, right) in zip(sums, pairs)]
        return sums

    def rim(at, carry):
        fields(at, None)
        return carry

    loop(2, HALO, rim)
    sums = loop(HALO, HALO + own, fields, [jnp.zeros((8, 128), jnp.float32)] * PRODUCTS)
    loop(HALO + own, rows - 2, rim)
    clear_outside(tile, last_tile, (q_ref, r_ref), own)
    lane = lax.broadcasted_iota(jnp.int32, (1, 128), 1)
    result = jnp.zeros((1, 128), jnp.float32)
    for which in range(PRODUCTS):
        result = jnp.where(lane == which, jnp.sum(sums[which]), result)
    sums_ref[...] = jnp.broadcast_to(result, sums_ref.shape)


def path_scalars(place_ref, all_ref, tiles, cells):
    devices = all_ref.shape[0]
    images = devices // tiles
    table = jnp.sum(all_ref[...].reshape(images, tiles, 128), axis=1)
    lane = lax.broadcasted_iota(jnp.int32, (images, 128), 1)
    image = lax.broadcasted_iota(jnp.int32, (images, 128), 0)
    one = image[:, :1]

    def column(which):
        return jnp.sum(jnp.where(lane == which, table, 0.0), axis=1, keepdims=True)

    live = one < images - 1
    seg = jnp.where(live, jnp.sqrt(column(2) + epsilon), 0.0)
    drv = jnp.where(live, jnp.sqrt(0.25 * column(10) + epsilon), 0.0)
    path_len = jnp.sum(seg, axis=0, keepdims=True)
    tau = path_len / jnp.sum(drv, axis=0, keepdims=True)
    before = jnp.sum(jnp.where(image < lane, seg, 0.0), axis=0, keepdims=True)
    before = jnp.sum(jnp.where(image == lane, before, 0.0), axis=1, keepdims=True)
    target = one.astype(jnp.float32) / (images - 1)
    pull = spring_coef * (before / path_len - target) * (images - 1) / (2.0 * path_len)
    inv = 1.0 / tau
    near, far = inv + pull, pull - inv
    norm = near * near * column(0) + far * far * column(2) + 2.0 * near * far * column(1)
    norm += 2.0 * (near * column(3) + far * column(4))
    norm += 2.0 * tau * (near * column(5) + far * column(6))
    norm += column(7) + tau * (2.0 * column(8) + tau * column(9))
    inner = (one > 0) & (one < images - 1)
    total = jnp.sum(jnp.where(inner, norm, 0.0), axis=0, keepdims=True)
    step = step_scale / jnp.sqrt(total / cells + epsilon)
    mine = jnp.sum(jnp.where(one == place_ref[0], pull, 0.0), axis=0, keepdims=True)
    return tau[0, 0], mine[0, 0], step[0, 0]


def gradients(
    phi_ref, m_ref, n_ref, coef_ref, fa_ref, fb_ref, fs_ref, sm_ref, sn_ref, g_ref, tau, pull, out
):
    inv = 1.0 / tau
    turned = 0.25 * tau

    def grad(at, total):
        adjoint = [laplace(fs_ref, comp, at)[1] for comp in range(3)]
        for place in TILES:
            phi, m, n = (vector(ref, at, place) for ref in (phi_ref, m_ref, n_ref))
            fa, fb = vector(fa_ref, at, place), vector(fb_ref, at, place)
            square_m, square_n = flat_of(sm_ref, at, place), flat_of(sn_ref, at, place)
            coefs = flat_of(coef_ref, at, place)
            stiff_m, stiff_n = stiffness(square_m, coefs), stiffness(square_n, coefs)
            gap = 0.125 * (square_m - square_n) + 4.0 * inv
            lean_m = (
                0.25 * (dot(m, phi) - turned * dot(m, fa)) - 0.125 * square_m - (pull + inv)
            )
            lean_n = (
                0.125 * square_n - 0.25 * (dot(n, phi) + turned * dot(n, fb)) + (pull - inv)
            )
            cells = [
                phi[c] * gap
                + (m[c] * lean_m + n[c] * lean_n)
                + turned * (adjoint[c][place] + (stiff_m[c] * fa[c] + stiff_n[c] * fb[c]))
                for c in range(3)
            ]
            for c in range(3):
                put(g_ref, c, at - out, place, cells[c])
            total = total + dot(cells, cells)
        return total

    def rim(at, carry):
        grad(at, 0.0)
        return carry

    return rim, grad


def interior(place_ref):
    return jnp.where((place_ref[0] > 0) & (place_ref[0] < place_ref[3] - 1), 1.0, 0.0)


def second_kernel(
    tiles, cells, place_ref, all_ref, p_ref, m0_ref, n0_ref, q_ref, r_ref, coef_ref,
    phi_ref, m_ref, n_ref, g_ref, scal_ref, sums_ref, fa_ref, fb_ref, fs_ref, sm_ref, sn_ref
):
    rows = p_ref.shape[1]
    own = rows - 2 * HALO
    tile, last_tile = place_ref[1], place_ref[2] - 1
    tau, pull, step = path_scalars(place_ref, all_ref, tiles, cells)
    live = interior(place_ref)
    step = step * live
    inv = 1.0 / tau
    scal_ref[0] = tau
    scal_ref[1] = pull
    from_p, from_m, from_n = -4.0 * step * inv, step * (inv + pull), step * (inv - pull)
    bend = step * tau

    def update(at, carry):
        for comp in range(3):
            for place in TILES:
                p, m, n, q, r = (
                    tile_of(ref, comp, at, place) for ref in (p_ref, m0_ref, n0_ref, q_ref, r_ref)
                )
                move = (from_p * p + from_m * m) + (from_n * n - step * q) - bend * r
                put(phi_ref, comp, at, place, p + move)
                put(m_ref, comp, at, place, m + move)
                put(n_ref, comp, at, place, n + move)
        return carry

    loop(2, rows - 2, update)
    drives(m_ref, n_ref, coef_ref, fa_ref, fb_ref, fs_ref, sm_ref, sn_ref, 3, rows - 3)
    clear_outside(tile, last_tile, (fa_ref, fb_ref, fs_ref), own)
    rim, inside = gradients(
        phi_ref, m_ref, n_ref, coef_ref, fa_ref, fb_ref, fs_ref, sm_ref, sn_ref, g_ref, tau, pull, 0
    )
    loop(4, HALO, rim)
    total = loop(HALO, HALO + own, inside, jnp.zeros((8, 128), jnp.float32))
    loop(HALO + own, rows - 4, rim)
    clear_outside(tile, last_tile, (g_ref,), own)
    sums = jnp.sum(total, axis=0, keepdims=True) * live
    sums_ref[...] = jnp.broadcast_to(sums, sums_ref.shape)


def step_of(all_ref, cells):
    return step_scale / jnp.sqrt(jnp.sum(all_ref[...]) / cells + epsilon)


def third_kernel(
    cells, place_ref, scal_ref, all_ref, p_ref, m0_ref, n0_ref, h_ref, coef_ref,
    phi_ref, g_ref, sums_ref, m_ref, n_ref, fa_ref, fb_ref, fs_ref, sm_ref, sn_ref
):
    rows = p_ref.shape[1]
    own = rows - 2 * HALO
    tile, last_tile = place_ref[1], place_ref[2] - 1
    live = interior(place_ref)
    tau, pull = scal_ref[0], scal_ref[1]
    step = step_of(all_ref, cells) * live

    def update(at, carry):
        for comp in range(3):
            for place in TILES:
                move = step * tile_of(h_ref, comp, at, place)
                for old, new in ((p_ref, phi_ref), (m0_ref, m_ref), (n0_ref, n_ref)):
                    put(new, comp, at, place, tile_of(old, comp, at, place) - move)
        return carry

    loop(4, rows - 4, update)
    drives(m_ref, n_ref, coef_ref, fa_ref, fb_ref, fs_ref, sm_ref, sn_ref, 5, rows - 5)
    clear_outside(tile, last_tile, (fa_ref, fb_ref, fs_ref), own)
    _, inside = gradients(
        phi_ref, m_ref, n_ref, coef_ref, fa_ref, fb_ref, fs_ref, sm_ref, sn_ref, g_ref, tau, pull,
        HALO,
    )
    total = loop(HALO, HALO + own, inside, jnp.zeros((8, 128), jnp.float32))
    sums = jnp.sum(total, axis=0, keepdims=True) * live
    sums_ref[...] = jnp.broadcast_to(sums, sums_ref.shape)


def last_kernel(cells, place_ref, all_ref, p_ref, g_ref, edge_ref, mid_ref):
    own = g_ref.shape[1]
    step = step_of(all_ref, cells) * interior(place_ref)
    for ref, low, high, shift in (
        (edge_ref, 0, HALO, 0),
        (mid_ref, HALO, own - HALO, HALO),
        (edge_ref, own - HALO, own, own - 2 * HALO),
    ):

        def move(at, carry, ref=ref, shift=shift):
            for comp in range(3):
                for place in TILES:
                    old = tile_of(p_ref, comp, at + HALO, place)
                    put(ref, comp, at - shift, place, old - step * tile_of(g_ref, comp, at, place))
            return carry

        loop(low, high, move)


def f32(*shape):
    return jax.ShapeDtypeStruct(shape, jnp.float32)


def call(kernel, operands, outs, scratch, scalars=1, small_out=()):
    smem = pl.BlockSpec(memory_space=pltpu.SMEM)
    vmem = pl.BlockSpec(memory_space=pltpu.VMEM)
    return pl.pallas_call(
        kernel,
        out_shape=outs,
        in_specs=[smem if i < scalars else vmem for i in range(len(operands))],
        out_specs=[smem if i in small_out else vmem for i in range(len(outs))],
        scratch_shapes=[pltpu.VMEM(shape, jnp.float32) for shape in scratch],
        compiler_params=pltpu.CompilerParams(vmem_limit_bytes=VMEM_LIMIT),
    )(*operands)


def beside(cells, axis, forward):
    count = lax.axis_size(axis)
    pairs = [(i, i + 1) if forward else (i + 1, i) for i in range(count - 1)]
    return lax.ppermute(cells, axis, pairs)


def from_everyone(rows):
    return lax.all_to_all(rows, IMG_TILE, 0, 0, tiled=True)


def body(spins, aniso):
    _, comps, depth, own, width = spins.shape
    images, tiles = lax.axis_size(IMG), lax.axis_size(TILE)
    devices = images * tiles
    cells = float(images * comps * depth * own * tiles * width)
    rows = own + 2 * HALO
    place = jnp.stack(
        [lax.axis_index(IMG), lax.axis_index(TILE), jnp.int32(tiles), jnp.int32(images)]
    ).astype(jnp.int32)
    start = jnp.swapaxes(spins[0], 1, 2)
    coefs = jnp.swapaxes(aniso, 0, 1)
    coefs = jnp.concatenate(
        [beside(coefs[own - HALO :], TILE, True), coefs, beside(coefs[:HALO], TILE, False)]
    )
    edge = jnp.concatenate([start[:, :HALO], start[:, own - HALO :]], axis=1)
    mid = start[:, HALO : own - HALO]
    ext = (3, rows, depth, width)
    whole = f32(*ext)
    table = f32(devices, 128)
    scratch = [ext, ext, ext, ext[1:], ext[1:]]
    for _ in range(OUTER):
        a_edge, b_edge = beside(edge, IMG, True), beside(edge, IMG, False)
        trio = jnp.stack([a_edge, edge, b_edge])
        up = beside(trio[:, :, HALO:], TILE, True)
        down = beside(trio[:, :, :HALO], TILE, False)
        a_mid, b_mid = beside(mid, IMG, True), beside(mid, IMG, False)
        phi, m, n, q, r, sums = call(
            first_kernel,
            [place, edge, mid, a_edge, a_mid, b_edge, b_mid, up, down, coefs],
            [whole, whole, whole, whole, whole, table],
            scratch,
        )
        phi, m, n, g, scal, sums = call(
            lambda *refs: second_kernel(tiles, cells, *refs),
            [place, from_everyone(sums), phi, m, n, q, r, coefs],
            [whole, whole, whole, whole, f32(2), table],
            scratch,
            small_out=(4,),
        )
        phi, g, sums = call(
            lambda *refs: third_kernel(cells, *refs),
            [place, scal, from_everyone(sums), phi, m, n, g, coefs],
            [whole, f32(3, own, depth, width), table],
            [ext, ext, *scratch],
            scalars=2,
        )
        edge, mid = call(
            lambda *refs: last_kernel(cells, *refs),
            [place, from_everyone(sums), phi, g],
            [f32(3, 2 * HALO, depth, width), f32(3, own - 2 * HALO, depth, width)],
            [],
        )
    final = jnp.concatenate([edge[:, :HALO], mid, edge[:, HALO:]], axis=1)
    return jnp.swapaxes(final, 1, 2)[None]


def solution(mesh):
    split = Mesh(mesh.devices.reshape(4, 4, 4, 2), IMG_TILE)
    return jax.shard_map(
        body,
        mesh=split,
        in_specs=(P(IMG, None, None, TILE, None), P(None, TILE, None)),
        out_specs=P(IMG, None, None, TILE, None),
        check_vma=False,
    )
```

```python
import jax
import jax.numpy as jnp
from jax import lax
from jax.experimental import pallas as pl
from jax.experimental.pallas import tpu as pltpu
from jax.sharding import Mesh
from jax.sharding import PartitionSpec as P

OUTER = 2
INNER = 3
IMG = ("img_0", "img_1")
TILE = ("tile_0", "tile_1")
IMG_TILE = ("img_0", "img_1", "tile_0", "tile_1")

spring_coef = 20.0
step_scale = 0.25
epsilon = 1e-06

HALO = 2 * INNER
PRODUCTS = 11
SUBLANES = 2
LANES = 2
TILES = range(SUBLANES * LANES)
VMEM_LIMIT = 24 * 1024 * 1024


def tile_of(ref, comp, at, place):
    z, y = divmod(place, LANES)
    return ref[comp, at, z * 8 : z * 8 + 8, y * 128 : y * 128 + 128]


def put(ref, comp, at, place, cells):
    z, y = divmod(place, LANES)
    ref[comp, at, z * 8 : z * 8 + 8, y * 128 : y * 128 + 128] = cells


def flat_of(ref, at, place):
    z, y = divmod(place, LANES)
    return ref[at, z * 8 : z * 8 + 8, y * 128 : y * 128 + 128]


def put_flat(ref, at, place, cells):
    z, y = divmod(place, LANES)
    ref[at, z * 8 : z * 8 + 8, y * 128 : y * 128 + 128] = cells


def vector(ref, at, place):
    return [tile_of(ref, comp, at, place) for comp in range(3)]


def around(line, axis):
    size = line[0].shape[axis]
    where = lax.broadcasted_iota(jnp.int32, line[0].shape, axis)
    first, last = where == 0, where == size - 1
    later = [pltpu.roll(cells, 1, axis) for cells in line]
    earlier = [pltpu.roll(cells, size - 1, axis) for cells in line]
    later, earlier = [0.0, *later], [*earlier, 0.0]
    return [
        jnp.where(first, later[i], later[i + 1]) + jnp.where(last, earlier[i + 1], earlier[i])
        for i in range(len(line))
    ]


def laplace(ref, comp, at):
    cells = [tile_of(ref, comp, at, place) for place in TILES]
    total = [
        (tile_of(ref, comp, at - 1, place) + tile_of(ref, comp, at + 1, place)) - 6.0 * cells[place]
        for place in TILES
    ]
    for z in range(SUBLANES):
        picked = range(z * LANES, z * LANES + LANES)
        for place, side in zip(picked, around([cells[i] for i in picked], 1)):
            total[place] = total[place] + side
    for y in range(LANES):
        picked = range(y, SUBLANES * LANES, LANES)
        for place, side in zip(picked, around([cells[i] for i in picked], 0)):
            total[place] = total[place] + side
    return cells, total


def dot(left, right):
    return left[0] * right[0] + left[1] * right[1] + left[2] * right[2]


def stiffness(square, coefs):
    plain = 0.5 - 0.125 * square
    return [plain, plain, plain + coefs]


def loop(low, high, body, carry=0):
    return lax.fori_loop(low, high, body, carry, unroll=4)


def clear_outside(tile, last_tile, refs, own):
    rows = refs[0].shape[1]

    @pl.when(tile == 0)
    def _():
        for ref in refs:
            ref[:, 0:HALO] = jnp.zeros((3, HALO) + ref.shape[2:], jnp.float32)

    @pl.when(tile == last_tile)
    def _():
        for ref in refs:
            ref[:, HALO + own :] = jnp.zeros((3, rows - HALO - own) + ref.shape[2:], jnp.float32)


def block(phi_ref, m_ref, n_ref, lm_ref, ln_ref, q_ref, r_ref, coef_ref, offset, scratch, cuts, clear, sums):
    fa_ref, fb_ref, fs_ref, sm_ref, sn_ref = scratch
    rows = phi_ref.shape[1]

    def drive(at, carry):
        for ref, lap_ref, out, squares, before in (
            (m_ref, lm_ref, fa_ref, sm_ref, None),
            (n_ref, ln_ref, fb_ref, sn_ref, (fa_ref, fs_ref)),
        ):
            stiff = []
            for place in TILES:
                cells = vector(ref, at, place)
                square = dot(cells, cells)
                put_flat(squares, at, place, square)
                stiff.append(stiffness(square, flat_of(coef_ref, at + offset, place)))
            for comp in range(3):
                cells, bent = laplace(ref, comp, at)
                for place in TILES:
                    put(lap_ref, comp, at, place, bent[place])
                    total = bent[place] + stiff[place][comp] * cells[place]
                    put(out, comp, at, place, total)
                    if before is not None:
                        total = total + tile_of(fa_ref, comp, at, place)
                        put(fs_ref, comp, at, place, total)
        return carry

    loop(1, rows - 1, drive)
    clear((fa_ref, fb_ref, fs_ref))

    def fields(at, sums):
        adjoint = [laplace(fs_ref, comp, at)[1] for comp in range(3)]
        for place in TILES:
            phi, m, n = (vector(ref, at, place) for ref in (phi_ref, m_ref, n_ref))
            fa, fb = vector(fa_ref, at, place), vector(fb_ref, at, place)
            square_m, square_n = flat_of(sm_ref, at, place), flat_of(sn_ref, at, place)
            coefs = flat_of(coef_ref, at + offset, place)
            stiff_m, stiff_n = stiffness(square_m, coefs), stiffness(square_n, coefs)
            turn_m, turn_n = 0.25 * dot(m, fa), 0.25 * dot(n, fb)
            gap = 0.125 * (square_m - square_n)
            rise_m = 0.25 * dot(m, phi) - 0.125 * square_m
            rise_n = 0.125 * square_n - 0.25 * dot(n, phi)
            flat, bent = [], []
            for c in range(3):
                flat.append(phi[c] * gap + m[c] * rise_m + n[c] * rise_n)
                bent.append(
                    0.25
                    * (
                        adjoint[c][place]
                        + (stiff_m[c] * fa[c] + stiff_n[c] * fb[c])
                        - (m[c] * turn_m + n[c] * turn_n)
                    )
                )
                put(q_ref, c, at, place, flat[c])
                put(r_ref, c, at, place, bent[c])
            if sums:
                behind = [2.0 * one - other for one, other in zip(phi, m)]
                ahead = [other - 2.0 * one for one, other in zip(phi, n)]
                pairs = (
                    (behind, behind), (behind, ahead), (ahead, ahead),
                    (flat, behind), (flat, ahead), (bent, behind), (bent, ahead),
                    (flat, flat), (flat, bent), (bent, bent), (fb, fb),
                )
                sums = [total + dot(left, right) for total, (left, right) in zip(sums, pairs)]
        return sums

    def rim(at, carry):
        fields(at, None)
        return carry

    loop(2, cuts[0], rim)
    sums = loop(cuts[0], cuts[1], fields, sums)
    loop(cuts[1], rows - 2, rim)
    clear((q_ref, r_ref))
    return sums


def join(pieces, outs, low, high, shift):
    own_ref, a_ref, b_ref = pieces
    phi_ref, m_ref, n_ref = outs

    def one(at, carry):
        for comp in range(3):
            for place in TILES:
                phi = tile_of(own_ref, comp, at, place)
                put(phi_ref, comp, at + shift, place, phi)
                put(m_ref, comp, at + shift, place, phi + tile_of(a_ref, comp, at, place))
                put(n_ref, comp, at + shift, place, phi + tile_of(b_ref, comp, at, place))
        return carry

    loop(low, high, one)


def ends_kernel(
    place_ref, own_edge, a_edge, b_edge, up_ref, down_ref, coef_ref,
    phi_ref, m_ref, n_ref, lm_ref, ln_ref, q_ref, r_ref, sums_ref,
    fa_ref, fb_ref, fs_ref, sm_ref, sn_ref
):
    tile, last_tile = place_ref[1], place_ref[2] - 1
    span = 2 * HALO
    fields = (phi_ref, m_ref, n_ref, lm_ref, ln_ref, q_ref, r_ref)
    scratch = (fa_ref, fb_ref, fs_ref, sm_ref, sn_ref)
    halos = [[ref.at[3 * which : 3 * which + 3] for which in (1, 0, 2)] for ref in (up_ref, down_ref)]
    edges = (own_edge, a_edge, b_edge)
    sums = [jnp.zeros((8, 128), jnp.float32)] * PRODUCTS
    for top in (True, False):
        first = 0 if top else span
        here = [ref.at[:, first : first + span] for ref in fields]
        join(halos[0 if top else 1], here[:3], 0, HALO, 0 if top else HALO)
        if top:
            join(edges, here[:3], 0, HALO, HALO)
        else:
            join(edges, here[:3], HALO, span, -HALO)

        def clear(refs, top=top):
            outside = slice(0, HALO) if top else slice(HALO, span)

            @pl.when(tile == (0 if top else last_tile))
            def _():
                for ref in refs:
                    ref[:, outside] = jnp.zeros((3, HALO) + ref.shape[2:], jnp.float32)

        cuts = (HALO, span - 2) if top else (2, HALO)
        offset = 0 if top else coef_ref.shape[0] - span
        sums = block(*here, coef_ref, offset, scratch, cuts, clear, sums)
    for which in range(PRODUCTS):
        sums_ref[which] = sums[which]


def middle_kernel(
    place_ref, own_mid, a_mid, b_mid, phi_end, m_end, n_end, part_ref, coef_ref,
    phi_ref, m_ref, n_ref, lm_ref, ln_ref, q_ref, r_ref, sums_ref,
    fa_ref, fb_ref, fs_ref, sm_ref, sn_ref
):
    span = 2 * HALO
    rows = phi_ref.shape[1]
    outs = (phi_ref, m_ref, n_ref)
    for end, ref in zip((phi_end, m_end, n_end), outs):
        ref[:, 0:4] = end[:, span - 4 : span]
        ref[:, rows - 4 :] = end[:, span : span + 4]
    join((own_mid, a_mid, b_mid), outs, 0, rows - 8, 4)
    sums = block(
        *outs, lm_ref, ln_ref, q_ref, r_ref, coef_ref, span - 4,
        (fa_ref, fb_ref, fs_ref, sm_ref, sn_ref), (2, rows - 2), lambda refs: None,
        [part_ref[which] for which in range(PRODUCTS)],
    )
    lane = lax.broadcasted_iota(jnp.int32, (1, 128), 1)
    result = jnp.zeros((1, 128), jnp.float32)
    for which in range(PRODUCTS):
        result = jnp.where(lane == which, jnp.sum(sums[which]), result)
    sums_ref[...] = jnp.broadcast_to(result, sums_ref.shape)


def path_scalars(place_ref, all_ref, tiles, cells):
    devices = all_ref.shape[0]
    images = devices // tiles
    table = jnp.sum(all_ref[...].reshape(images, tiles, 128), axis=1)
    lane = lax.broadcasted_iota(jnp.int32, (images, 128), 1)
    image = lax.broadcasted_iota(jnp.int32, (images, 128), 0)
    one = image[:, :1]

    def column(which):
        return jnp.sum(jnp.where(lane == which, table, 0.0), axis=1, keepdims=True)

    live = one < images - 1
    seg = jnp.where(live, jnp.sqrt(column(2) + epsilon), 0.0)
    drv = jnp.where(live, jnp.sqrt(0.25 * column(10) + epsilon), 0.0)
    path_len = jnp.sum(seg, axis=0, keepdims=True)
    tau = path_len / jnp.sum(drv, axis=0, keepdims=True)
    before = jnp.sum(jnp.where(image < lane, seg, 0.0), axis=0, keepdims=True)
    before = jnp.sum(jnp.where(image == lane, before, 0.0), axis=1, keepdims=True)
    target = one.astype(jnp.float32) / (images - 1)
    pull = spring_coef * (before / path_len - target) * (images - 1) / (2.0 * path_len)
    inv = 1.0 / tau
    near, far = inv + pull, pull - inv
    norm = near * near * column(0) + far * far * column(2) + 2.0 * near * far * column(1)
    norm += 2.0 * (near * column(3) + far * column(4))
    norm += 2.0 * tau * (near * column(5) + far * column(6))
    norm += column(7) + tau * (2.0 * column(8) + tau * column(9))
    inner = (one > 0) & (one < images - 1)
    total = jnp.sum(jnp.where(inner, norm, 0.0), axis=0, keepdims=True)
    step = step_scale / jnp.sqrt(total / cells + epsilon)
    mine = jnp.sum(jnp.where(one == place_ref[0], pull, 0.0), axis=0, keepdims=True)
    return tau[0, 0], mine[0, 0], step[0, 0]


def gradients(
    phi_ref, m_ref, n_ref, coef_ref, fa_ref, fb_ref, fs_ref, sm_ref, sn_ref, g_ref, tau, pull, out
):
    inv = 1.0 / tau
    turned = 0.25 * tau

    def grad(at, total):
        adjoint = [laplace(fs_ref, comp, at)[1] for comp in range(3)]
        for place in TILES:
            phi, m, n = (vector(ref, at, place) for ref in (phi_ref, m_ref, n_ref))
            fa, fb = vector(fa_ref, at, place), vector(fb_ref, at, place)
            square_m, square_n = flat_of(sm_ref, at, place), flat_of(sn_ref, at, place)
            coefs = flat_of(coef_ref, at, place)
            stiff_m, stiff_n = stiffness(square_m, coefs), stiffness(square_n, coefs)
            gap = 0.125 * (square_m - square_n) + 4.0 * inv
            lean_m = (
                0.25 * (dot(m, phi) - turned * dot(m, fa)) - 0.125 * square_m - (pull + inv)
            )
            lean_n = (
                0.125 * square_n - 0.25 * (dot(n, phi) + turned * dot(n, fb)) + (pull - inv)
            )
            cells = [
                phi[c] * gap
                + (m[c] * lean_m + n[c] * lean_n)
                + turned * (adjoint[c][place] + (stiff_m[c] * fa[c] + stiff_n[c] * fb[c]))
                for c in range(3)
            ]
            for c in range(3):
                put(g_ref, c, at - out, place, cells[c])
            total = total + dot(cells, cells)
        return total

    def rim(at, carry):
        grad(at, 0.0)
        return carry

    return rim, grad


def interior(place_ref):
    return jnp.where((place_ref[0] > 0) & (place_ref[0] < place_ref[3] - 1), 1.0, 0.0)


def advance(
    step_ref, scale, old, old_shift, new, coef_ref, scratch, low, high, keep
):
    p_ref, m0_ref, n0_ref, lm0_ref, ln0_ref = old
    phi_ref, m_ref, n_ref, lm_ref, ln_ref = new
    fa_ref, fb_ref, fs_ref, sm_ref, sn_ref = scratch

    def body(at, carry):
        was = at + old_shift
        moves, bends = [], []
        for comp in range(3):
            cells, bent = laplace(step_ref, comp, at)
            if scale is not None:
                cells, bent = [scale * cell for cell in cells], [scale * cell for cell in bent]
            moves.append(cells)
            bends.append(bent)
            for place in TILES:
                put(phi_ref, comp, at, place, tile_of(p_ref, comp, was, place) + cells[place])
        for ref, lap_old, out, lap_new, drive_ref, squares, last in (
            (m0_ref, lm0_ref, m_ref, lm_ref, fa_ref, sm_ref, False),
            (n0_ref, ln0_ref, n_ref, ln_ref, fb_ref, sn_ref, True),
        ):
            for place in TILES:
                cells = [tile_of(ref, comp, was, place) + moves[comp][place] for comp in range(3)]
                square = dot(cells, cells)
                put_flat(squares, at, place, square)
                stiff = stiffness(square, flat_of(coef_ref, at, place))
                for comp in range(3):
                    put(out, comp, at, place, cells[comp])
                    bent = tile_of(lap_old, comp, was, place) + bends[comp][place]
                    if keep:
                        put(lap_new, comp, at, place, bent)
                    total = bent + stiff[comp] * cells[comp]
                    put(drive_ref, comp, at, place, total)
                    if last:
                        total = total + tile_of(fa_ref, comp, at, place)
                        put(fs_ref, comp, at, place, total)
        return carry

    loop(low, high, body)


def second_kernel(tiles, cells, place_ref, all_ref, *refs):
    ends, mids, refs = refs[:7], refs[7:14], refs[14:]
    coef_ref, phi_ref, m_ref, n_ref, lm_ref, ln_ref, g_ref, scal_ref, sums_ref, d_ref = refs[:10]
    scratch = refs[10:]
    rows = phi_ref.shape[1]
    own = rows - 2 * HALO
    span = 2 * HALO
    tile, last_tile = place_ref[1], place_ref[2] - 1
    tau, pull, step = path_scalars(place_ref, all_ref, tiles, cells)
    live = interior(place_ref)
    step = step * live
    inv = 1.0 / tau
    scal_ref[0] = tau
    scal_ref[1] = pull
    from_p, from_m, from_n = -4.0 * step * inv, step * (inv + pull), step * (inv - pull)
    bend = step * tau
    regions = (
        (ends, 2, span - 2, 0),
        (mids, span - 2, rows - span + 2, 4 - span),
        (ends, rows - span + 2, rows - 2, 2 * span - rows),
    )
    for here, low, high, shift in regions:

        def direction(at, carry, here=here, shift=shift):
            was = at + shift
            for comp in range(3):
                for place in TILES:
                    p, m, n, q, r = (
                        tile_of(here[i], comp, was, place) for i in (0, 1, 2, 5, 6)
                    )
                    move = (from_p * p + from_m * m) + (from_n * n - step * q) - bend * r
                    put(d_ref, comp, at, place, move)
            return carry

        loop(low, high, direction)
    new = (phi_ref, m_ref, n_ref, lm_ref, ln_ref)
    for here, low, high, shift in regions:
        low, high = max(low, 3), min(high, rows - 3)
        advance(d_ref, None, here[:5], shift, new, coef_ref, scratch, low, high, True)
    fa_ref, fb_ref, fs_ref, sm_ref, sn_ref = scratch
    clear_outside(tile, last_tile, (fa_ref, fb_ref, fs_ref), own)
    rim, inside = gradients(
        phi_ref, m_ref, n_ref, coef_ref, fa_ref, fb_ref, fs_ref, sm_ref, sn_ref, g_ref, tau, pull, 0
    )
    loop(4, HALO, rim)
    total = loop(HALO, HALO + own, inside, jnp.zeros((8, 128), jnp.float32))
    loop(HALO + own, rows - 4, rim)
    clear_outside(tile, last_tile, (g_ref,), own)
    sums = jnp.sum(total, axis=0, keepdims=True) * live
    sums_ref[...] = jnp.broadcast_to(sums, sums_ref.shape)


def step_of(all_ref, cells):
    return step_scale / jnp.sqrt(jnp.sum(all_ref[...]) / cells + epsilon)


def third_kernel(
    cells, place_ref, scal_ref, all_ref, p_ref, m0_ref, n0_ref, lm0_ref, ln0_ref, h_ref, coef_ref,
    phi_ref, g_ref, sums_ref, m_ref, n_ref, fa_ref, fb_ref, fs_ref, sm_ref, sn_ref
):
    rows = p_ref.shape[1]
    own = rows - 2 * HALO
    tile, last_tile = place_ref[1], place_ref[2] - 1
    live = interior(place_ref)
    tau, pull = scal_ref[0], scal_ref[1]
    step = step_of(all_ref, cells) * live
    advance(
        h_ref, -step, (p_ref, m0_ref, n0_ref, lm0_ref, ln0_ref), 0,
        (phi_ref, m_ref, n_ref, None, None), coef_ref,
        (fa_ref, fb_ref, fs_ref, sm_ref, sn_ref), HALO - 1, HALO + own + 1, False,
    )
    clear_outside(tile, last_tile, (fa_ref, fb_ref, fs_ref), own)
    _, inside = gradients(
        phi_ref, m_ref, n_ref, coef_ref, fa_ref, fb_ref, fs_ref, sm_ref, sn_ref, g_ref, tau, pull,
        HALO,
    )
    total = loop(HALO, HALO + own, inside, jnp.zeros((8, 128), jnp.float32))
    sums = jnp.sum(total, axis=0, keepdims=True) * live
    sums_ref[...] = jnp.broadcast_to(sums, sums_ref.shape)


def last_kernel(cells, place_ref, all_ref, p_ref, g_ref, edge_ref, mid_ref):
    own = g_ref.shape[1]
    step = step_of(all_ref, cells) * interior(place_ref)
    for ref, low, high, shift in (
        (edge_ref, 0, HALO, 0),
        (mid_ref, HALO, own - HALO, HALO),
        (edge_ref, own - HALO, own, own - 2 * HALO),
    ):

        def move(at, carry, ref=ref, shift=shift):
            for comp in range(3):
                for place in TILES:
                    old = tile_of(p_ref, comp, at + HALO, place)
                    put(ref, comp, at - shift, place, old - step * tile_of(g_ref, comp, at, place))
            return carry

        loop(low, high, move)


def f32(*shape):
    return jax.ShapeDtypeStruct(shape, jnp.float32)


def call(kernel, operands, outs, scratch, scalars=1, small_out=()):
    smem = pl.BlockSpec(memory_space=pltpu.SMEM)
    vmem = pl.BlockSpec(memory_space=pltpu.VMEM)
    return pl.pallas_call(
        kernel,
        out_shape=outs,
        in_specs=[smem if i < scalars else vmem for i in range(len(operands))],
        out_specs=[smem if i in small_out else vmem for i in range(len(outs))],
        scratch_shapes=[pltpu.VMEM(shape, jnp.float32) for shape in scratch],
        compiler_params=pltpu.CompilerParams(vmem_limit_bytes=VMEM_LIMIT),
    )(*operands)


def beside(cells, axis, forward):
    count = lax.axis_size(axis)
    pairs = [(i, i + 1) if forward else (i + 1, i) for i in range(count - 1)]
    return lax.ppermute(cells, axis, pairs)


def from_everyone(rows):
    return lax.all_to_all(rows, IMG_TILE, 0, 0, tiled=True)


def body(spins, aniso):
    _, comps, depth, own, width = spins.shape
    images, tiles = lax.axis_size(IMG), lax.axis_size(TILE)
    devices = images * tiles
    cells = float(images * comps * depth * own * tiles * width)
    rows = own + 2 * HALO
    place = jnp.stack(
        [lax.axis_index(IMG), lax.axis_index(TILE), jnp.int32(tiles), jnp.int32(images)]
    ).astype(jnp.int32)
    start = jnp.swapaxes(spins[0], 1, 2)
    coefs = jnp.swapaxes(aniso, 0, 1)
    edge = jnp.concatenate([start[:, :HALO], start[:, own - HALO :]], axis=1)
    mid = start[:, HALO : own - HALO]
    ext = (3, rows, depth, width)
    ends, middle = (3, 4 * HALO, depth, width), (3, own - 4, depth, width)
    whole = f32(*ext)
    table = f32(devices, 128)
    coef_ext = None

    def scratch(count):
        return [(3, count, depth, width)] * 3 + [(count, depth, width)] * 2

    for _ in range(OUTER):
        a_edge, b_edge = beside(edge, IMG, True), beside(edge, IMG, False)
        a_mid, b_mid = beside(mid, IMG, True), beside(mid, IMG, False)
        heads = [cells_[:, :HALO] for cells_ in (a_edge, edge, b_edge)]
        tails = [cells_[:, HALO:] for cells_ in (a_edge, edge, b_edge)]
        if coef_ext is None:
            heads.append(coefs[None, :HALO])
            tails.append(coefs[None, own - HALO :])
        up = beside(jnp.concatenate(tails), TILE, True)
        down = beside(jnp.concatenate(heads), TILE, False)
        if coef_ext is None:
            coef_ext = jnp.concatenate([up[9], coefs, down[9]])
        *far, part = call(
            ends_kernel,
            [place, edge, a_edge, b_edge, up, down, coef_ext],
            [f32(*ends)] * 7 + [f32(PRODUCTS, 8, 128)],
            scratch(2 * HALO),
        )
        *near, sums = call(
            middle_kernel,
            [place, mid, a_mid, b_mid, *far[:3], part, coef_ext],
            [f32(*middle)] * 7 + [table],
            scratch(own - 4),
        )
        phi, m, n, lm, ln, g, scal, sums = call(
            lambda *refs: second_kernel(tiles, cells, *refs),
            [place, from_everyone(sums), *far, *near, coef_ext],
            [whole] * 6 + [f32(2), table],
            [ext, *scratch(rows)],
            small_out=(6,),
        )
        phi, g, sums = call(
            lambda *refs: third_kernel(cells, *refs),
            [place, scal, from_everyone(sums), phi, m, n, lm, ln, g, coef_ext],
            [whole, f32(3, own, depth, width), table],
            [ext, ext, *scratch(rows)],
            scalars=2,
        )
        edge, mid = call(
            lambda *refs: last_kernel(cells, *refs),
            [place, from_everyone(sums), phi, g],
            [f32(3, 2 * HALO, depth, width), f32(3, own - 2 * HALO, depth, width)],
            [],
        )
    final = jnp.concatenate([edge[:, :HALO], mid, edge[:, HALO:]], axis=1)
    return jnp.swapaxes(final, 1, 2)[None]


def solution(mesh):
    split = Mesh(mesh.devices.reshape(4, 4, 4, 2), IMG_TILE)
    return jax.shard_map(
        body,
        mesh=split,
        in_specs=(P(IMG, None, None, TILE, None), P(None, TILE, None)),
        out_specs=P(IMG, None, None, TILE, None),
        check_vma=False,
    )
```

```python
import jax
import jax.numpy as jnp
from jax import lax
from jax.experimental import pallas as pl
from jax.experimental.pallas import tpu as pltpu
from jax.sharding import Mesh
from jax.sharding import PartitionSpec as P

OUTER = 2
INNER = 3
IMG = ("img_0", "img_1")
TILE = ("tile_0", "tile_1")
IMG_TILE = ("img_0", "img_1", "tile_0", "tile_1")

spring_coef = 20.0
step_scale = 0.25
epsilon = 1e-06

HALO = 2 * INNER
PRODUCTS = 11
SUBLANES = 2
LANES = 2
TILES = range(SUBLANES * LANES)
VMEM_LIMIT = 16 * 1024 * 1024


def tile_of(ref, comp, at, place):
    z, y = divmod(place, LANES)
    return ref[comp, at, z * 8 : z * 8 + 8, y * 128 : y * 128 + 128]


def put(ref, comp, at, place, cells):
    z, y = divmod(place, LANES)
    ref[comp, at, z * 8 : z * 8 + 8, y * 128 : y * 128 + 128] = cells


def flat_of(ref, at, place):
    z, y = divmod(place, LANES)
    return ref[at, z * 8 : z * 8 + 8, y * 128 : y * 128 + 128]


def put_flat(ref, at, place, cells):
    z, y = divmod(place, LANES)
    ref[at, z * 8 : z * 8 + 8, y * 128 : y * 128 + 128] = cells


def vector(ref, at, place):
    return [tile_of(ref, comp, at, place) for comp in range(3)]


def around(line, axis):
    size = line[0].shape[axis]
    where = lax.broadcasted_iota(jnp.int32, line[0].shape, axis)
    first, last = where == 0, where == size - 1
    later = [pltpu.roll(cells, 1, axis) for cells in line]
    earlier = [pltpu.roll(cells, size - 1, axis) for cells in line]
    later, earlier = [0.0, *later], [*earlier, 0.0]
    return [
        jnp.where(first, later[i], later[i + 1]) + jnp.where(last, earlier[i + 1], earlier[i])
        for i in range(len(line))
    ]


def laplace(ref, comp, at):
    cells = [tile_of(ref, comp, at, place) for place in TILES]
    total = [
        (tile_of(ref, comp, at - 1, place) + tile_of(ref, comp, at + 1, place)) - 6.0 * cells[place]
        for place in TILES
    ]
    for z in range(SUBLANES):
        picked = range(z * LANES, z * LANES + LANES)
        for place, side in zip(picked, around([cells[i] for i in picked], 1)):
            total[place] = total[place] + side
    for y in range(LANES):
        picked = range(y, SUBLANES * LANES, LANES)
        for place, side in zip(picked, around([cells[i] for i in picked], 0)):
            total[place] = total[place] + side
    return cells, total


def dot(left, right):
    return left[0] * right[0] + left[1] * right[1] + left[2] * right[2]


def stiffness(square, coefs):
    plain = 0.5 - 0.125 * square
    return [plain, plain, plain + coefs]


def loop(low, high, body, carry=0):
    return lax.fori_loop(low, high, body, carry, unroll=4)


def clear_outside(tile, last_tile, refs, own):
    rows = refs[0].shape[1]

    @pl.when(tile == 0)
    def _():
        for ref in refs:
            ref[:, 0:HALO] = jnp.zeros((3, HALO) + ref.shape[2:], jnp.float32)

    @pl.when(tile == last_tile)
    def _():
        for ref in refs:
            ref[:, HALO + own :] = jnp.zeros((3, rows - HALO - own) + ref.shape[2:], jnp.float32)


def block(phi_ref, m_ref, n_ref, lm_ref, ln_ref, q_ref, r_ref, coef_ref, offset, scratch, cuts, clear, sums):
    fa_ref, fb_ref, fs_ref, sm_ref, sn_ref = scratch
    rows = phi_ref.shape[1]

    def drive(at, carry):
        for ref, lap_ref, out, squares, before in (
            (m_ref, lm_ref, fa_ref, sm_ref, None),
            (n_ref, ln_ref, fb_ref, sn_ref, (fa_ref, fs_ref)),
        ):
            stiff = []
            for place in TILES:
                cells = vector(ref, at, place)
                square = dot(cells, cells)
                put_flat(squares, at, place, square)
                stiff.append(stiffness(square, flat_of(coef_ref, at + offset, place)))
            for comp in range(3):
                cells, bent = laplace(ref, comp, at)
                for place in TILES:
                    put(lap_ref, comp, at, place, bent[place])
                    total = bent[place] + stiff[place][comp] * cells[place]
                    put(out, comp, at, place, total)
                    if before is not None:
                        total = total + tile_of(fa_ref, comp, at, place)
                        put(fs_ref, comp, at, place, total)
        return carry

    loop(1, rows - 1, drive)
    clear((fa_ref, fb_ref, fs_ref))

    def fields(at, sums):
        adjoint = [laplace(fs_ref, comp, at)[1] for comp in range(3)]
        for place in TILES:
            phi, m, n = (vector(ref, at, place) for ref in (phi_ref, m_ref, n_ref))
            fa, fb = vector(fa_ref, at, place), vector(fb_ref, at, place)
            square_m, square_n = flat_of(sm_ref, at, place), flat_of(sn_ref, at, place)
            coefs = flat_of(coef_ref, at + offset, place)
            stiff_m, stiff_n = stiffness(square_m, coefs), stiffness(square_n, coefs)
            turn_m, turn_n = 0.25 * dot(m, fa), 0.25 * dot(n, fb)
            gap = 0.125 * (square_m - square_n)
            rise_m = 0.25 * dot(m, phi) - 0.125 * square_m
            rise_n = 0.125 * square_n - 0.25 * dot(n, phi)
            flat, bent = [], []
            for c in range(3):
                flat.append(phi[c] * gap + m[c] * rise_m + n[c] * rise_n)
                bent.append(
                    0.25
                    * (
                        adjoint[c][place]
                        + (stiff_m[c] * fa[c] + stiff_n[c] * fb[c])
                        - (m[c] * turn_m + n[c] * turn_n)
                    )
                )
                put(q_ref, c, at, place, flat[c])
                put(r_ref, c, at, place, bent[c])
            if sums:
                behind = [2.0 * one - other for one, other in zip(phi, m)]
                ahead = [other - 2.0 * one for one, other in zip(phi, n)]
                pairs = (
                    (behind, behind), (behind, ahead), (ahead, ahead),
                    (flat, behind), (flat, ahead), (bent, behind), (bent, ahead),
                    (flat, flat), (flat, bent), (bent, bent), (fb, fb),
                )
                sums = [total + dot(left, right) for total, (left, right) in zip(sums, pairs)]
        return sums

    def rim(at, carry):
        fields(at, None)
        return carry

    loop(2, cuts[0], rim)
    sums = loop(cuts[0], cuts[1], fields, sums)
    loop(cuts[1], rows - 2, rim)
    clear((q_ref, r_ref))
    return sums


def join(pieces, outs, low, high, shift):
    own_ref, a_ref, b_ref = pieces
    phi_ref, m_ref, n_ref = outs

    def one(at, carry):
        for comp in range(3):
            for place in TILES:
                phi = tile_of(own_ref, comp, at, place)
                put(phi_ref, comp, at + shift, place, phi)
                put(m_ref, comp, at + shift, place, phi + tile_of(a_ref, comp, at, place))
                put(n_ref, comp, at + shift, place, phi + tile_of(b_ref, comp, at, place))
        return carry

    loop(low, high, one)


def first_ends_kernel(
    place_ref, own_edge, a_edge, b_edge, up_ref, down_ref, coef_up, coef_ref, coef_down, *refs
):
    own = coef_ref.shape[0]
    coef_out, refs = refs[8], refs[:8] + refs[9:]
    coef_out[0:HALO] = coef_up[...]
    coef_out[HALO : HALO + own] = coef_ref[...]
    coef_out[HALO + own :] = coef_down[...]
    ends_kernel(place_ref, own_edge, a_edge, b_edge, up_ref, down_ref, coef_out, *refs)


def ends_kernel(
    place_ref, own_edge, a_edge, b_edge, up_ref, down_ref, coef_ref,
    phi_ref, m_ref, n_ref, lm_ref, ln_ref, q_ref, r_ref, sums_ref,
    fa_ref, fb_ref, fs_ref, sm_ref, sn_ref
):
    tile, last_tile = place_ref[1], place_ref[2] - 1
    span = 2 * HALO
    fields = (phi_ref, m_ref, n_ref, lm_ref, ln_ref, q_ref, r_ref)
    scratch = (fa_ref, fb_ref, fs_ref, sm_ref, sn_ref)
    halos = [[ref.at[3 * which : 3 * which + 3] for which in (1, 0, 2)] for ref in (up_ref, down_ref)]
    edges = (own_edge, a_edge, b_edge)
    sums = [jnp.zeros((8, 128), jnp.float32)] * PRODUCTS
    for top in (True, False):
        first = 0 if top else span
        here = [ref.at[:, first : first + span] for ref in fields]
        join(halos[0 if top else 1], here[:3], 0, HALO, 0 if top else HALO)
        if top:
            join(edges, here[:3], 0, HALO, HALO)
        else:
            join(edges, here[:3], HALO, span, -HALO)

        def clear(refs, top=top):
            outside = slice(0, HALO) if top else slice(HALO, span)

            @pl.when(tile == (0 if top else last_tile))
            def _():
                for ref in refs:
                    ref[:, outside] = jnp.zeros((3, HALO) + ref.shape[2:], jnp.float32)

        cuts = (HALO, span - 2) if top else (2, HALO)
        offset = 0 if top else coef_ref.shape[0] - span
        sums = block(*here, coef_ref, offset, scratch, cuts, clear, sums)
    for which in range(PRODUCTS):
        sums_ref[which] = sums[which]


def middle_kernel(
    place_ref, own_mid, a_mid, b_mid, phi_end, m_end, n_end, part_ref, coef_ref,
    phi_ref, m_ref, n_ref, lm_ref, ln_ref, q_ref, r_ref, sums_ref,
    fa_ref, fb_ref, fs_ref, sm_ref, sn_ref
):
    span = 2 * HALO
    rows = phi_ref.shape[1]
    outs = (phi_ref, m_ref, n_ref)
    for end, ref in zip((phi_end, m_end, n_end), outs):
        ref[:, 0:4] = end[:, span - 4 : span]
        ref[:, rows - 4 :] = end[:, span : span + 4]
    join((own_mid, a_mid, b_mid), outs, 0, rows - 8, 4)
    sums = block(
        *outs, lm_ref, ln_ref, q_ref, r_ref, coef_ref, span - 4,
        (fa_ref, fb_ref, fs_ref, sm_ref, sn_ref), (2, rows - 2), lambda refs: None,
        [part_ref[which] for which in range(PRODUCTS)],
    )
    lane = lax.broadcasted_iota(jnp.int32, (1, 128), 1)
    result = jnp.zeros((1, 128), jnp.float32)
    for which in range(PRODUCTS):
        result = jnp.where(lane == which, jnp.sum(sums[which]), result)
    sums_ref[...] = jnp.broadcast_to(result, sums_ref.shape)


def path_scalars(place_ref, all_ref, tiles, cells):
    devices = all_ref.shape[0]
    images = devices // tiles
    table = jnp.sum(all_ref[...].reshape(images, tiles, 128), axis=1)
    lane = lax.broadcasted_iota(jnp.int32, (images, 128), 1)
    image = lax.broadcasted_iota(jnp.int32, (images, 128), 0)
    one = image[:, :1]

    def column(which):
        return jnp.sum(jnp.where(lane == which, table, 0.0), axis=1, keepdims=True)

    live = one < images - 1
    seg = jnp.where(live, jnp.sqrt(column(2) + epsilon), 0.0)
    drv = jnp.where(live, jnp.sqrt(0.25 * column(10) + epsilon), 0.0)
    path_len = jnp.sum(seg, axis=0, keepdims=True)
    tau = path_len / jnp.sum(drv, axis=0, keepdims=True)
    before = jnp.sum(jnp.where(image < lane, seg, 0.0), axis=0, keepdims=True)
    before = jnp.sum(jnp.where(image == lane, before, 0.0), axis=1, keepdims=True)
    target = one.astype(jnp.float32) / (images - 1)
    pull = spring_coef * (before / path_len - target) * (images - 1) / (2.0 * path_len)
    inv = 1.0 / tau
    near, far = inv + pull, pull - inv
    norm = near * near * column(0) + far * far * column(2) + 2.0 * near * far * column(1)
    norm += 2.0 * (near * column(3) + far * column(4))
    norm += 2.0 * tau * (near * column(5) + far * column(6))
    norm += column(7) + tau * (2.0 * column(8) + tau * column(9))
    inner = (one > 0) & (one < images - 1)
    total = jnp.sum(jnp.where(inner, norm, 0.0), axis=0, keepdims=True)
    step = step_scale / jnp.sqrt(total / cells + epsilon)
    mine = jnp.sum(jnp.where(one == place_ref[0], pull, 0.0), axis=0, keepdims=True)
    return tau[0, 0], mine[0, 0], step[0, 0]


def gradients(
    phi_ref, m_ref, n_ref, coef_ref, fa_ref, fb_ref, fs_ref, sm_ref, sn_ref, g_ref, tau, pull, out
):
    inv = 1.0 / tau
    turned = 0.25 * tau

    def grad(at, total):
        adjoint = [laplace(fs_ref, comp, at)[1] for comp in range(3)]
        for place in TILES:
            phi, m, n = (vector(ref, at, place) for ref in (phi_ref, m_ref, n_ref))
            fa, fb = vector(fa_ref, at, place), vector(fb_ref, at, place)
            square_m, square_n = flat_of(sm_ref, at, place), flat_of(sn_ref, at, place)
            coefs = flat_of(coef_ref, at, place)
            stiff_m, stiff_n = stiffness(square_m, coefs), stiffness(square_n, coefs)
            gap = 0.125 * (square_m - square_n) + 4.0 * inv
            lean_m = (
                0.25 * (dot(m, phi) - turned * dot(m, fa)) - 0.125 * square_m - (pull + inv)
            )
            lean_n = (
                0.125 * square_n - 0.25 * (dot(n, phi) + turned * dot(n, fb)) + (pull - inv)
            )
            cells = [
                phi[c] * gap
                + (m[c] * lean_m + n[c] * lean_n)
                + turned * (adjoint[c][place] + (stiff_m[c] * fa[c] + stiff_n[c] * fb[c]))
                for c in range(3)
            ]
            for c in range(3):
                put(g_ref, c, at - out, place, cells[c])
            total = total + dot(cells, cells)
        return total

    def rim(at, carry):
        grad(at, 0.0)
        return carry

    return rim, grad


def interior(place_ref):
    return jnp.where((place_ref[0] > 0) & (place_ref[0] < place_ref[3] - 1), 1.0, 0.0)


def advance(
    step_ref, scale, old, old_shift, new, coef_ref, scratch, low, high, keep
):
    p_ref, m0_ref, n0_ref, lm0_ref, ln0_ref = old
    phi_ref, m_ref, n_ref, lm_ref, ln_ref = new
    fa_ref, fb_ref, fs_ref, sm_ref, sn_ref = scratch

    def body(at, carry):
        was = at + old_shift
        moves, bends = [], []
        for comp in range(3):
            cells, bent = laplace(step_ref, comp, at)
            if scale is not None:
                cells, bent = [scale * cell for cell in cells], [scale * cell for cell in bent]
            moves.append(cells)
            bends.append(bent)
            for place in TILES:
                put(phi_ref, comp, at, place, tile_of(p_ref, comp, was, place) + cells[place])
        for ref, lap_old, out, lap_new, drive_ref, squares, last in (
            (m0_ref, lm0_ref, m_ref, lm_ref, fa_ref, sm_ref, False),
            (n0_ref, ln0_ref, n_ref, ln_ref, fb_ref, sn_ref, True),
        ):
            for place in TILES:
                cells = [tile_of(ref, comp, was, place) + moves[comp][place] for comp in range(3)]
                square = dot(cells, cells)
                put_flat(squares, at, place, square)
                stiff = stiffness(square, flat_of(coef_ref, at, place))
                for comp in range(3):
                    put(out, comp, at, place, cells[comp])
                    bent = tile_of(lap_old, comp, was, place) + bends[comp][place]
                    if keep:
                        put(lap_new, comp, at, place, bent)
                    total = bent + stiff[comp] * cells[comp]
                    put(drive_ref, comp, at, place, total)
                    if last:
                        total = total + tile_of(fa_ref, comp, at, place)
                        put(fs_ref, comp, at, place, total)
        return carry

    loop(low, high, body)


def second_kernel(tiles, cells, place_ref, all_ref, *refs):
    ends, mids, refs = refs[:7], refs[7:14], refs[14:]
    coef_ref, phi_ref, m_ref, n_ref, lm_ref, ln_ref, g_ref, scal_ref, sums_ref, d_ref = refs[:10]
    scratch = refs[10:]
    rows = phi_ref.shape[1]
    own = rows - 2 * HALO
    span = 2 * HALO
    tile, last_tile = place_ref[1], place_ref[2] - 1
    tau, pull, step = path_scalars(place_ref, all_ref, tiles, cells)
    live = interior(place_ref)
    step = step * live
    inv = 1.0 / tau
    scal_ref[0] = tau
    scal_ref[1] = pull
    from_p, from_m, from_n = -4.0 * step * inv, step * (inv + pull), step * (inv - pull)
    bend = step * tau
    regions = (
        (ends, 2, span - 2, 0),
        (mids, span - 2, rows - span + 2, 4 - span),
        (ends, rows - span + 2, rows - 2, 2 * span - rows),
    )
    for here, low, high, shift in regions:

        def direction(at, carry, here=here, shift=shift):
            was = at + shift
            for comp in range(3):
                for place in TILES:
                    p, m, n, q, r = (
                        tile_of(here[i], comp, was, place) for i in (0, 1, 2, 5, 6)
                    )
                    move = (from_p * p + from_m * m) + (from_n * n - step * q) - bend * r
                    put(d_ref, comp, at, place, move)
            return carry

        loop(low, high, direction)
    new = (phi_ref, m_ref, n_ref, lm_ref, ln_ref)
    for here, low, high, shift in regions:
        low, high = max(low, 3), min(high, rows - 3)
        advance(d_ref, None, here[:5], shift, new, coef_ref, scratch, low, high, True)
    fa_ref, fb_ref, fs_ref, sm_ref, sn_ref = scratch
    clear_outside(tile, last_tile, (fa_ref, fb_ref, fs_ref), own)
    rim, inside = gradients(
        phi_ref, m_ref, n_ref, coef_ref, fa_ref, fb_ref, fs_ref, sm_ref, sn_ref, g_ref, tau, pull, 0
    )
    loop(4, HALO, rim)
    total = loop(HALO, HALO + own, inside, jnp.zeros((8, 128), jnp.float32))
    loop(HALO + own, rows - 4, rim)
    clear_outside(tile, last_tile, (g_ref,), own)
    sums = jnp.sum(total, axis=0, keepdims=True) * live
    sums_ref[...] = jnp.broadcast_to(sums, sums_ref.shape)


def step_of(all_ref, cells):
    return step_scale / jnp.sqrt(jnp.sum(all_ref[...]) / cells + epsilon)


def third_kernel(
    cells, place_ref, scal_ref, all_ref, p_ref, m0_ref, n0_ref, lm0_ref, ln0_ref, h_ref, coef_ref,
    phi_ref, g_ref, sums_ref, m_ref, n_ref, fa_ref, fb_ref, fs_ref, sm_ref, sn_ref
):
    rows = p_ref.shape[1]
    own = rows - 2 * HALO
    tile, last_tile = place_ref[1], place_ref[2] - 1
    live = interior(place_ref)
    tau, pull = scal_ref[0], scal_ref[1]
    step = step_of(all_ref, cells) * live
    advance(
        h_ref, -step, (p_ref, m0_ref, n0_ref, lm0_ref, ln0_ref), 0,
        (phi_ref, m_ref, n_ref, None, None), coef_ref,
        (fa_ref, fb_ref, fs_ref, sm_ref, sn_ref), HALO - 1, HALO + own + 1, False,
    )
    clear_outside(tile, last_tile, (fa_ref, fb_ref, fs_ref), own)
    _, inside = gradients(
        phi_ref, m_ref, n_ref, coef_ref, fa_ref, fb_ref, fs_ref, sm_ref, sn_ref, g_ref, tau, pull,
        HALO,
    )
    total = loop(HALO, HALO + own, inside, jnp.zeros((8, 128), jnp.float32))
    sums = jnp.sum(total, axis=0, keepdims=True) * live
    sums_ref[...] = jnp.broadcast_to(sums, sums_ref.shape)


def last_kernel(cells, place_ref, all_ref, p_ref, g_ref, edge_ref, mid_ref):
    own = g_ref.shape[1]
    step = step_of(all_ref, cells) * interior(place_ref)
    for ref, low, high, shift in (
        (edge_ref, 0, HALO, 0),
        (mid_ref, HALO, own - HALO, HALO),
        (edge_ref, own - HALO, own, own - 2 * HALO),
    ):

        def move(at, carry, ref=ref, shift=shift):
            for comp in range(3):
                for place in TILES:
                    old = tile_of(p_ref, comp, at + HALO, place)
                    put(ref, comp, at - shift, place, old - step * tile_of(g_ref, comp, at, place))
            return carry

        loop(low, high, move)


def f32(*shape):
    return jax.ShapeDtypeStruct(shape, jnp.float32)


def call(kernel, operands, outs, scratch, scalars=1, small_out=()):
    smem = pl.BlockSpec(memory_space=pltpu.SMEM)
    vmem = pl.BlockSpec(memory_space=pltpu.VMEM)
    return pl.pallas_call(
        kernel,
        out_shape=outs,
        in_specs=[smem if i < scalars else vmem for i in range(len(operands))],
        out_specs=[smem if i in small_out else vmem for i in range(len(outs))],
        scratch_shapes=[pltpu.VMEM(shape, jnp.float32) for shape in scratch],
        compiler_params=pltpu.CompilerParams(vmem_limit_bytes=VMEM_LIMIT),
    )(*operands)


def beside(cells, axis, forward):
    count = lax.axis_size(axis)
    pairs = [(i, i + 1) if forward else (i + 1, i) for i in range(count - 1)]
    return lax.ppermute(cells, axis, pairs)


def from_everyone(rows):
    return lax.all_to_all(rows, IMG_TILE, 0, 0, tiled=True)


def body(spins, aniso):
    _, comps, depth, own, width = spins.shape
    images, tiles = lax.axis_size(IMG), lax.axis_size(TILE)
    devices = images * tiles
    cells = float(images * comps * depth * own * tiles * width)
    rows = own + 2 * HALO
    place = jnp.stack(
        [lax.axis_index(IMG), lax.axis_index(TILE), jnp.int32(tiles), jnp.int32(images)]
    ).astype(jnp.int32)
    start = jnp.swapaxes(spins[0], 1, 2)
    coefs = jnp.swapaxes(aniso, 0, 1)
    edge = jnp.concatenate([start[:, :HALO], start[:, own - HALO :]], axis=1)
    mid = start[:, HALO : own - HALO]
    ext = (3, rows, depth, width)
    ends, middle = (3, 4 * HALO, depth, width), (3, own - 4, depth, width)
    whole = f32(*ext)
    table = f32(devices, 128)
    coef_ext = None

    def scratch(count):
        return [(3, count, depth, width)] * 3 + [(count, depth, width)] * 2

    for _ in range(OUTER):
        a_edge, b_edge = beside(edge, IMG, True), beside(edge, IMG, False)
        a_mid, b_mid = beside(mid, IMG, True), beside(mid, IMG, False)
        heads = [cells_[:, :HALO] for cells_ in (a_edge, edge, b_edge)]
        tails = [cells_[:, HALO:] for cells_ in (a_edge, edge, b_edge)]
        if coef_ext is None:
            coef_up = beside(coefs[own - HALO :], TILE, True)
            coef_down = beside(coefs[:HALO], TILE, False)
            heads, tails, coef_up, coef_down = lax.optimization_barrier(
                (heads, tails, coef_up, coef_down)
            )
        up = beside(jnp.concatenate(tails), TILE, True)
        down = beside(jnp.concatenate(heads), TILE, False)
        shapes = [f32(*ends)] * 7 + [f32(PRODUCTS, 8, 128)]
        if coef_ext is None:
            *far, part, coef_ext = call(
                first_ends_kernel,
                [place, edge, a_edge, b_edge, up, down, coef_up, coefs, coef_down],
                [*shapes, f32(*ext[1:])],
                scratch(2 * HALO),
            )
        else:
            *far, part = call(
                ends_kernel,
                [place, edge, a_edge, b_edge, up, down, coef_ext],
                shapes,
                scratch(2 * HALO),
            )
        *near, sums = call(
            middle_kernel,
            [place, mid, a_mid, b_mid, *far[:3], part, coef_ext],
            [f32(*middle)] * 7 + [table],
            scratch(own - 4),
        )
        phi, m, n, lm, ln, g, scal, sums = call(
            lambda *refs: second_kernel(tiles, cells, *refs),
            [place, from_everyone(sums), *far, *near, coef_ext],
            [whole] * 6 + [f32(2), table],
            [ext, *scratch(rows)],
            small_out=(6,),
        )
        phi, g, sums = call(
            lambda *refs: third_kernel(cells, *refs),
            [place, scal, from_everyone(sums), phi, m, n, lm, ln, g, coef_ext],
            [whole, f32(3, own, depth, width), table],
            [ext, ext, *scratch(rows)],
            scalars=2,
        )
        edge, mid = call(
            lambda *refs: last_kernel(cells, *refs),
            [place, from_everyone(sums), phi, g],
            [f32(3, 2 * HALO, depth, width), f32(3, own - 2 * HALO, depth, width)],
            [],
        )
    final = jnp.concatenate([edge[:, :HALO], mid, edge[:, HALO:]], axis=1)
    return jnp.swapaxes(final, 1, 2)[None]


def solution(mesh):
    split = Mesh(mesh.devices.reshape(4, 4, 4, 2), IMG_TILE)
    return jax.shard_map(
        body,
        mesh=split,
        in_specs=(P(IMG, None, None, TILE, None), P(None, TILE, None)),
        out_specs=P(IMG, None, None, TILE, None),
        check_vma=False,
    )
```

```python
import jax
import jax.numpy as jnp
from jax import lax
from jax.experimental import pallas as pl
from jax.experimental.pallas import tpu as pltpu
from jax.sharding import Mesh
from jax.sharding import PartitionSpec as P

OUTER = 2
INNER = 3
IMG = ("img_0", "img_1")
TILE = ("tile_0", "tile_1")
IMG_TILE = ("img_0", "img_1", "tile_0", "tile_1")

spring_coef = 20.0
step_scale = 0.25
epsilon = 1e-06

HALO = 2 * INNER
PRODUCTS = 11
SUBLANES = 2
LANES = 2
TILES = range(SUBLANES * LANES)
VMEM_LIMIT = 16 * 1024 * 1024


def tile_of(ref, comp, at, place):
    z, y = divmod(place, LANES)
    return ref[comp, at, z * 8 : z * 8 + 8, y * 128 : y * 128 + 128]


def put(ref, comp, at, place, cells):
    z, y = divmod(place, LANES)
    ref[comp, at, z * 8 : z * 8 + 8, y * 128 : y * 128 + 128] = cells


def flat_of(ref, at, place):
    z, y = divmod(place, LANES)
    return ref[at, z * 8 : z * 8 + 8, y * 128 : y * 128 + 128]


def put_flat(ref, at, place, cells):
    z, y = divmod(place, LANES)
    ref[at, z * 8 : z * 8 + 8, y * 128 : y * 128 + 128] = cells


def vector(ref, at, place):
    return [tile_of(ref, comp, at, place) for comp in range(3)]


def around(line, axis):
    size = line[0].shape[axis]
    where = lax.broadcasted_iota(jnp.int32, line[0].shape, axis)
    first, last = where == 0, where == size - 1
    later = [pltpu.roll(cells, 1, axis) for cells in line]
    earlier = [pltpu.roll(cells, size - 1, axis) for cells in line]
    later, earlier = [0.0, *later], [*earlier, 0.0]
    return [
        jnp.where(first, later[i], later[i + 1]) + jnp.where(last, earlier[i + 1], earlier[i])
        for i in range(len(line))
    ]


def laplace(ref, comp, at):
    cells = [tile_of(ref, comp, at, place) for place in TILES]
    total = [
        (tile_of(ref, comp, at - 1, place) + tile_of(ref, comp, at + 1, place)) - 6.0 * cells[place]
        for place in TILES
    ]
    for z in range(SUBLANES):
        picked = range(z * LANES, z * LANES + LANES)
        for place, side in zip(picked, around([cells[i] for i in picked], 1)):
            total[place] = total[place] + side
    for y in range(LANES):
        picked = range(y, SUBLANES * LANES, LANES)
        for place, side in zip(picked, around([cells[i] for i in picked], 0)):
            total[place] = total[place] + side
    return cells, total


def dot(left, right):
    return left[0] * right[0] + left[1] * right[1] + left[2] * right[2]


def stiffness(square, coefs):
    plain = 0.5 - 0.125 * square
    return [plain, plain, plain + coefs]


def loop(low, high, body, carry=0):
    return lax.fori_loop(low, high, body, carry, unroll=4)


def clear_outside(tile, last_tile, refs, own):
    rows = refs[0].shape[1]

    @pl.when(tile == 0)
    def _():
        for ref in refs:
            ref[:, 0:HALO] = jnp.zeros((3, HALO) + ref.shape[2:], jnp.float32)

    @pl.when(tile == last_tile)
    def _():
        for ref in refs:
            ref[:, HALO + own :] = jnp.zeros((3, rows - HALO - own) + ref.shape[2:], jnp.float32)


def block(phi_ref, m_ref, n_ref, lm_ref, ln_ref, q_ref, r_ref, coef_ref, offset, scratch, cuts, clear, sums):
    fa_ref, fb_ref, fs_ref, sm_ref, sn_ref = scratch
    rows = phi_ref.shape[1]

    def drive(at, carry):
        for ref, lap_ref, out, squares, before in (
            (m_ref, lm_ref, fa_ref, sm_ref, None),
            (n_ref, ln_ref, fb_ref, sn_ref, (fa_ref, fs_ref)),
        ):
            stiff = []
            for place in TILES:
                cells = vector(ref, at, place)
                square = dot(cells, cells)
                put_flat(squares, at, place, square)
                stiff.append(stiffness(square, flat_of(coef_ref, at + offset, place)))
            for comp in range(3):
                cells, bent = laplace(ref, comp, at)
                for place in TILES:
                    put(lap_ref, comp, at, place, bent[place])
                    total = bent[place] + stiff[place][comp] * cells[place]
                    put(out, comp, at, place, total)
                    if before is not None:
                        total = total + tile_of(fa_ref, comp, at, place)
                        put(fs_ref, comp, at, place, total)
        return carry

    loop(1, rows - 1, drive)
    clear((fa_ref, fb_ref, fs_ref))

    def fields(at, sums):
        adjoint = [laplace(fs_ref, comp, at)[1] for comp in range(3)]
        for place in TILES:
            phi, m, n = (vector(ref, at, place) for ref in (phi_ref, m_ref, n_ref))
            fa, fb = vector(fa_ref, at, place), vector(fb_ref, at, place)
            square_m, square_n = flat_of(sm_ref, at, place), flat_of(sn_ref, at, place)
            coefs = flat_of(coef_ref, at + offset, place)
            stiff_m, stiff_n = stiffness(square_m, coefs), stiffness(square_n, coefs)
            turn_m, turn_n = 0.25 * dot(m, fa), 0.25 * dot(n, fb)
            gap = 0.125 * (square_m - square_n)
            rise_m = 0.25 * dot(m, phi) - 0.125 * square_m
            rise_n = 0.125 * square_n - 0.25 * dot(n, phi)
            flat, bent = [], []
            for c in range(3):
                flat.append(phi[c] * gap + m[c] * rise_m + n[c] * rise_n)
                bent.append(
                    0.25
                    * (
                        adjoint[c][place]
                        + (stiff_m[c] * fa[c] + stiff_n[c] * fb[c])
                        - (m[c] * turn_m + n[c] * turn_n)
                    )
                )
                put(q_ref, c, at, place, flat[c])
                put(r_ref, c, at, place, bent[c])
            if sums:
                behind = [2.0 * one - other for one, other in zip(phi, m)]
                ahead = [other - 2.0 * one for one, other in zip(phi, n)]
                pairs = (
                    (behind, behind), (behind, ahead), (ahead, ahead),
                    (flat, behind), (flat, ahead), (bent, behind), (bent, ahead),
                    (flat, flat), (flat, bent), (bent, bent), (fb, fb),
                )
                sums = [total + dot(left, right) for total, (left, right) in zip(sums, pairs)]
        return sums

    def rim(at, carry):
        fields(at, None)
        return carry

    loop(2, cuts[0], rim)
    sums = loop(cuts[0], cuts[1], fields, sums)
    loop(cuts[1], rows - 2, rim)
    clear((q_ref, r_ref))
    return sums


def join(pieces, outs, low, high, shift):
    own_ref, a_ref, b_ref = pieces
    phi_ref, m_ref, n_ref = outs

    def one(at, carry):
        for comp in range(3):
            for place in TILES:
                phi = tile_of(own_ref, comp, at, place)
                put(phi_ref, comp, at + shift, place, phi)
                put(m_ref, comp, at + shift, place, phi + tile_of(a_ref, comp, at, place))
                put(n_ref, comp, at + shift, place, phi + tile_of(b_ref, comp, at, place))
        return carry

    loop(low, high, one)


def first_ends_kernel(
    place_ref, own_edge, a_edge, b_edge, up_ref, down_ref, coef_up, coef_ref, coef_down, *refs
):
    own = coef_ref.shape[0]
    coef_out, refs = refs[8], refs[:8] + refs[9:]
    coef_out[0:HALO] = coef_up[...]
    coef_out[HALO : HALO + own] = coef_ref[...]
    coef_out[HALO + own :] = coef_down[...]
    ends_kernel(place_ref, own_edge, a_edge, b_edge, up_ref, down_ref, coef_out, *refs)


def ends_kernel(
    place_ref, own_edge, a_edge, b_edge, up_ref, down_ref, coef_ref,
    phi_ref, m_ref, n_ref, lm_ref, ln_ref, q_ref, r_ref, sums_ref,
    fa_ref, fb_ref, fs_ref, sm_ref, sn_ref
):
    tile, last_tile = place_ref[1], place_ref[2] - 1
    span = 2 * HALO
    fields = (phi_ref, m_ref, n_ref, lm_ref, ln_ref, q_ref, r_ref)
    scratch = (fa_ref, fb_ref, fs_ref, sm_ref, sn_ref)
    halos = [[ref.at[3 * which : 3 * which + 3] for which in (1, 0, 2)] for ref in (up_ref, down_ref)]
    edges = (own_edge, a_edge, b_edge)
    sums = [jnp.zeros((8, 128), jnp.float32)] * PRODUCTS
    for top in (True, False):
        first = 0 if top else span
        here = [ref.at[:, first : first + span] for ref in fields]
        join(halos[0 if top else 1], here[:3], 0, HALO, 0 if top else HALO)
        if top:
            join(edges, here[:3], 0, HALO, HALO)
        else:
            join(edges, here[:3], HALO, span, -HALO)

        def clear(refs, top=top):
            outside = slice(0, HALO) if top else slice(HALO, span)

            @pl.when(tile == (0 if top else last_tile))
            def _():
                for ref in refs:
                    ref[:, outside] = jnp.zeros((3, HALO) + ref.shape[2:], jnp.float32)

        cuts = (HALO, span - 2) if top else (2, HALO)
        offset = 0 if top else coef_ref.shape[0] - span
        sums = block(*here, coef_ref, offset, scratch, cuts, clear, sums)
    for which in range(PRODUCTS):
        sums_ref[which] = sums[which]


def middle_kernel(
    place_ref, own_mid, a_mid, b_mid, phi_end, m_end, n_end, part_ref, coef_ref,
    phi_ref, m_ref, n_ref, lm_ref, ln_ref, q_ref, r_ref, sums_ref,
    fa_ref, fb_ref, fs_ref, sm_ref, sn_ref
):
    span = 2 * HALO
    rows = phi_ref.shape[1]
    outs = (phi_ref, m_ref, n_ref)
    for end, ref in zip((phi_end, m_end, n_end), outs):
        ref[:, 0:4] = end[:, span - 4 : span]
        ref[:, rows - 4 :] = end[:, span : span + 4]
    join((own_mid, a_mid, b_mid), outs, 0, rows - 8, 4)
    sums = block(
        *outs, lm_ref, ln_ref, q_ref, r_ref, coef_ref, span - 4,
        (fa_ref, fb_ref, fs_ref, sm_ref, sn_ref), (2, rows - 2), lambda refs: None,
        [part_ref[which] for which in range(PRODUCTS)],
    )
    lane = lax.broadcasted_iota(jnp.int32, (1, 128), 1)
    result = jnp.zeros((1, 128), jnp.float32)
    for which in range(PRODUCTS):
        result = jnp.where(lane == which, jnp.sum(sums[which]), result)
    sums_ref[...] = jnp.broadcast_to(result, sums_ref.shape)


def path_scalars(place_ref, all_ref, tiles, cells):
    devices = all_ref.shape[0]
    images = devices // tiles
    table = jnp.sum(all_ref[...].reshape(images, tiles, 128), axis=1)
    lane = lax.broadcasted_iota(jnp.int32, (images, 128), 1)
    image = lax.broadcasted_iota(jnp.int32, (images, 128), 0)
    one = image[:, :1]

    def column(which):
        return jnp.sum(jnp.where(lane == which, table, 0.0), axis=1, keepdims=True)

    live = one < images - 1
    seg = jnp.where(live, jnp.sqrt(column(2) + epsilon), 0.0)
    drv = jnp.where(live, jnp.sqrt(0.25 * column(10) + epsilon), 0.0)
    path_len = jnp.sum(seg, axis=0, keepdims=True)
    tau = path_len / jnp.sum(drv, axis=0, keepdims=True)
    before = jnp.sum(jnp.where(image < lane, seg, 0.0), axis=0, keepdims=True)
    before = jnp.sum(jnp.where(image == lane, before, 0.0), axis=1, keepdims=True)
    target = one.astype(jnp.float32) / (images - 1)
    pull = spring_coef * (before / path_len - target) * (images - 1) / (2.0 * path_len)
    inv = 1.0 / tau
    near, far = inv + pull, pull - inv
    norm = near * near * column(0) + far * far * column(2) + 2.0 * near * far * column(1)
    norm += 2.0 * (near * column(3) + far * column(4))
    norm += 2.0 * tau * (near * column(5) + far * column(6))
    norm += column(7) + tau * (2.0 * column(8) + tau * column(9))
    inner = (one > 0) & (one < images - 1)
    total = jnp.sum(jnp.where(inner, norm, 0.0), axis=0, keepdims=True)
    step = step_scale / jnp.sqrt(total / cells + epsilon)
    mine = jnp.sum(jnp.where(one == place_ref[0], pull, 0.0), axis=0, keepdims=True)
    return tau[0, 0], mine[0, 0], step[0, 0]


def gradients(
    phi_ref, m_ref, n_ref, coef_ref, fa_ref, fb_ref, fs_ref, sm_ref, sn_ref, g_ref, tau, pull, out
):
    inv = 1.0 / tau
    turned = 0.25 * tau

    def grad(at, total):
        adjoint = [laplace(fs_ref, comp, at)[1] for comp in range(3)]
        for place in TILES:
            phi, m, n = (vector(ref, at, place) for ref in (phi_ref, m_ref, n_ref))
            fa, fb = vector(fa_ref, at, place), vector(fb_ref, at, place)
            square_m, square_n = flat_of(sm_ref, at, place), flat_of(sn_ref, at, place)
            coefs = flat_of(coef_ref, at, place)
            stiff_m, stiff_n = stiffness(square_m, coefs), stiffness(square_n, coefs)
            gap = 0.125 * (square_m - square_n) + 4.0 * inv
            lean_m = (
                0.25 * (dot(m, phi) - turned * dot(m, fa)) - 0.125 * square_m - (pull + inv)
            )
            lean_n = (
                0.125 * square_n - 0.25 * (dot(n, phi) + turned * dot(n, fb)) + (pull - inv)
            )
            cells = [
                phi[c] * gap
                + (m[c] * lean_m + n[c] * lean_n)
                + turned * (adjoint[c][place] + (stiff_m[c] * fa[c] + stiff_n[c] * fb[c]))
                for c in range(3)
            ]
            for c in range(3):
                put(g_ref, c, at - out, place, cells[c])
            total = total + dot(cells, cells)
        return total

    def rim(at, carry):
        grad(at, 0.0)
        return carry

    return rim, grad


def interior(place_ref):
    return jnp.where((place_ref[0] > 0) & (place_ref[0] < place_ref[3] - 1), 1.0, 0.0)


def advance(
    step_ref, scale, old, old_shift, new, coef_ref, scratch, low, high, keep
):
    p_ref, m0_ref, n0_ref, lm0_ref, ln0_ref = old
    phi_ref, m_ref, n_ref, lm_ref, ln_ref = new
    fa_ref, fb_ref, fs_ref, sm_ref, sn_ref = scratch

    def body(at, carry):
        was = at + old_shift
        moves, bends = [], []
        for comp in range(3):
            cells, bent = laplace(step_ref, comp, at)
            if scale is not None:
                cells, bent = [scale * cell for cell in cells], [scale * cell for cell in bent]
            moves.append(cells)
            bends.append(bent)
            for place in TILES:
                put(phi_ref, comp, at, place, tile_of(p_ref, comp, was, place) + cells[place])
        for ref, lap_old, out, lap_new, drive_ref, squares, last in (
            (m0_ref, lm0_ref, m_ref, lm_ref, fa_ref, sm_ref, False),
            (n0_ref, ln0_ref, n_ref, ln_ref, fb_ref, sn_ref, True),
        ):
            for place in TILES:
                cells = [tile_of(ref, comp, was, place) + moves[comp][place] for comp in range(3)]
                square = dot(cells, cells)
                put_flat(squares, at, place, square)
                stiff = stiffness(square, flat_of(coef_ref, at, place))
                for comp in range(3):
                    put(out, comp, at, place, cells[comp])
                    bent = tile_of(lap_old, comp, was, place) + bends[comp][place]
                    if keep:
                        put(lap_new, comp, at, place, bent)
                    total = bent + stiff[comp] * cells[comp]
                    put(drive_ref, comp, at, place, total)
                    if last:
                        total = total + tile_of(fa_ref, comp, at, place)
                        put(fs_ref, comp, at, place, total)
        return carry

    loop(low, high, body)


def second_kernel(tiles, cells, place_ref, all_ref, *refs):
    ends, mids, refs = refs[:7], refs[7:14], refs[14:]
    coef_ref, phi_ref, m_ref, n_ref, lm_ref, ln_ref, g_ref, scal_ref, sums_ref, d_ref = refs[:10]
    scratch = refs[10:]
    rows = phi_ref.shape[1]
    own = rows - 2 * HALO
    span = 2 * HALO
    tile, last_tile = place_ref[1], place_ref[2] - 1
    tau, pull, step = path_scalars(place_ref, all_ref, tiles, cells)
    live = interior(place_ref)
    step = step * live
    inv = 1.0 / tau
    scal_ref[0] = tau
    scal_ref[1] = pull
    from_p, from_m, from_n = -4.0 * step * inv, step * (inv + pull), step * (inv - pull)
    bend = step * tau
    regions = (
        (ends, 2, span - 2, 0),
        (mids, span - 2, rows - span + 2, 4 - span),
        (ends, rows - span + 2, rows - 2, 2 * span - rows),
    )
    for here, low, high, shift in regions:

        def direction(at, carry, here=here, shift=shift):
            was = at + shift
            for comp in range(3):
                for place in TILES:
                    p, m, n, q, r = (
                        tile_of(here[i], comp, was, place) for i in (0, 1, 2, 5, 6)
                    )
                    move = (from_p * p + from_m * m) + (from_n * n - step * q) - bend * r
                    put(d_ref, comp, at, place, move)
            return carry

        loop(low, high, direction)
    new = (phi_ref, m_ref, n_ref, lm_ref, ln_ref)
    for here, low, high, shift in regions:
        low, high = max(low, 3), min(high, rows - 3)
        advance(d_ref, None, here[:5], shift, new, coef_ref, scratch, low, high, True)
    fa_ref, fb_ref, fs_ref, sm_ref, sn_ref = scratch
    clear_outside(tile, last_tile, (fa_ref, fb_ref, fs_ref), own)
    rim, inside = gradients(
        phi_ref, m_ref, n_ref, coef_ref, fa_ref, fb_ref, fs_ref, sm_ref, sn_ref, g_ref, tau, pull, 0
    )
    loop(4, HALO, rim)
    total = loop(HALO, HALO + own, inside, jnp.zeros((8, 128), jnp.float32))
    loop(HALO + own, rows - 4, rim)
    clear_outside(tile, last_tile, (g_ref,), own)
    sums = jnp.sum(total, axis=0, keepdims=True) * live
    sums_ref[...] = jnp.broadcast_to(sums, sums_ref.shape)


def step_of(all_ref, cells):
    return step_scale / jnp.sqrt(jnp.sum(all_ref[...]) / cells + epsilon)


def third_kernel(
    cells, place_ref, scal_ref, all_ref, p_ref, m0_ref, n0_ref, lm0_ref, ln0_ref, h_ref, coef_ref,
    phi_ref, g_ref, sums_ref, m_ref, n_ref, fa_ref, fb_ref, fs_ref, sm_ref, sn_ref
):
    rows = p_ref.shape[1]
    own = rows - 2 * HALO
    tile, last_tile = place_ref[1], place_ref[2] - 1
    live = interior(place_ref)
    tau, pull = scal_ref[0], scal_ref[1]
    step = step_of(all_ref, cells) * live
    advance(
        h_ref, -step, (p_ref, m0_ref, n0_ref, lm0_ref, ln0_ref), 0,
        (phi_ref, m_ref, n_ref, None, None), coef_ref,
        (fa_ref, fb_ref, fs_ref, sm_ref, sn_ref), HALO - 1, HALO + own + 1, False,
    )
    clear_outside(tile, last_tile, (fa_ref, fb_ref, fs_ref), own)
    _, inside = gradients(
        phi_ref, m_ref, n_ref, coef_ref, fa_ref, fb_ref, fs_ref, sm_ref, sn_ref, g_ref, tau, pull,
        HALO,
    )
    total = loop(HALO, HALO + own, inside, jnp.zeros((8, 128), jnp.float32))
    sums = jnp.sum(total, axis=0, keepdims=True) * live
    sums_ref[...] = jnp.broadcast_to(sums, sums_ref.shape)


def last_kernel(cells, place_ref, all_ref, p_ref, g_ref, edge_ref, mid_ref):
    own = g_ref.shape[1]
    step = step_of(all_ref, cells) * interior(place_ref)
    for ref, low, high, shift in (
        (edge_ref, 0, HALO, 0),
        (mid_ref, HALO, own - HALO, HALO),
        (edge_ref, own - HALO, own, own - 2 * HALO),
    ):

        def move(at, carry, ref=ref, shift=shift):
            for comp in range(3):
                for place in TILES:
                    old = tile_of(p_ref, comp, at + HALO, place)
                    put(ref, comp, at - shift, place, old - step * tile_of(g_ref, comp, at, place))
            return carry

        loop(low, high, move)


def f32(*shape):
    return jax.ShapeDtypeStruct(shape, jnp.float32)


def call(kernel, operands, outs, scratch, scalars=1, small_out=()):
    smem = pl.BlockSpec(memory_space=pltpu.SMEM)
    vmem = pl.BlockSpec(memory_space=pltpu.VMEM)
    return pl.pallas_call(
        kernel,
        out_shape=outs,
        in_specs=[smem if i < scalars else vmem for i in range(len(operands))],
        out_specs=[smem if i in small_out else vmem for i in range(len(outs))],
        scratch_shapes=[pltpu.VMEM(shape, jnp.float32) for shape in scratch],
        compiler_params=pltpu.CompilerParams(vmem_limit_bytes=VMEM_LIMIT),
    )(*operands)


def beside(cells, axis, forward):
    count = lax.axis_size(axis)
    pairs = [(i, i + 1) if forward else (i + 1, i) for i in range(count - 1)]
    return lax.ppermute(cells, axis, pairs)


def from_everyone(rows):
    return lax.all_to_all(rows, IMG_TILE, 0, 0, tiled=True)


def body(spins, aniso):
    _, comps, depth, own, width = spins.shape
    images, tiles = lax.axis_size(IMG), lax.axis_size(TILE)
    devices = images * tiles
    cells = float(images * comps * depth * own * tiles * width)
    rows = own + 2 * HALO
    place = jnp.stack(
        [lax.axis_index(IMG), lax.axis_index(TILE), jnp.int32(tiles), jnp.int32(images)]
    ).astype(jnp.int32)
    start = jnp.swapaxes(spins[0], 1, 2)
    coefs = jnp.swapaxes(aniso, 0, 1)
    edge = jnp.concatenate([start[:, :HALO], start[:, own - HALO :]], axis=1)
    mid = start[:, HALO : own - HALO]
    coef_up = beside(coefs[own - HALO :], TILE, True)
    coef_down = beside(coefs[:HALO], TILE, False)
    edge, mid, coef_up, coef_down = lax.optimization_barrier((edge, mid, coef_up, coef_down))
    ext = (3, rows, depth, width)
    ends, middle = (3, 4 * HALO, depth, width), (3, own - 4, depth, width)
    whole = f32(*ext)
    table = f32(devices, 128)
    coef_ext = None

    def scratch(count):
        return [(3, count, depth, width)] * 3 + [(count, depth, width)] * 2

    for _ in range(OUTER):
        a_edge, b_edge = beside(edge, IMG, True), beside(edge, IMG, False)
        a_mid, b_mid = beside(mid, IMG, True), beside(mid, IMG, False)
        heads = [cells_[:, :HALO] for cells_ in (a_edge, edge, b_edge)]
        tails = [cells_[:, HALO:] for cells_ in (a_edge, edge, b_edge)]
        up = beside(jnp.concatenate(tails), TILE, True)
        down = beside(jnp.concatenate(heads), TILE, False)
        shapes = [f32(*ends)] * 7 + [f32(PRODUCTS, 8, 128)]
        if coef_ext is None:
            *far, part, coef_ext = call(
                first_ends_kernel,
                [place, edge, a_edge, b_edge, up, down, coef_up, coefs, coef_down],
                [*shapes, f32(*ext[1:])],
                scratch(2 * HALO),
            )
        else:
            *far, part = call(
                ends_kernel,
                [place, edge, a_edge, b_edge, up, down, coef_ext],
                shapes,
                scratch(2 * HALO),
            )
        *near, sums = call(
            middle_kernel,
            [place, mid, a_mid, b_mid, *far[:3], part, coef_ext],
            [f32(*middle)] * 7 + [table],
            scratch(own - 4),
        )
        phi, m, n, lm, ln, g, scal, sums = call(
            lambda *refs: second_kernel(tiles, cells, *refs),
            [place, from_everyone(sums), *far, *near, coef_ext],
            [whole] * 6 + [f32(2), table],
            [ext, *scratch(rows)],
            small_out=(6,),
        )
        phi, g, sums = call(
            lambda *refs: third_kernel(cells, *refs),
            [place, scal, from_everyone(sums), phi, m, n, lm, ln, g, coef_ext],
            [whole, f32(3, own, depth, width), table],
            [ext, ext, *scratch(rows)],
            scalars=2,
        )
        edge, mid = call(
            lambda *refs: last_kernel(cells, *refs),
            [place, from_everyone(sums), phi, g],
            [f32(3, 2 * HALO, depth, width), f32(3, own - 2 * HALO, depth, width)],
            [],
        )
    final = jnp.concatenate([edge[:, :HALO], mid, edge[:, HALO:]], axis=1)
    return jnp.swapaxes(final, 1, 2)[None]


def solution(mesh):
    split = Mesh(mesh.devices.reshape(4, 4, 4, 2), IMG_TILE)
    return jax.shard_map(
        body,
        mesh=split,
        in_specs=(P(IMG, None, None, TILE, None), P(None, TILE, None)),
        out_specs=P(IMG, None, None, TILE, None),
        check_vma=False,
    )
```

```python
import jax
import jax.numpy as jnp
from jax import lax
from jax.experimental import pallas as pl
from jax.experimental.pallas import tpu as pltpu
from jax.sharding import Mesh
from jax.sharding import PartitionSpec as P

OUTER = 2
INNER = 3
IMG = ("img_0", "img_1")
TILE = ("tile_0", "tile_1")
IMG_TILE = ("img_0", "img_1", "tile_0", "tile_1")

spring_coef = 20.0
step_scale = 0.25
epsilon = 1e-06

HALO = 2 * INNER
PRODUCTS = 11
SUBLANES = 2
LANES = 2
TILES = range(SUBLANES * LANES)
VMEM_LIMIT = 16 * 1024 * 1024


def tile_of(ref, comp, at, place):
    z, y = divmod(place, LANES)
    return ref[comp, at, z * 8 : z * 8 + 8, y * 128 : y * 128 + 128]


def put(ref, comp, at, place, cells):
    z, y = divmod(place, LANES)
    ref[comp, at, z * 8 : z * 8 + 8, y * 128 : y * 128 + 128] = cells


def flat_of(ref, at, place):
    z, y = divmod(place, LANES)
    return ref[at, z * 8 : z * 8 + 8, y * 128 : y * 128 + 128]


def put_flat(ref, at, place, cells):
    z, y = divmod(place, LANES)
    ref[at, z * 8 : z * 8 + 8, y * 128 : y * 128 + 128] = cells


def vector(ref, at, place):
    return [tile_of(ref, comp, at, place) for comp in range(3)]


def around(line, axis):
    size = line[0].shape[axis]
    where = lax.broadcasted_iota(jnp.int32, line[0].shape, axis)
    first, last = where == 0, where == size - 1
    later = [pltpu.roll(cells, 1, axis) for cells in line]
    earlier = [pltpu.roll(cells, size - 1, axis) for cells in line]
    later, earlier = [0.0, *later], [*earlier, 0.0]
    return [
        jnp.where(first, later[i], later[i + 1]) + jnp.where(last, earlier[i + 1], earlier[i])
        for i in range(len(line))
    ]


def laplace(ref, comp, at):
    cells = [tile_of(ref, comp, at, place) for place in TILES]
    total = [
        (tile_of(ref, comp, at - 1, place) + tile_of(ref, comp, at + 1, place)) - 6.0 * cells[place]
        for place in TILES
    ]
    for z in range(SUBLANES):
        picked = range(z * LANES, z * LANES + LANES)
        for place, side in zip(picked, around([cells[i] for i in picked], 1)):
            total[place] = total[place] + side
    for y in range(LANES):
        picked = range(y, SUBLANES * LANES, LANES)
        for place, side in zip(picked, around([cells[i] for i in picked], 0)):
            total[place] = total[place] + side
    return cells, total


def dot(left, right):
    return left[0] * right[0] + left[1] * right[1] + left[2] * right[2]


def stiffness(square, coefs):
    plain = 0.5 - 0.125 * square
    return [plain, plain, plain + coefs]


def loop(low, high, body, carry=0):
    return lax.fori_loop(low, high, body, carry, unroll=4)


def clear_outside(tile, last_tile, refs, own):
    rows = refs[0].shape[1]

    @pl.when(tile == 0)
    def _():
        for ref in refs:
            ref[:, 0:HALO] = jnp.zeros((3, HALO) + ref.shape[2:], jnp.float32)

    @pl.when(tile == last_tile)
    def _():
        for ref in refs:
            ref[:, HALO + own :] = jnp.zeros((3, rows - HALO - own) + ref.shape[2:], jnp.float32)


def block(phi_ref, m_ref, n_ref, lm_ref, ln_ref, q_ref, r_ref, coef_ref, offset, scratch, cuts, clear, sums):
    fa_ref, fb_ref, fs_ref, sm_ref, sn_ref = scratch
    rows = phi_ref.shape[1]

    def drive(at, carry):
        for ref, lap_ref, out, squares, before in (
            (m_ref, lm_ref, fa_ref, sm_ref, None),
            (n_ref, ln_ref, fb_ref, sn_ref, (fa_ref, fs_ref)),
        ):
            stiff = []
            for place in TILES:
                cells = vector(ref, at, place)
                square = dot(cells, cells)
                put_flat(squares, at, place, square)
                stiff.append(stiffness(square, flat_of(coef_ref, at + offset, place)))
            for comp in range(3):
                cells, bent = laplace(ref, comp, at)
                for place in TILES:
                    put(lap_ref, comp, at, place, bent[place])
                    total = bent[place] + stiff[place][comp] * cells[place]
                    put(out, comp, at, place, total)
                    if before is not None:
                        total = total + tile_of(fa_ref, comp, at, place)
                        put(fs_ref, comp, at, place, total)
        return carry

    loop(1, rows - 1, drive)
    clear((fa_ref, fb_ref, fs_ref))

    def fields(at, sums):
        adjoint = [laplace(fs_ref, comp, at)[1] for comp in range(3)]
        for place in TILES:
            phi, m, n = (vector(ref, at, place) for ref in (phi_ref, m_ref, n_ref))
            fa, fb = vector(fa_ref, at, place), vector(fb_ref, at, place)
            square_m, square_n = flat_of(sm_ref, at, place), flat_of(sn_ref, at, place)
            coefs = flat_of(coef_ref, at + offset, place)
            stiff_m, stiff_n = stiffness(square_m, coefs), stiffness(square_n, coefs)
            turn_m, turn_n = 0.25 * dot(m, fa), 0.25 * dot(n, fb)
            gap = 0.125 * (square_m - square_n)
            rise_m = 0.25 * dot(m, phi) - 0.125 * square_m
            rise_n = 0.125 * square_n - 0.25 * dot(n, phi)
            flat, bent = [], []
            for c in range(3):
                flat.append(phi[c] * gap + m[c] * rise_m + n[c] * rise_n)
                bent.append(
                    0.25
                    * (
                        adjoint[c][place]
                        + (stiff_m[c] * fa[c] + stiff_n[c] * fb[c])
                        - (m[c] * turn_m + n[c] * turn_n)
                    )
                )
                put(q_ref, c, at, place, flat[c])
                put(r_ref, c, at, place, bent[c])
            if sums:
                behind = [2.0 * one - other for one, other in zip(phi, m)]
                ahead = [other - 2.0 * one for one, other in zip(phi, n)]
                pairs = (
                    (behind, behind), (behind, ahead), (ahead, ahead),
                    (flat, behind), (flat, ahead), (bent, behind), (bent, ahead),
                    (flat, flat), (flat, bent), (bent, bent), (fb, fb),
                )
                sums = [total + dot(left, right) for total, (left, right) in zip(sums, pairs)]
        return sums

    def rim(at, carry):
        fields(at, None)
        return carry

    loop(2, cuts[0], rim)
    sums = loop(cuts[0], cuts[1], fields, sums)
    loop(cuts[1], rows - 2, rim)
    clear((q_ref, r_ref))
    return sums


def join(pieces, outs, low, high, shift):
    own_ref, a_ref, b_ref = pieces
    phi_ref, m_ref, n_ref = outs

    def one(at, carry):
        for comp in range(3):
            for place in TILES:
                phi = tile_of(own_ref, comp, at, place)
                put(phi_ref, comp, at + shift, place, phi)
                put(m_ref, comp, at + shift, place, phi + tile_of(a_ref, comp, at, place))
                put(n_ref, comp, at + shift, place, phi + tile_of(b_ref, comp, at, place))
        return carry

    loop(low, high, one)


def first_ends_kernel(
    place_ref, own_edge, a_edge, b_edge, up_own, down_own, up_ref, down_ref, coef_ref, *refs
):
    own = coef_ref.shape[0]
    coef_out, refs = refs[8], refs[:8] + refs[9:]
    coef_out[0:HALO] = up_own[3]
    coef_out[HALO : HALO + own] = coef_ref[...]
    coef_out[HALO + own :] = down_own[3]
    ends_kernel(
        place_ref, own_edge, a_edge, b_edge, up_own, down_own, up_ref, down_ref, coef_out, *refs
    )


def ends_kernel(
    place_ref, own_edge, a_edge, b_edge, up_own, down_own, up_ref, down_ref, coef_ref,
    phi_ref, m_ref, n_ref, lm_ref, ln_ref, q_ref, r_ref, sums_ref,
    fa_ref, fb_ref, fs_ref, sm_ref, sn_ref
):
    tile, last_tile = place_ref[1], place_ref[2] - 1
    span = 2 * HALO
    fields = (phi_ref, m_ref, n_ref, lm_ref, ln_ref, q_ref, r_ref)
    scratch = (fa_ref, fb_ref, fs_ref, sm_ref, sn_ref)
    halos = [
        (first, ref.at[0:3], ref.at[3:6])
        for first, ref in ((up_own, up_ref), (down_own, down_ref))
    ]
    edges = (own_edge, a_edge, b_edge)
    sums = [jnp.zeros((8, 128), jnp.float32)] * PRODUCTS
    for top in (True, False):
        first = 0 if top else span
        here = [ref.at[:, first : first + span] for ref in fields]
        join(halos[0 if top else 1], here[:3], 0, HALO, 0 if top else HALO)
        if top:
            join(edges, here[:3], 0, HALO, HALO)
        else:
            join(edges, here[:3], HALO, span, -HALO)

        def clear(refs, top=top):
            outside = slice(0, HALO) if top else slice(HALO, span)

            @pl.when(tile == (0 if top else last_tile))
            def _():
                for ref in refs:
                    ref[:, outside] = jnp.zeros((3, HALO) + ref.shape[2:], jnp.float32)

        cuts = (HALO, span - 2) if top else (2, HALO)
        offset = 0 if top else coef_ref.shape[0] - span
        sums = block(*here, coef_ref, offset, scratch, cuts, clear, sums)
    for which in range(PRODUCTS):
        sums_ref[which] = sums[which]


def middle_kernel(
    place_ref, own_mid, a_mid, b_mid, phi_end, m_end, n_end, part_ref, coef_ref,
    phi_ref, m_ref, n_ref, lm_ref, ln_ref, q_ref, r_ref, sums_ref,
    fa_ref, fb_ref, fs_ref, sm_ref, sn_ref
):
    span = 2 * HALO
    rows = phi_ref.shape[1]
    outs = (phi_ref, m_ref, n_ref)
    for end, ref in zip((phi_end, m_end, n_end), outs):
        ref[:, 0:4] = end[:, span - 4 : span]
        ref[:, rows - 4 :] = end[:, span : span + 4]
    join((own_mid, a_mid, b_mid), outs, 0, rows - 8, 4)
    sums = block(
        *outs, lm_ref, ln_ref, q_ref, r_ref, coef_ref, span - 4,
        (fa_ref, fb_ref, fs_ref, sm_ref, sn_ref), (2, rows - 2), lambda refs: None,
        [part_ref[which] for which in range(PRODUCTS)],
    )
    lane = lax.broadcasted_iota(jnp.int32, (1, 128), 1)
    result = jnp.zeros((1, 128), jnp.float32)
    for which in range(PRODUCTS):
        result = jnp.where(lane == which, jnp.sum(sums[which]), result)
    sums_ref[...] = jnp.broadcast_to(result, sums_ref.shape)


def path_scalars(place_ref, all_ref, tiles, cells):
    devices = all_ref.shape[0]
    images = devices // tiles
    table = jnp.sum(all_ref[...].reshape(images, tiles, 128), axis=1)
    lane = lax.broadcasted_iota(jnp.int32, (images, 128), 1)
    image = lax.broadcasted_iota(jnp.int32, (images, 128), 0)
    one = image[:, :1]

    def column(which):
        return jnp.sum(jnp.where(lane == which, table, 0.0), axis=1, keepdims=True)

    live = one < images - 1
    seg = jnp.where(live, jnp.sqrt(column(2) + epsilon), 0.0)
    drv = jnp.where(live, jnp.sqrt(0.25 * column(10) + epsilon), 0.0)
    path_len = jnp.sum(seg, axis=0, keepdims=True)
    tau = path_len / jnp.sum(drv, axis=0, keepdims=True)
    before = jnp.sum(jnp.where(image < lane, seg, 0.0), axis=0, keepdims=True)
    before = jnp.sum(jnp.where(image == lane, before, 0.0), axis=1, keepdims=True)
    target = one.astype(jnp.float32) / (images - 1)
    pull = spring_coef * (before / path_len - target) * (images - 1) / (2.0 * path_len)
    inv = 1.0 / tau
    near, far = inv + pull, pull - inv
    norm = near * near * column(0) + far * far * column(2) + 2.0 * near * far * column(1)
    norm += 2.0 * (near * column(3) + far * column(4))
    norm += 2.0 * tau * (near * column(5) + far * column(6))
    norm += column(7) + tau * (2.0 * column(8) + tau * column(9))
    inner = (one > 0) & (one < images - 1)
    total = jnp.sum(jnp.where(inner, norm, 0.0), axis=0, keepdims=True)
    step = step_scale / jnp.sqrt(total / cells + epsilon)
    mine = jnp.sum(jnp.where(one == place_ref[0], pull, 0.0), axis=0, keepdims=True)
    return tau[0, 0], mine[0, 0], step[0, 0]


def gradients(
    phi_ref, m_ref, n_ref, coef_ref, fa_ref, fb_ref, fs_ref, sm_ref, sn_ref, g_ref, tau, pull, out
):
    inv = 1.0 / tau
    turned = 0.25 * tau

    def grad(at, total):
        adjoint = [laplace(fs_ref, comp, at)[1] for comp in range(3)]
        for place in TILES:
            phi, m, n = (vector(ref, at, place) for ref in (phi_ref, m_ref, n_ref))
            fa, fb = vector(fa_ref, at, place), vector(fb_ref, at, place)
            square_m, square_n = flat_of(sm_ref, at, place), flat_of(sn_ref, at, place)
            coefs = flat_of(coef_ref, at, place)
            stiff_m, stiff_n = stiffness(square_m, coefs), stiffness(square_n, coefs)
            gap = 0.125 * (square_m - square_n) + 4.0 * inv
            lean_m = (
                0.25 * (dot(m, phi) - turned * dot(m, fa)) - 0.125 * square_m - (pull + inv)
            )
            lean_n = (
                0.125 * square_n - 0.25 * (dot(n, phi) + turned * dot(n, fb)) + (pull - inv)
            )
            cells = [
                phi[c] * gap
                + (m[c] * lean_m + n[c] * lean_n)
                + turned * (adjoint[c][place] + (stiff_m[c] * fa[c] + stiff_n[c] * fb[c]))
                for c in range(3)
            ]
            for c in range(3):
                put(g_ref, c, at - out, place, cells[c])
            total = total + dot(cells, cells)
        return total

    def rim(at, carry):
        grad(at, 0.0)
        return carry

    return rim, grad


def interior(place_ref):
    return jnp.where((place_ref[0] > 0) & (place_ref[0] < place_ref[3] - 1), 1.0, 0.0)


def advance(
    step_ref, scale, old, old_shift, new, coef_ref, scratch, low, high, keep
):
    p_ref, m0_ref, n0_ref, lm0_ref, ln0_ref = old
    phi_ref, m_ref, n_ref, lm_ref, ln_ref = new
    fa_ref, fb_ref, fs_ref, sm_ref, sn_ref = scratch

    def body(at, carry):
        was = at + old_shift
        moves, bends = [], []
        for comp in range(3):
            cells, bent = laplace(step_ref, comp, at)
            if scale is not None:
                cells, bent = [scale * cell for cell in cells], [scale * cell for cell in bent]
            moves.append(cells)
            bends.append(bent)
            for place in TILES:
                put(phi_ref, comp, at, place, tile_of(p_ref, comp, was, place) + cells[place])
        for ref, lap_old, out, lap_new, drive_ref, squares, last in (
            (m0_ref, lm0_ref, m_ref, lm_ref, fa_ref, sm_ref, False),
            (n0_ref, ln0_ref, n_ref, ln_ref, fb_ref, sn_ref, True),
        ):
            for place in TILES:
                cells = [tile_of(ref, comp, was, place) + moves[comp][place] for comp in range(3)]
                square = dot(cells, cells)
                put_flat(squares, at, place, square)
                stiff = stiffness(square, flat_of(coef_ref, at, place))
                for comp in range(3):
                    put(out, comp, at, place, cells[comp])
                    bent = tile_of(lap_old, comp, was, place) + bends[comp][place]
                    if keep:
                        put(lap_new, comp, at, place, bent)
                    total = bent + stiff[comp] * cells[comp]
                    put(drive_ref, comp, at, place, total)
                    if last:
                        total = total + tile_of(fa_ref, comp, at, place)
                        put(fs_ref, comp, at, place, total)
        return carry

    loop(low, high, body)


def second_kernel(tiles, cells, place_ref, all_ref, *refs):
    ends, mids, refs = refs[:7], refs[7:14], refs[14:]
    coef_ref, phi_ref, m_ref, n_ref, lm_ref, ln_ref, g_ref, scal_ref, sums_ref, d_ref = refs[:10]
    scratch = refs[10:]
    rows = phi_ref.shape[1]
    own = rows - 2 * HALO
    span = 2 * HALO
    tile, last_tile = place_ref[1], place_ref[2] - 1
    tau, pull, step = path_scalars(place_ref, all_ref, tiles, cells)
    live = interior(place_ref)
    step = step * live
    inv = 1.0 / tau
    scal_ref[0] = tau
    scal_ref[1] = pull
    from_p, from_m, from_n = -4.0 * step * inv, step * (inv + pull), step * (inv - pull)
    bend = step * tau
    regions = (
        (ends, 2, span - 2, 0),
        (mids, span - 2, rows - span + 2, 4 - span),
        (ends, rows - span + 2, rows - 2, 2 * span - rows),
    )
    for here, low, high, shift in regions:

        def direction(at, carry, here=here, shift=shift):
            was = at + shift
            for comp in range(3):
                for place in TILES:
                    p, m, n, q, r = (
                        tile_of(here[i], comp, was, place) for i in (0, 1, 2, 5, 6)
                    )
                    move = (from_p * p + from_m * m) + (from_n * n - step * q) - bend * r
                    put(d_ref, comp, at, place, move)
            return carry

        loop(low, high, direction)
    new = (phi_ref, m_ref, n_ref, lm_ref, ln_ref)
    for here, low, high, shift in regions:
        low, high = max(low, 3), min(high, rows - 3)
        advance(d_ref, None, here[:5], shift, new, coef_ref, scratch, low, high, True)
    fa_ref, fb_ref, fs_ref, sm_ref, sn_ref = scratch
    clear_outside(tile, last_tile, (fa_ref, fb_ref, fs_ref), own)
    rim, inside = gradients(
        phi_ref, m_ref, n_ref, coef_ref, fa_ref, fb_ref, fs_ref, sm_ref, sn_ref, g_ref, tau, pull, 0
    )
    loop(4, HALO, rim)
    total = loop(HALO, HALO + own, inside, jnp.zeros((8, 128), jnp.float32))
    loop(HALO + own, rows - 4, rim)
    clear_outside(tile, last_tile, (g_ref,), own)
    sums = jnp.sum(total, axis=0, keepdims=True) * live
    sums_ref[...] = jnp.broadcast_to(sums, sums_ref.shape)


def step_of(all_ref, cells):
    return step_scale / jnp.sqrt(jnp.sum(all_ref[...]) / cells + epsilon)


def third_kernel(
    cells, place_ref, scal_ref, all_ref, p_ref, m0_ref, n0_ref, lm0_ref, ln0_ref, h_ref, coef_ref,
    phi_ref, g_ref, sums_ref, m_ref, n_ref, fa_ref, fb_ref, fs_ref, sm_ref, sn_ref
):
    rows = p_ref.shape[1]
    own = rows - 2 * HALO
    tile, last_tile = place_ref[1], place_ref[2] - 1
    live = interior(place_ref)
    tau, pull = scal_ref[0], scal_ref[1]
    step = step_of(all_ref, cells) * live
    advance(
        h_ref, -step, (p_ref, m0_ref, n0_ref, lm0_ref, ln0_ref), 0,
        (phi_ref, m_ref, n_ref, None, None), coef_ref,
        (fa_ref, fb_ref, fs_ref, sm_ref, sn_ref), HALO - 1, HALO + own + 1, False,
    )
    clear_outside(tile, last_tile, (fa_ref, fb_ref, fs_ref), own)
    _, inside = gradients(
        phi_ref, m_ref, n_ref, coef_ref, fa_ref, fb_ref, fs_ref, sm_ref, sn_ref, g_ref, tau, pull,
        HALO,
    )
    total = loop(HALO, HALO + own, inside, jnp.zeros((8, 128), jnp.float32))
    sums = jnp.sum(total, axis=0, keepdims=True) * live
    sums_ref[...] = jnp.broadcast_to(sums, sums_ref.shape)


def last_kernel(cells, place_ref, all_ref, p_ref, g_ref, edge_ref, mid_ref):
    own = g_ref.shape[1]
    step = step_of(all_ref, cells) * interior(place_ref)
    for ref, low, high, shift in (
        (edge_ref, 0, HALO, 0),
        (mid_ref, HALO, own - HALO, HALO),
        (edge_ref, own - HALO, own, own - 2 * HALO),
    ):

        def move(at, carry, ref=ref, shift=shift):
            for comp in range(3):
                for place in TILES:
                    old = tile_of(p_ref, comp, at + HALO, place)
                    put(ref, comp, at - shift, place, old - step * tile_of(g_ref, comp, at, place))
            return carry

        loop(low, high, move)


def f32(*shape):
    return jax.ShapeDtypeStruct(shape, jnp.float32)


def call(kernel, operands, outs, scratch, scalars=1, small_out=()):
    smem = pl.BlockSpec(memory_space=pltpu.SMEM)
    vmem = pl.BlockSpec(memory_space=pltpu.VMEM)
    return pl.pallas_call(
        kernel,
        out_shape=outs,
        in_specs=[smem if i < scalars else vmem for i in range(len(operands))],
        out_specs=[smem if i in small_out else vmem for i in range(len(outs))],
        scratch_shapes=[pltpu.VMEM(shape, jnp.float32) for shape in scratch],
        compiler_params=pltpu.CompilerParams(vmem_limit_bytes=VMEM_LIMIT),
    )(*operands)


def beside(cells, axis, forward):
    count = lax.axis_size(axis)
    pairs = [(i, i + 1) if forward else (i + 1, i) for i in range(count - 1)]
    return lax.ppermute(cells, axis, pairs)


def from_everyone(rows):
    return lax.all_to_all(rows, IMG_TILE, 0, 0, tiled=True)


def body(spins, aniso):
    _, comps, depth, own, width = spins.shape
    images, tiles = lax.axis_size(IMG), lax.axis_size(TILE)
    devices = images * tiles
    cells = float(images * comps * depth * own * tiles * width)
    rows = own + 2 * HALO
    place = jnp.stack(
        [lax.axis_index(IMG), lax.axis_index(TILE), jnp.int32(tiles), jnp.int32(images)]
    ).astype(jnp.int32)
    start = jnp.swapaxes(spins[0], 1, 2)
    coefs = jnp.swapaxes(aniso, 0, 1)
    edge = jnp.concatenate([start[:, :HALO], start[:, own - HALO :]], axis=1)
    mid = start[:, HALO : own - HALO]
    ext = (3, rows, depth, width)
    ends, middle = (3, 4 * HALO, depth, width), (3, own - 4, depth, width)
    whole = f32(*ext)
    table = f32(devices, 128)
    coef_ext = None

    def scratch(count):
        return [(3, count, depth, width)] * 3 + [(count, depth, width)] * 2

    for _ in range(OUTER):
        a_edge, b_edge = beside(edge, IMG, True), beside(edge, IMG, False)
        a_mid, b_mid = beside(mid, IMG, True), beside(mid, IMG, False)
        bottom, top = edge[:, HALO:], edge[:, :HALO]
        if coef_ext is None:
            bottom = jnp.concatenate([bottom, coefs[None, own - HALO :]])
            top = jnp.concatenate([top, coefs[None, :HALO]])
        up_own, down_own = beside(bottom, TILE, True), beside(top, TILE, False)
        a_edge, b_edge, up_own, down_own = lax.optimization_barrier((a_edge, b_edge, up_own, down_own))
        up = beside(jnp.concatenate([a_edge[:, HALO:], b_edge[:, HALO:]]), TILE, True)
        down = beside(jnp.concatenate([a_edge[:, :HALO], b_edge[:, :HALO]]), TILE, False)
        shapes = [f32(*ends)] * 7 + [f32(PRODUCTS, 8, 128)]
        if coef_ext is None:
            *far, part, coef_ext = call(
                first_ends_kernel,
                [place, edge, a_edge, b_edge, up_own, down_own, up, down, coefs],
                [*shapes, f32(*ext[1:])],
                scratch(2 * HALO),
            )
        else:
            *far, part = call(
                ends_kernel,
                [place, edge, a_edge, b_edge, up_own, down_own, up, down, coef_ext],
                shapes,
                scratch(2 * HALO),
            )
        *near, sums = call(
            middle_kernel,
            [place, mid, a_mid, b_mid, *far[:3], part, coef_ext],
            [f32(*middle)] * 7 + [table],
            scratch(own - 4),
        )
        phi, m, n, lm, ln, g, scal, sums = call(
            lambda *refs: second_kernel(tiles, cells, *refs),
            [place, from_everyone(sums), *far, *near, coef_ext],
            [whole] * 6 + [f32(2), table],
            [ext, *scratch(rows)],
            small_out=(6,),
        )
        phi, g, sums = call(
            lambda *refs: third_kernel(cells, *refs),
            [place, scal, from_everyone(sums), phi, m, n, lm, ln, g, coef_ext],
            [whole, f32(3, own, depth, width), table],
            [ext, ext, *scratch(rows)],
            scalars=2,
        )
        edge, mid = call(
            lambda *refs: last_kernel(cells, *refs),
            [place, from_everyone(sums), phi, g],
            [f32(3, 2 * HALO, depth, width), f32(3, own - 2 * HALO, depth, width)],
            [],
        )
    final = jnp.concatenate([edge[:, :HALO], mid, edge[:, HALO:]], axis=1)
    return jnp.swapaxes(final, 1, 2)[None]


def solution(mesh):
    split = Mesh(mesh.devices.reshape(4, 4, 4, 2), IMG_TILE)
    return jax.shard_map(
        body,
        mesh=split,
        in_specs=(P(IMG, None, None, TILE, None), P(None, TILE, None)),
        out_specs=P(IMG, None, None, TILE, None),
        check_vma=False,
    )
```

```python
import jax
import jax.numpy as jnp
from jax import lax
from jax.experimental import pallas as pl
from jax.experimental.pallas import tpu as pltpu
from jax.sharding import Mesh
from jax.sharding import PartitionSpec as P

OUTER = 2
INNER = 3
IMG = ("img_0", "img_1")
TILE = ("tile_0", "tile_1")
IMG_TILE = ("img_0", "img_1", "tile_0", "tile_1")

spring_coef = 20.0
step_scale = 0.25
epsilon = 1e-06

HALO = 2 * INNER
PRODUCTS = 11
SUBLANES = 2
LANES = 2
TILES = range(SUBLANES * LANES)
VMEM_LIMIT = 16 * 1024 * 1024


def tile_of(ref, comp, at, place):
    z, y = divmod(place, LANES)
    return ref[comp, at, z * 8 : z * 8 + 8, y * 128 : y * 128 + 128]


def put(ref, comp, at, place, cells):
    z, y = divmod(place, LANES)
    ref[comp, at, z * 8 : z * 8 + 8, y * 128 : y * 128 + 128] = cells


def flat_of(ref, at, place):
    z, y = divmod(place, LANES)
    return ref[at, z * 8 : z * 8 + 8, y * 128 : y * 128 + 128]


def put_flat(ref, at, place, cells):
    z, y = divmod(place, LANES)
    ref[at, z * 8 : z * 8 + 8, y * 128 : y * 128 + 128] = cells


def vector(ref, at, place):
    return [tile_of(ref, comp, at, place) for comp in range(3)]


def around(line, axis):
    size = line[0].shape[axis]
    where = lax.broadcasted_iota(jnp.int32, line[0].shape, axis)
    first, last = where == 0, where == size - 1
    later = [pltpu.roll(cells, 1, axis) for cells in line]
    earlier = [pltpu.roll(cells, size - 1, axis) for cells in line]
    later, earlier = [0.0, *later], [*earlier, 0.0]
    return [
        jnp.where(first, later[i], later[i + 1]) + jnp.where(last, earlier[i + 1], earlier[i])
        for i in range(len(line))
    ]


def laplace(ref, comp, at):
    cells = [tile_of(ref, comp, at, place) for place in TILES]
    total = [
        (tile_of(ref, comp, at - 1, place) + tile_of(ref, comp, at + 1, place)) - 6.0 * cells[place]
        for place in TILES
    ]
    for z in range(SUBLANES):
        picked = range(z * LANES, z * LANES + LANES)
        for place, side in zip(picked, around([cells[i] for i in picked], 1)):
            total[place] = total[place] + side
    for y in range(LANES):
        picked = range(y, SUBLANES * LANES, LANES)
        for place, side in zip(picked, around([cells[i] for i in picked], 0)):
            total[place] = total[place] + side
    return cells, total


def dot(left, right):
    return left[0] * right[0] + left[1] * right[1] + left[2] * right[2]


def stiffness(square, coefs):
    plain = 0.5 - 0.125 * square
    return [plain, plain, plain + coefs]


def loop(low, high, body, carry=0):
    return lax.fori_loop(low, high, body, carry, unroll=4)


def clear_outside(tile, last_tile, refs, own):
    rows = refs[0].shape[1]

    @pl.when(tile == 0)
    def _():
        for ref in refs:
            ref[:, 0:HALO] = jnp.zeros((3, HALO) + ref.shape[2:], jnp.float32)

    @pl.when(tile == last_tile)
    def _():
        for ref in refs:
            ref[:, HALO + own :] = jnp.zeros((3, rows - HALO - own) + ref.shape[2:], jnp.float32)


def block(phi_ref, m_ref, n_ref, lm_ref, ln_ref, q_ref, r_ref, coef_ref, offset, scratch, cuts, clear, sums):
    fa_ref, fb_ref, fs_ref, sm_ref, sn_ref = scratch
    rows = phi_ref.shape[1]

    def drive(at, carry):
        for ref, lap_ref, out, squares, before in (
            (m_ref, lm_ref, fa_ref, sm_ref, None),
            (n_ref, ln_ref, fb_ref, sn_ref, (fa_ref, fs_ref)),
        ):
            stiff = []
            for place in TILES:
                cells = vector(ref, at, place)
                square = dot(cells, cells)
                put_flat(squares, at, place, square)
                stiff.append(stiffness(square, flat_of(coef_ref, at + offset, place)))
            for comp in range(3):
                cells, bent = laplace(ref, comp, at)
                for place in TILES:
                    put(lap_ref, comp, at, place, bent[place])
                    total = bent[place] + stiff[place][comp] * cells[place]
                    put(out, comp, at, place, total)
                    if before is not None:
                        total = total + tile_of(fa_ref, comp, at, place)
                        put(fs_ref, comp, at, place, total)
        return carry

    loop(1, rows - 1, drive)
    clear((fa_ref, fb_ref, fs_ref))

    def fields(at, sums):
        adjoint = [laplace(fs_ref, comp, at)[1] for comp in range(3)]
        for place in TILES:
            phi, m, n = (vector(ref, at, place) for ref in (phi_ref, m_ref, n_ref))
            fa, fb = vector(fa_ref, at, place), vector(fb_ref, at, place)
            square_m, square_n = flat_of(sm_ref, at, place), flat_of(sn_ref, at, place)
            coefs = flat_of(coef_ref, at + offset, place)
            stiff_m, stiff_n = stiffness(square_m, coefs), stiffness(square_n, coefs)
            turn_m, turn_n = 0.25 * dot(m, fa), 0.25 * dot(n, fb)
            gap = 0.125 * (square_m - square_n)
            rise_m = 0.25 * dot(m, phi) - 0.125 * square_m
            rise_n = 0.125 * square_n - 0.25 * dot(n, phi)
            flat, bent = [], []
            for c in range(3):
                flat.append(phi[c] * gap + m[c] * rise_m + n[c] * rise_n)
                bent.append(
                    0.25
                    * (
                        adjoint[c][place]
                        + (stiff_m[c] * fa[c] + stiff_n[c] * fb[c])
                        - (m[c] * turn_m + n[c] * turn_n)
                    )
                )
                put(q_ref, c, at, place, flat[c])
                put(r_ref, c, at, place, bent[c])
            if sums:
                behind = [2.0 * one - other for one, other in zip(phi, m)]
                ahead = [other - 2.0 * one for one, other in zip(phi, n)]
                pairs = (
                    (behind, behind), (behind, ahead), (ahead, ahead),
                    (flat, behind), (flat, ahead), (bent, behind), (bent, ahead),
                    (flat, flat), (flat, bent), (bent, bent), (fb, fb),
                )
                sums = [total + dot(left, right) for total, (left, right) in zip(sums, pairs)]
        return sums

    def rim(at, carry):
        fields(at, None)
        return carry

    loop(2, cuts[0], rim)
    sums = loop(cuts[0], cuts[1], fields, sums)
    loop(cuts[1], rows - 2, rim)
    clear((q_ref, r_ref))
    return sums


def join(pieces, outs, low, high, shift):
    own_ref, a_ref, b_ref = pieces
    phi_ref, m_ref, n_ref = outs

    def one(at, carry):
        for comp in range(3):
            for place in TILES:
                phi = tile_of(own_ref, comp, at, place)
                put(phi_ref, comp, at + shift, place, phi)
                put(m_ref, comp, at + shift, place, phi + tile_of(a_ref, comp, at, place))
                put(n_ref, comp, at + shift, place, phi + tile_of(b_ref, comp, at, place))
        return carry

    loop(low, high, one)


def first_ends_kernel(
    where, own_edge, a_edge, b_edge, up_own, down_own, up_ref, down_ref, coef_ref, *refs
):
    own = coef_ref.shape[0]
    coef_out, refs = refs[8], refs[:8] + refs[9:]
    coef_out[0:HALO] = up_own[3]
    coef_out[HALO : HALO + own] = coef_ref[...]
    coef_out[HALO + own :] = down_own[3]
    ends_kernel(
        where, own_edge, a_edge, b_edge, up_own, down_own, up_ref, down_ref, coef_out, *refs
    )


def ends_kernel(
    where, own_edge, a_edge, b_edge, up_own, down_own, up_ref, down_ref, coef_ref,
    phi_ref, m_ref, n_ref, lm_ref, ln_ref, q_ref, r_ref, sums_ref,
    fa_ref, fb_ref, fs_ref, sm_ref, sn_ref
):
    tile, last_tile = where[1], where[2] - 1
    span = 2 * HALO
    fields = (phi_ref, m_ref, n_ref, lm_ref, ln_ref, q_ref, r_ref)
    scratch = (fa_ref, fb_ref, fs_ref, sm_ref, sn_ref)
    halos = [
        (first, ref.at[0:3], ref.at[3:6])
        for first, ref in ((up_own, up_ref), (down_own, down_ref))
    ]
    edges = (own_edge, a_edge, b_edge)
    sums = [jnp.zeros((8, 128), jnp.float32)] * PRODUCTS
    for top in (True, False):
        first = 0 if top else span
        here = [ref.at[:, first : first + span] for ref in fields]
        join(halos[0 if top else 1], here[:3], 0, HALO, 0 if top else HALO)
        if top:
            join(edges, here[:3], 0, HALO, HALO)
        else:
            join(edges, here[:3], HALO, span, -HALO)

        def clear(refs, top=top):
            outside = slice(0, HALO) if top else slice(HALO, span)

            @pl.when(tile == (0 if top else last_tile))
            def _():
                for ref in refs:
                    ref[:, outside] = jnp.zeros((3, HALO) + ref.shape[2:], jnp.float32)

        cuts = (HALO, span - 2) if top else (2, HALO)
        offset = 0 if top else coef_ref.shape[0] - span
        sums = block(*here, coef_ref, offset, scratch, cuts, clear, sums)
    for which in range(PRODUCTS):
        sums_ref[which] = sums[which]


def middle_kernel(
    where, own_mid, a_mid, b_mid, phi_end, m_end, n_end, part_ref, coef_ref,
    phi_ref, m_ref, n_ref, lm_ref, ln_ref, q_ref, r_ref, sums_ref,
    fa_ref, fb_ref, fs_ref, sm_ref, sn_ref
):
    span = 2 * HALO
    rows = phi_ref.shape[1]
    outs = (phi_ref, m_ref, n_ref)
    for end, ref in zip((phi_end, m_end, n_end), outs):
        ref[:, 0:4] = end[:, span - 4 : span]
        ref[:, rows - 4 :] = end[:, span : span + 4]
    join((own_mid, a_mid, b_mid), outs, 0, rows - 8, 4)
    sums = block(
        *outs, lm_ref, ln_ref, q_ref, r_ref, coef_ref, span - 4,
        (fa_ref, fb_ref, fs_ref, sm_ref, sn_ref), (2, rows - 2), lambda refs: None,
        [part_ref[which] for which in range(PRODUCTS)],
    )
    lane = lax.broadcasted_iota(jnp.int32, (1, 128), 1)
    result = jnp.zeros((1, 128), jnp.float32)
    for which in range(PRODUCTS):
        result = jnp.where(lane == which, jnp.sum(sums[which]), result)
    sums_ref[...] = jnp.broadcast_to(result, sums_ref.shape)


def path_scalars(where, all_ref, tiles, cells):
    devices = all_ref.shape[0]
    images = devices // tiles
    table = jnp.sum(all_ref[...].reshape(images, tiles, 128), axis=1)
    lane = lax.broadcasted_iota(jnp.int32, (images, 128), 1)
    image = lax.broadcasted_iota(jnp.int32, (images, 128), 0)
    one = image[:, :1]

    def column(which):
        return jnp.sum(jnp.where(lane == which, table, 0.0), axis=1, keepdims=True)

    live = one < images - 1
    seg = jnp.where(live, jnp.sqrt(column(2) + epsilon), 0.0)
    drv = jnp.where(live, jnp.sqrt(0.25 * column(10) + epsilon), 0.0)
    path_len = jnp.sum(seg, axis=0, keepdims=True)
    tau = path_len / jnp.sum(drv, axis=0, keepdims=True)
    before = jnp.sum(jnp.where(image < lane, seg, 0.0), axis=0, keepdims=True)
    before = jnp.sum(jnp.where(image == lane, before, 0.0), axis=1, keepdims=True)
    target = one.astype(jnp.float32) / (images - 1)
    pull = spring_coef * (before / path_len - target) * (images - 1) / (2.0 * path_len)
    inv = 1.0 / tau
    near, far = inv + pull, pull - inv
    norm = near * near * column(0) + far * far * column(2) + 2.0 * near * far * column(1)
    norm += 2.0 * (near * column(3) + far * column(4))
    norm += 2.0 * tau * (near * column(5) + far * column(6))
    norm += column(7) + tau * (2.0 * column(8) + tau * column(9))
    inner = (one > 0) & (one < images - 1)
    total = jnp.sum(jnp.where(inner, norm, 0.0), axis=0, keepdims=True)
    step = step_scale / jnp.sqrt(total / cells + epsilon)
    mine = jnp.sum(jnp.where(one == where[0], pull, 0.0), axis=0, keepdims=True)
    return tau[0, 0], mine[0, 0], step[0, 0]


def gradients(
    phi_ref, m_ref, n_ref, coef_ref, fa_ref, fb_ref, fs_ref, sm_ref, sn_ref, g_ref, tau, pull, out
):
    inv = 1.0 / tau
    turned = 0.25 * tau

    def grad(at, total):
        adjoint = [laplace(fs_ref, comp, at)[1] for comp in range(3)]
        for place in TILES:
            phi, m, n = (vector(ref, at, place) for ref in (phi_ref, m_ref, n_ref))
            fa, fb = vector(fa_ref, at, place), vector(fb_ref, at, place)
            square_m, square_n = flat_of(sm_ref, at, place), flat_of(sn_ref, at, place)
            coefs = flat_of(coef_ref, at, place)
            stiff_m, stiff_n = stiffness(square_m, coefs), stiffness(square_n, coefs)
            gap = 0.125 * (square_m - square_n) + 4.0 * inv
            lean_m = (
                0.25 * (dot(m, phi) - turned * dot(m, fa)) - 0.125 * square_m - (pull + inv)
            )
            lean_n = (
                0.125 * square_n - 0.25 * (dot(n, phi) + turned * dot(n, fb)) + (pull - inv)
            )
            cells = [
                phi[c] * gap
                + (m[c] * lean_m + n[c] * lean_n)
                + turned * (adjoint[c][place] + (stiff_m[c] * fa[c] + stiff_n[c] * fb[c]))
                for c in range(3)
            ]
            for c in range(3):
                put(g_ref, c, at - out, place, cells[c])
            total = total + dot(cells, cells)
        return total

    def rim(at, carry):
        grad(at, 0.0)
        return carry

    return rim, grad


def interior(where):
    return jnp.where((where[0] > 0) & (where[0] < where[3] - 1), 1.0, 0.0)


def advance(
    step_ref, scale, old, old_shift, new, coef_ref, scratch, low, high, keep
):
    p_ref, m0_ref, n0_ref, lm0_ref, ln0_ref = old
    phi_ref, m_ref, n_ref, lm_ref, ln_ref = new
    fa_ref, fb_ref, fs_ref, sm_ref, sn_ref = scratch

    def body(at, carry):
        was = at + old_shift
        moves, bends = [], []
        for comp in range(3):
            cells, bent = laplace(step_ref, comp, at)
            if scale is not None:
                cells, bent = [scale * cell for cell in cells], [scale * cell for cell in bent]
            moves.append(cells)
            bends.append(bent)
            for place in TILES:
                put(phi_ref, comp, at, place, tile_of(p_ref, comp, was, place) + cells[place])
        for ref, lap_old, out, lap_new, drive_ref, squares, last in (
            (m0_ref, lm0_ref, m_ref, lm_ref, fa_ref, sm_ref, False),
            (n0_ref, ln0_ref, n_ref, ln_ref, fb_ref, sn_ref, True),
        ):
            for place in TILES:
                cells = [tile_of(ref, comp, was, place) + moves[comp][place] for comp in range(3)]
                square = dot(cells, cells)
                put_flat(squares, at, place, square)
                stiff = stiffness(square, flat_of(coef_ref, at, place))
                for comp in range(3):
                    put(out, comp, at, place, cells[comp])
                    bent = tile_of(lap_old, comp, was, place) + bends[comp][place]
                    if keep:
                        put(lap_new, comp, at, place, bent)
                    total = bent + stiff[comp] * cells[comp]
                    put(drive_ref, comp, at, place, total)
                    if last:
                        total = total + tile_of(fa_ref, comp, at, place)
                        put(fs_ref, comp, at, place, total)
        return carry

    loop(low, high, body)


def second_kernel(tiles, cells, where, all_ref, *refs):
    ends, mids, refs = refs[:7], refs[7:14], refs[14:]
    coef_ref, phi_ref, m_ref, n_ref, lm_ref, ln_ref, g_ref, scal_ref, sums_ref, d_ref = refs[:10]
    scratch = refs[10:]
    rows = phi_ref.shape[1]
    own = rows - 2 * HALO
    span = 2 * HALO
    tile, last_tile = where[1], where[2] - 1
    tau, pull, step = path_scalars(where, all_ref, tiles, cells)
    live = interior(where)
    step = step * live
    inv = 1.0 / tau
    scal_ref[0] = tau
    scal_ref[1] = pull
    from_p, from_m, from_n = -4.0 * step * inv, step * (inv + pull), step * (inv - pull)
    bend = step * tau
    regions = (
        (ends, 2, span - 2, 0),
        (mids, span - 2, rows - span + 2, 4 - span),
        (ends, rows - span + 2, rows - 2, 2 * span - rows),
    )
    for here, low, high, shift in regions:

        def direction(at, carry, here=here, shift=shift):
            was = at + shift
            for comp in range(3):
                for place in TILES:
                    p, m, n, q, r = (
                        tile_of(here[i], comp, was, place) for i in (0, 1, 2, 5, 6)
                    )
                    move = (from_p * p + from_m * m) + (from_n * n - step * q) - bend * r
                    put(d_ref, comp, at, place, move)
            return carry

        loop(low, high, direction)
    new = (phi_ref, m_ref, n_ref, lm_ref, ln_ref)
    for here, low, high, shift in regions:
        low, high = max(low, 3), min(high, rows - 3)
        advance(d_ref, None, here[:5], shift, new, coef_ref, scratch, low, high, True)
    fa_ref, fb_ref, fs_ref, sm_ref, sn_ref = scratch
    clear_outside(tile, last_tile, (fa_ref, fb_ref, fs_ref), own)
    rim, inside = gradients(
        phi_ref, m_ref, n_ref, coef_ref, fa_ref, fb_ref, fs_ref, sm_ref, sn_ref, g_ref, tau, pull, 0
    )
    loop(4, HALO, rim)
    total = loop(HALO, HALO + own, inside, jnp.zeros((8, 128), jnp.float32))
    loop(HALO + own, rows - 4, rim)
    clear_outside(tile, last_tile, (g_ref,), own)
    sums = jnp.sum(total, axis=0, keepdims=True) * live
    sums_ref[...] = jnp.broadcast_to(sums, sums_ref.shape)


def step_of(all_ref, cells):
    return step_scale / jnp.sqrt(jnp.sum(all_ref[...]) / cells + epsilon)


def third_kernel(
    cells, where, scal_ref, all_ref, p_ref, m0_ref, n0_ref, lm0_ref, ln0_ref, h_ref, coef_ref,
    phi_ref, g_ref, sums_ref, m_ref, n_ref, fa_ref, fb_ref, fs_ref, sm_ref, sn_ref
):
    rows = p_ref.shape[1]
    own = rows - 2 * HALO
    tile, last_tile = where[1], where[2] - 1
    live = interior(where)
    tau, pull = scal_ref[0], scal_ref[1]
    step = step_of(all_ref, cells) * live
    advance(
        h_ref, -step, (p_ref, m0_ref, n0_ref, lm0_ref, ln0_ref), 0,
        (phi_ref, m_ref, n_ref, None, None), coef_ref,
        (fa_ref, fb_ref, fs_ref, sm_ref, sn_ref), HALO - 1, HALO + own + 1, False,
    )
    clear_outside(tile, last_tile, (fa_ref, fb_ref, fs_ref), own)
    _, inside = gradients(
        phi_ref, m_ref, n_ref, coef_ref, fa_ref, fb_ref, fs_ref, sm_ref, sn_ref, g_ref, tau, pull,
        HALO,
    )
    total = loop(HALO, HALO + own, inside, jnp.zeros((8, 128), jnp.float32))
    sums = jnp.sum(total, axis=0, keepdims=True) * live
    sums_ref[...] = jnp.broadcast_to(sums, sums_ref.shape)


def last_kernel(cells, where, all_ref, p_ref, g_ref, edge_ref, mid_ref):
    own = g_ref.shape[1]
    step = step_of(all_ref, cells) * interior(where)
    for ref, low, high, shift in (
        (edge_ref, 0, HALO, 0),
        (mid_ref, HALO, own - HALO, HALO),
        (edge_ref, own - HALO, own, own - 2 * HALO),
    ):

        def move(at, carry, ref=ref, shift=shift):
            for comp in range(3):
                for place in TILES:
                    old = tile_of(p_ref, comp, at + HALO, place)
                    put(ref, comp, at - shift, place, old - step * tile_of(g_ref, comp, at, place))
            return carry

        loop(low, high, move)


def f32(*shape):
    return jax.ShapeDtypeStruct(shape, jnp.float32)


def position():
    found = []
    for axes in (IMG, TILE):
        index = 0
        for axis in axes:
            index = index * lax.axis_size(axis) + lax.axis_index(axis)
        found.append(index)
    return (*found, lax.axis_size(TILE), lax.axis_size(IMG))


def call(kernel, operands, outs, scratch, scalars=0, small_out=()):
    smem = pl.BlockSpec(memory_space=pltpu.SMEM)
    vmem = pl.BlockSpec(memory_space=pltpu.VMEM)
    return pl.pallas_call(
        lambda *refs: kernel(position(), *refs),
        out_shape=outs,
        in_specs=[smem if i < scalars else vmem for i in range(len(operands))],
        out_specs=[smem if i in small_out else vmem for i in range(len(outs))],
        scratch_shapes=[pltpu.VMEM(shape, jnp.float32) for shape in scratch],
        compiler_params=pltpu.CompilerParams(vmem_limit_bytes=VMEM_LIMIT),
    )(*operands)


def beside(cells, axis, forward):
    count = lax.axis_size(axis)
    pairs = [(i, i + 1) if forward else (i + 1, i) for i in range(count - 1)]
    return lax.ppermute(cells, axis, pairs)


def from_everyone(rows):
    return lax.all_to_all(rows, IMG_TILE, 0, 0, tiled=True)


def body(spins, aniso):
    _, comps, depth, own, width = spins.shape
    images, tiles = lax.axis_size(IMG), lax.axis_size(TILE)
    devices = images * tiles
    cells = float(images * comps * depth * own * tiles * width)
    rows = own + 2 * HALO
    start = jnp.swapaxes(spins[0], 1, 2)
    coefs = jnp.swapaxes(aniso, 0, 1)
    edge = jnp.concatenate([start[:, :HALO], start[:, own - HALO :]], axis=1)
    mid = start[:, HALO : own - HALO]
    ext = (3, rows, depth, width)
    ends, middle = (3, 4 * HALO, depth, width), (3, own - 4, depth, width)
    whole = f32(*ext)
    table = f32(devices, 128)
    coef_ext = None

    def scratch(count):
        return [(3, count, depth, width)] * 3 + [(count, depth, width)] * 2

    for _ in range(OUTER):
        a_edge, b_edge = beside(edge, IMG, True), beside(edge, IMG, False)
        a_mid, b_mid = beside(mid, IMG, True), beside(mid, IMG, False)
        bottom, top = edge[:, HALO:], edge[:, :HALO]
        if coef_ext is None:
            bottom = jnp.concatenate([bottom, coefs[None, own - HALO :]])
            top = jnp.concatenate([top, coefs[None, :HALO]])
        up_own, down_own = beside(bottom, TILE, True), beside(top, TILE, False)
        a_edge, b_edge, up_own, down_own = lax.optimization_barrier((a_edge, b_edge, up_own, down_own))
        up = beside(jnp.concatenate([a_edge[:, HALO:], b_edge[:, HALO:]]), TILE, True)
        down = beside(jnp.concatenate([a_edge[:, :HALO], b_edge[:, :HALO]]), TILE, False)
        shapes = [f32(*ends)] * 7 + [f32(PRODUCTS, 8, 128)]
        if coef_ext is None:
            *far, part, coef_ext = call(
                first_ends_kernel,
                [edge, a_edge, b_edge, up_own, down_own, up, down, coefs],
                [*shapes, f32(*ext[1:])],
                scratch(2 * HALO),
            )
        else:
            *far, part = call(
                ends_kernel,
                [edge, a_edge, b_edge, up_own, down_own, up, down, coef_ext],
                shapes,
                scratch(2 * HALO),
            )
        *near, sums = call(
            middle_kernel,
            [mid, a_mid, b_mid, *far[:3], part, coef_ext],
            [f32(*middle)] * 7 + [table],
            scratch(own - 4),
        )
        phi, m, n, lm, ln, g, scal, sums = call(
            lambda *refs: second_kernel(tiles, cells, *refs),
            [from_everyone(sums), *far, *near, coef_ext],
            [whole] * 6 + [f32(2), table],
            [ext, *scratch(rows)],
            small_out=(6,),
        )
        phi, g, sums = call(
            lambda *refs: third_kernel(cells, *refs),
            [scal, from_everyone(sums), phi, m, n, lm, ln, g, coef_ext],
            [whole, f32(3, own, depth, width), table],
            [ext, ext, *scratch(rows)],
            scalars=1,
        )
        edge, mid = call(
            lambda *refs: last_kernel(cells, *refs),
            [from_everyone(sums), phi, g],
            [f32(3, 2 * HALO, depth, width), f32(3, own - 2 * HALO, depth, width)],
            [],
        )
    final = jnp.concatenate([edge[:, :HALO], mid, edge[:, HALO:]], axis=1)
    return jnp.swapaxes(final, 1, 2)[None]


def solution(mesh):
    split = Mesh(mesh.devices.reshape(4, 4, 4, 2), IMG_TILE)
    return jax.shard_map(
        body,
        mesh=split,
        in_specs=(P(IMG, None, None, TILE, None), P(None, TILE, None)),
        out_specs=P(IMG, None, None, TILE, None),
        check_vma=False,
    )
```

```python
import jax
import jax.numpy as jnp
from jax import lax
from jax.experimental import pallas as pl
from jax.experimental.pallas import tpu as pltpu
from jax.sharding import Mesh
from jax.sharding import PartitionSpec as P

OUTER = 2
INNER = 3
IMG = ("img_0", "img_1")
TILE = ("tile_0", "tile_1")
IMG_TILE = ("img_0", "img_1", "tile_0", "tile_1")

spring_coef = 20.0
step_scale = 0.25
epsilon = 1e-06

HALO = 2 * INNER
PRODUCTS = 11
SUBLANES = 2
LANES = 2
TILES = range(SUBLANES * LANES)
VMEM_LIMIT = 16 * 1024 * 1024


def tile_of(ref, comp, at, place):
    z, y = divmod(place, LANES)
    return ref[comp, at, z * 8 : z * 8 + 8, y * 128 : y * 128 + 128]


def put(ref, comp, at, place, cells):
    z, y = divmod(place, LANES)
    ref[comp, at, z * 8 : z * 8 + 8, y * 128 : y * 128 + 128] = cells


def flat_of(ref, at, place):
    z, y = divmod(place, LANES)
    return ref[at, z * 8 : z * 8 + 8, y * 128 : y * 128 + 128]


def put_flat(ref, at, place, cells):
    z, y = divmod(place, LANES)
    ref[at, z * 8 : z * 8 + 8, y * 128 : y * 128 + 128] = cells


def vector(ref, at, place):
    return [tile_of(ref, comp, at, place) for comp in range(3)]


def around(line, axis):
    size = line[0].shape[axis]
    where = lax.broadcasted_iota(jnp.int32, line[0].shape, axis)
    first, last = where == 0, where == size - 1
    later = [pltpu.roll(cells, 1, axis) for cells in line]
    earlier = [pltpu.roll(cells, size - 1, axis) for cells in line]
    later, earlier = [0.0, *later], [*earlier, 0.0]
    return [
        jnp.where(first, later[i], later[i + 1]) + jnp.where(last, earlier[i + 1], earlier[i])
        for i in range(len(line))
    ]


def laplace(ref, comp, at):
    cells = [tile_of(ref, comp, at, place) for place in TILES]
    total = [
        (tile_of(ref, comp, at - 1, place) + tile_of(ref, comp, at + 1, place)) - 6.0 * cells[place]
        for place in TILES
    ]
    for z in range(SUBLANES):
        picked = range(z * LANES, z * LANES + LANES)
        for place, side in zip(picked, around([cells[i] for i in picked], 1)):
            total[place] = total[place] + side
    for y in range(LANES):
        picked = range(y, SUBLANES * LANES, LANES)
        for place, side in zip(picked, around([cells[i] for i in picked], 0)):
            total[place] = total[place] + side
    return cells, total


def dot(left, right):
    return left[0] * right[0] + left[1] * right[1] + left[2] * right[2]


def stiffness(square, coefs):
    plain = 0.5 - 0.125 * square
    return [plain, plain, plain + coefs]


def loop(low, high, body, carry=0):
    return lax.fori_loop(low, high, body, carry, unroll=4)


def clear_outside(tile, last_tile, refs, own):
    rows = refs[0].shape[1]

    @pl.when(tile == 0)
    def _():
        for ref in refs:
            ref[:, 0:HALO] = jnp.zeros((3, HALO) + ref.shape[2:], jnp.float32)

    @pl.when(tile == last_tile)
    def _():
        for ref in refs:
            ref[:, HALO + own :] = jnp.zeros((3, rows - HALO - own) + ref.shape[2:], jnp.float32)


def block(phi_ref, m_ref, n_ref, lm_ref, ln_ref, q_ref, r_ref, coef_ref, offset, scratch, cuts, clear, sums):
    fa_ref, fb_ref, fs_ref, sm_ref, sn_ref = scratch
    rows = phi_ref.shape[1]

    def drive(at, carry):
        for ref, lap_ref, out, squares, before in (
            (m_ref, lm_ref, fa_ref, sm_ref, None),
            (n_ref, ln_ref, fb_ref, sn_ref, (fa_ref, fs_ref)),
        ):
            stiff = []
            for place in TILES:
                cells = vector(ref, at, place)
                square = dot(cells, cells)
                put_flat(squares, at, place, square)
                stiff.append(stiffness(square, flat_of(coef_ref, at + offset, place)))
            for comp in range(3):
                cells, bent = laplace(ref, comp, at)
                for place in TILES:
                    put(lap_ref, comp, at, place, bent[place])
                    total = bent[place] + stiff[place][comp] * cells[place]
                    put(out, comp, at, place, total)
                    if before is not None:
                        total = total + tile_of(fa_ref, comp, at, place)
                        put(fs_ref, comp, at, place, total)
        return carry

    loop(1, rows - 1, drive)
    clear((fa_ref, fb_ref, fs_ref))

    def fields(at, sums):
        adjoint = [laplace(fs_ref, comp, at)[1] for comp in range(3)]
        for place in TILES:
            phi, m, n = (vector(ref, at, place) for ref in (phi_ref, m_ref, n_ref))
            fa, fb = vector(fa_ref, at, place), vector(fb_ref, at, place)
            square_m, square_n = flat_of(sm_ref, at, place), flat_of(sn_ref, at, place)
            coefs = flat_of(coef_ref, at + offset, place)
            stiff_m, stiff_n = stiffness(square_m, coefs), stiffness(square_n, coefs)
            turn_m, turn_n = 0.25 * dot(m, fa), 0.25 * dot(n, fb)
            gap = 0.125 * (square_m - square_n)
            rise_m = 0.25 * dot(m, phi) - 0.125 * square_m
            rise_n = 0.125 * square_n - 0.25 * dot(n, phi)
            flat, bent = [], []
            for c in range(3):
                flat.append(phi[c] * gap + m[c] * rise_m + n[c] * rise_n)
                bent.append(
                    0.25
                    * (
                        adjoint[c][place]
                        + (stiff_m[c] * fa[c] + stiff_n[c] * fb[c])
                        - (m[c] * turn_m + n[c] * turn_n)
                    )
                )
                put(q_ref, c, at, place, flat[c])
                put(r_ref, c, at, place, bent[c])
            if sums:
                behind = [2.0 * one - other for one, other in zip(phi, m)]
                ahead = [other - 2.0 * one for one, other in zip(phi, n)]
                pairs = (
                    (behind, behind), (behind, ahead), (ahead, ahead),
                    (flat, behind), (flat, ahead), (bent, behind), (bent, ahead),
                    (flat, flat), (flat, bent), (bent, bent), (fb, fb),
                )
                sums = [total + dot(left, right) for total, (left, right) in zip(sums, pairs)]
        return sums

    def rim(at, carry):
        fields(at, None)
        return carry

    loop(2, cuts[0], rim)
    sums = loop(cuts[0], cuts[1], fields, sums)
    loop(cuts[1], rows - 2, rim)
    clear((q_ref, r_ref))
    return sums


def join(pieces, outs, low, high, shift):
    own_ref, a_ref, b_ref = pieces
    phi_ref, m_ref, n_ref = outs

    def one(at, carry):
        for comp in range(3):
            for place in TILES:
                phi = tile_of(own_ref, comp, at, place)
                put(phi_ref, comp, at + shift, place, phi)
                put(m_ref, comp, at + shift, place, phi + tile_of(a_ref, comp, at, place))
                put(n_ref, comp, at + shift, place, phi + tile_of(b_ref, comp, at, place))
        return carry

    loop(low, high, one)


def first_ends_kernel(
    where, own_edge, a_edge, b_edge, up_own, down_own, up_ref, down_ref, coef_ref, *refs
):
    own = coef_ref.shape[0]
    coef_out, refs = refs[8], refs[:8] + refs[9:]
    coef_out[0:HALO] = up_own[3]
    coef_out[HALO : HALO + own] = coef_ref[...]
    coef_out[HALO + own :] = down_own[3]
    ends_kernel(
        where, own_edge, a_edge, b_edge, up_own, down_own, up_ref, down_ref, coef_out, *refs
    )


def ends_kernel(
    where, own_edge, a_edge, b_edge, up_own, down_own, up_ref, down_ref, coef_ref,
    phi_ref, m_ref, n_ref, lm_ref, ln_ref, q_ref, r_ref, sums_ref,
    fa_ref, fb_ref, fs_ref, sm_ref, sn_ref
):
    tile, last_tile = where[1], where[2] - 1
    span = 2 * HALO
    fields = (phi_ref, m_ref, n_ref, lm_ref, ln_ref, q_ref, r_ref)
    scratch = (fa_ref, fb_ref, fs_ref, sm_ref, sn_ref)
    halos = [
        (first, ref.at[0:3], ref.at[3:6])
        for first, ref in ((up_own, up_ref), (down_own, down_ref))
    ]
    edges = (own_edge, a_edge, b_edge)
    sums = [jnp.zeros((8, 128), jnp.float32)] * PRODUCTS
    for top in (True, False):
        first = 0 if top else span
        here = [ref.at[:, first : first + span] for ref in fields]
        join(halos[0 if top else 1], here[:3], 0, HALO, 0 if top else HALO)
        if top:
            join(edges, here[:3], 0, HALO, HALO)
        else:
            join(edges, here[:3], HALO, span, -HALO)

        def clear(refs, top=top):
            outside = slice(0, HALO) if top else slice(HALO, span)

            @pl.when(tile == (0 if top else last_tile))
            def _():
                for ref in refs:
                    ref[:, outside] = jnp.zeros((3, HALO) + ref.shape[2:], jnp.float32)

        cuts = (HALO, span - 2) if top else (2, HALO)
        offset = 0 if top else coef_ref.shape[0] - span
        sums = block(*here, coef_ref, offset, scratch, cuts, clear, sums)
    for which in range(PRODUCTS):
        sums_ref[which] = sums[which]


def middle_kernel(
    where, own_mid, a_mid, b_mid, phi_end, m_end, n_end, part_ref, coef_ref,
    phi_ref, m_ref, n_ref, lm_ref, ln_ref, q_ref, r_ref, sums_ref,
    fa_ref, fb_ref, fs_ref, sm_ref, sn_ref
):
    span = 2 * HALO
    rows = phi_ref.shape[1]
    outs = (phi_ref, m_ref, n_ref)
    for end, ref in zip((phi_end, m_end, n_end), outs):
        ref[:, 0:4] = end[:, span - 4 : span]
        ref[:, rows - 4 :] = end[:, span : span + 4]
    join((own_mid, a_mid, b_mid), outs, 0, rows - 8, 4)
    sums = block(
        *outs, lm_ref, ln_ref, q_ref, r_ref, coef_ref, span - 4,
        (fa_ref, fb_ref, fs_ref, sm_ref, sn_ref), (2, rows - 2), lambda refs: None,
        [part_ref[which] for which in range(PRODUCTS)],
    )
    lane = lax.broadcasted_iota(jnp.int32, (1, 128), 1)
    result = jnp.zeros((1, 128), jnp.float32)
    for which in range(PRODUCTS):
        result = jnp.where(lane == which, jnp.sum(sums[which]), result)
    sums_ref[...] = jnp.broadcast_to(result, sums_ref.shape)


def path_scalars(where, all_ref, tiles, cells):
    devices = all_ref.shape[0]
    images = devices // tiles
    table = jnp.sum(all_ref[...].reshape(images, tiles, 128), axis=1)
    lane = lax.broadcasted_iota(jnp.int32, (images, 128), 1)
    image = lax.broadcasted_iota(jnp.int32, (images, 128), 0)
    one = image[:, :1]

    def column(which):
        return jnp.sum(jnp.where(lane == which, table, 0.0), axis=1, keepdims=True)

    live = one < images - 1
    seg = jnp.where(live, jnp.sqrt(column(2) + epsilon), 0.0)
    drv = jnp.where(live, jnp.sqrt(0.25 * column(10) + epsilon), 0.0)
    path_len = jnp.sum(seg, axis=0, keepdims=True)
    tau = path_len / jnp.sum(drv, axis=0, keepdims=True)
    before = jnp.sum(jnp.where(image < lane, seg, 0.0), axis=0, keepdims=True)
    before = jnp.sum(jnp.where(image == lane, before, 0.0), axis=1, keepdims=True)
    target = one.astype(jnp.float32) / (images - 1)
    pull = spring_coef * (before / path_len - target) * (images - 1) / (2.0 * path_len)
    inv = 1.0 / tau
    near, far = inv + pull, pull - inv
    norm = near * near * column(0) + far * far * column(2) + 2.0 * near * far * column(1)
    norm += 2.0 * (near * column(3) + far * column(4))
    norm += 2.0 * tau * (near * column(5) + far * column(6))
    norm += column(7) + tau * (2.0 * column(8) + tau * column(9))
    inner = (one > 0) & (one < images - 1)
    total = jnp.sum(jnp.where(inner, norm, 0.0), axis=0, keepdims=True)
    step = step_scale / jnp.sqrt(total / cells + epsilon)
    mine = jnp.sum(jnp.where(one == where[0], pull, 0.0), axis=0, keepdims=True)
    return tau[0, 0], mine[0, 0], step[0, 0]


def gradients(
    phi_ref, m_ref, n_ref, coef_ref, fa_ref, fb_ref, fs_ref, sm_ref, sn_ref, g_ref, tau, pull, out
):
    inv = 1.0 / tau
    turned = 0.25 * tau

    def grad(at, total):
        adjoint = [laplace(fs_ref, comp, at)[1] for comp in range(3)]
        for place in TILES:
            phi, m, n = (vector(ref, at, place) for ref in (phi_ref, m_ref, n_ref))
            fa, fb = vector(fa_ref, at, place), vector(fb_ref, at, place)
            square_m, square_n = flat_of(sm_ref, at, place), flat_of(sn_ref, at, place)
            coefs = flat_of(coef_ref, at, place)
            stiff_m, stiff_n = stiffness(square_m, coefs), stiffness(square_n, coefs)
            gap = 0.125 * (square_m - square_n) + 4.0 * inv
            lean_m = (
                0.25 * (dot(m, phi) - turned * dot(m, fa)) - 0.125 * square_m - (pull + inv)
            )
            lean_n = (
                0.125 * square_n - 0.25 * (dot(n, phi) + turned * dot(n, fb)) + (pull - inv)
            )
            cells = [
                phi[c] * gap
                + (m[c] * lean_m + n[c] * lean_n)
                + turned * (adjoint[c][place] + (stiff_m[c] * fa[c] + stiff_n[c] * fb[c]))
                for c in range(3)
            ]
            for c in range(3):
                put(g_ref, c, at - out, place, cells[c])
            total = total + dot(cells, cells)
        return total

    def rim(at, carry):
        grad(at, 0.0)
        return carry

    return rim, grad


def interior(where):
    return jnp.where((where[0] > 0) & (where[0] < where[3] - 1), 1.0, 0.0)


def advance(
    step_ref, scale, old, old_shift, new, coef_ref, scratch, low, high, keep
):
    p_ref, m0_ref, n0_ref, lm0_ref, ln0_ref = old
    phi_ref, m_ref, n_ref, lm_ref, ln_ref = new
    fa_ref, fb_ref, fs_ref, sm_ref, sn_ref = scratch

    def body(at, carry):
        was = at + old_shift
        moves, bends = [], []
        for comp in range(3):
            cells, bent = laplace(step_ref, comp, at)
            if scale is not None:
                cells, bent = [scale * cell for cell in cells], [scale * cell for cell in bent]
            moves.append(cells)
            bends.append(bent)
            for place in TILES:
                put(phi_ref, comp, at, place, tile_of(p_ref, comp, was, place) + cells[place])
        for ref, lap_old, out, lap_new, drive_ref, squares, last in (
            (m0_ref, lm0_ref, m_ref, lm_ref, fa_ref, sm_ref, False),
            (n0_ref, ln0_ref, n_ref, ln_ref, fb_ref, sn_ref, True),
        ):
            for place in TILES:
                cells = [tile_of(ref, comp, was, place) + moves[comp][place] for comp in range(3)]
                square = dot(cells, cells)
                put_flat(squares, at, place, square)
                stiff = stiffness(square, flat_of(coef_ref, at, place))
                for comp in range(3):
                    put(out, comp, at, place, cells[comp])
                    bent = tile_of(lap_old, comp, was, place) + bends[comp][place]
                    if keep:
                        put(lap_new, comp, at, place, bent)
                    total = bent + stiff[comp] * cells[comp]
                    put(drive_ref, comp, at, place, total)
                    if last:
                        total = total + tile_of(fa_ref, comp, at, place)
                        put(fs_ref, comp, at, place, total)
        return carry

    loop(low, high, body)


def second_kernel(tiles, cells, where, all_ref, *refs):
    ends, mids, refs = refs[:7], refs[7:14], refs[14:]
    coef_ref, phi_ref, m_ref, n_ref, lm_ref, ln_ref, g_ref, scal_ref, sums_ref, d_ref = refs[:10]
    scratch = refs[10:]
    rows = phi_ref.shape[1]
    own = rows - 2 * HALO
    span = 2 * HALO
    tile, last_tile = where[1], where[2] - 1
    tau, pull, step = path_scalars(where, all_ref, tiles, cells)
    live = interior(where)
    step = step * live
    inv = 1.0 / tau
    first = lax.broadcasted_iota(jnp.int32, scal_ref.shape, 0) == 0
    scal_ref[...] = jnp.where(first, tau, pull)
    from_p, from_m, from_n = -4.0 * step * inv, step * (inv + pull), step * (inv - pull)
    bend = step * tau
    regions = (
        (ends, 2, span - 2, 0),
        (mids, span - 2, rows - span + 2, 4 - span),
        (ends, rows - span + 2, rows - 2, 2 * span - rows),
    )
    for here, low, high, shift in regions:

        def direction(at, carry, here=here, shift=shift):
            was = at + shift
            for comp in range(3):
                for place in TILES:
                    p, m, n, q, r = (
                        tile_of(here[i], comp, was, place) for i in (0, 1, 2, 5, 6)
                    )
                    move = (from_p * p + from_m * m) + (from_n * n - step * q) - bend * r
                    put(d_ref, comp, at, place, move)
            return carry

        loop(low, high, direction)
    new = (phi_ref, m_ref, n_ref, lm_ref, ln_ref)
    for here, low, high, shift in regions:
        low, high = max(low, 3), min(high, rows - 3)
        advance(d_ref, None, here[:5], shift, new, coef_ref, scratch, low, high, True)
    fa_ref, fb_ref, fs_ref, sm_ref, sn_ref = scratch
    clear_outside(tile, last_tile, (fa_ref, fb_ref, fs_ref), own)
    rim, inside = gradients(
        phi_ref, m_ref, n_ref, coef_ref, fa_ref, fb_ref, fs_ref, sm_ref, sn_ref, g_ref, tau, pull, 0
    )
    loop(4, HALO, rim)
    total = loop(HALO, HALO + own, inside, jnp.zeros((8, 128), jnp.float32))
    loop(HALO + own, rows - 4, rim)
    clear_outside(tile, last_tile, (g_ref,), own)
    sums = jnp.sum(total, axis=0, keepdims=True) * live
    sums_ref[...] = jnp.broadcast_to(sums, sums_ref.shape)


def step_of(all_ref, cells):
    return step_scale / jnp.sqrt(jnp.sum(all_ref[...]) / cells + epsilon)


def third_kernel(
    cells, where, scal_ref, all_ref, p_ref, m0_ref, n0_ref, lm0_ref, ln0_ref, h_ref, coef_ref,
    phi_ref, g_ref, sums_ref, m_ref, n_ref, fa_ref, fb_ref, fs_ref, sm_ref, sn_ref
):
    rows = p_ref.shape[1]
    own = rows - 2 * HALO
    tile, last_tile = where[1], where[2] - 1
    live = interior(where)
    kept = scal_ref[...]
    tau, pull = kept[0, 0], kept[1, 0]
    step = step_of(all_ref, cells) * live
    advance(
        h_ref, -step, (p_ref, m0_ref, n0_ref, lm0_ref, ln0_ref), 0,
        (phi_ref, m_ref, n_ref, None, None), coef_ref,
        (fa_ref, fb_ref, fs_ref, sm_ref, sn_ref), HALO - 1, HALO + own + 1, False,
    )
    clear_outside(tile, last_tile, (fa_ref, fb_ref, fs_ref), own)
    _, inside = gradients(
        phi_ref, m_ref, n_ref, coef_ref, fa_ref, fb_ref, fs_ref, sm_ref, sn_ref, g_ref, tau, pull,
        HALO,
    )
    total = loop(HALO, HALO + own, inside, jnp.zeros((8, 128), jnp.float32))
    sums = jnp.sum(total, axis=0, keepdims=True) * live
    sums_ref[...] = jnp.broadcast_to(sums, sums_ref.shape)


def last_kernel(cells, where, all_ref, p_ref, g_ref, edge_ref, mid_ref):
    own = g_ref.shape[1]
    step = step_of(all_ref, cells) * interior(where)
    for ref, low, high, shift in (
        (edge_ref, 0, HALO, 0),
        (mid_ref, HALO, own - HALO, HALO),
        (edge_ref, own - HALO, own, own - 2 * HALO),
    ):

        def move(at, carry, ref=ref, shift=shift):
            for comp in range(3):
                for place in TILES:
                    old = tile_of(p_ref, comp, at + HALO, place)
                    put(ref, comp, at - shift, place, old - step * tile_of(g_ref, comp, at, place))
            return carry

        loop(low, high, move)


def f32(*shape):
    return jax.ShapeDtypeStruct(shape, jnp.float32)


def position():
    found = []
    for axes in (IMG, TILE):
        index = 0
        for axis in axes:
            index = index * lax.axis_size(axis) + lax.axis_index(axis)
        found.append(index)
    return (*found, lax.axis_size(TILE), lax.axis_size(IMG))


def call(kernel, operands, outs, scratch):
    vmem = pl.BlockSpec(memory_space=pltpu.VMEM)
    return pl.pallas_call(
        lambda *refs: kernel(position(), *refs),
        out_shape=outs,
        in_specs=[vmem] * len(operands),
        out_specs=[vmem] * len(outs),
        scratch_shapes=[pltpu.VMEM(shape, jnp.float32) for shape in scratch],
        compiler_params=pltpu.CompilerParams(vmem_limit_bytes=VMEM_LIMIT),
    )(*operands)


def beside(cells, axis, forward):
    count = lax.axis_size(axis)
    pairs = [(i, i + 1) if forward else (i + 1, i) for i in range(count - 1)]
    return lax.ppermute(cells, axis, pairs)


def from_everyone(rows):
    return lax.all_to_all(rows, IMG_TILE, 0, 0, tiled=True)


def body(spins, aniso):
    _, comps, depth, own, width = spins.shape
    images, tiles = lax.axis_size(IMG), lax.axis_size(TILE)
    devices = images * tiles
    cells = float(images * comps * depth * own * tiles * width)
    rows = own + 2 * HALO
    start = jnp.swapaxes(spins[0], 1, 2)
    coefs = jnp.swapaxes(aniso, 0, 1)
    edge = jnp.concatenate([start[:, :HALO], start[:, own - HALO :]], axis=1)
    mid = start[:, HALO : own - HALO]
    ext = (3, rows, depth, width)
    ends, middle = (3, 4 * HALO, depth, width), (3, own - 4, depth, width)
    whole = f32(*ext)
    table = f32(devices, 128)
    coef_ext = None

    def scratch(count):
        return [(3, count, depth, width)] * 3 + [(count, depth, width)] * 2

    for _ in range(OUTER):
        a_edge, b_edge = beside(edge, IMG, True), beside(edge, IMG, False)
        a_mid, b_mid = beside(mid, IMG, True), beside(mid, IMG, False)
        bottom, top = edge[:, HALO:], edge[:, :HALO]
        if coef_ext is None:
            bottom = jnp.concatenate([bottom, coefs[None, own - HALO :]])
            top = jnp.concatenate([top, coefs[None, :HALO]])
        up_own, down_own = beside(bottom, TILE, True), beside(top, TILE, False)
        a_edge, b_edge, up_own, down_own = lax.optimization_barrier((a_edge, b_edge, up_own, down_own))
        up = beside(jnp.concatenate([a_edge[:, HALO:], b_edge[:, HALO:]]), TILE, True)
        down = beside(jnp.concatenate([a_edge[:, :HALO], b_edge[:, :HALO]]), TILE, False)
        shapes = [f32(*ends)] * 7 + [f32(PRODUCTS, 8, 128)]
        if coef_ext is None:
            *far, part, coef_ext = call(
                first_ends_kernel,
                [edge, a_edge, b_edge, up_own, down_own, up, down, coefs],
                [*shapes, f32(*ext[1:])],
                scratch(2 * HALO),
            )
        else:
            *far, part = call(
                ends_kernel,
                [edge, a_edge, b_edge, up_own, down_own, up, down, coef_ext],
                shapes,
                scratch(2 * HALO),
            )
        *near, sums = call(
            middle_kernel,
            [mid, a_mid, b_mid, *far[:3], part, coef_ext],
            [f32(*middle)] * 7 + [table],
            scratch(own - 4),
        )
        phi, m, n, lm, ln, g, scal, sums = call(
            lambda *refs: second_kernel(tiles, cells, *refs),
            [from_everyone(sums), *far, *near, coef_ext],
            [whole] * 6 + [f32(8, 128), table],
            [ext, *scratch(rows)],
        )
        phi, g, sums = call(
            lambda *refs: third_kernel(cells, *refs),
            [scal, from_everyone(sums), phi, m, n, lm, ln, g, coef_ext],
            [whole, f32(3, own, depth, width), table],
            [ext, ext, *scratch(rows)],
        )
        edge, mid = call(
            lambda *refs: last_kernel(cells, *refs),
            [from_everyone(sums), phi, g],
            [f32(3, 2 * HALO, depth, width), f32(3, own - 2 * HALO, depth, width)],
            [],
        )
    final = jnp.concatenate([edge[:, :HALO], mid, edge[:, HALO:]], axis=1)
    return jnp.swapaxes(final, 1, 2)[None]


def solution(mesh):
    split = Mesh(mesh.devices.reshape(4, 4, 4, 2), IMG_TILE)
    return jax.shard_map(
        body,
        mesh=split,
        in_specs=(P(IMG, None, None, TILE, None), P(None, TILE, None)),
        out_specs=P(IMG, None, None, TILE, None),
        check_vma=False,
    )
```

```python
import jax
import jax.numpy as jnp
from jax import lax
from jax.experimental import pallas as pl
from jax.experimental.pallas import tpu as pltpu
from jax.sharding import Mesh
from jax.sharding import PartitionSpec as P

OUTER = 2
INNER = 3
IMG = ("img_0", "img_1")
TILE = ("tile_0", "tile_1")
IMG_TILE = ("img_0", "img_1", "tile_0", "tile_1")

spring_coef = 20.0
step_scale = 0.25
epsilon = 1e-06

HALO = 2 * INNER
PRODUCTS = 11
SUBLANES = 2
LANES = 2
TILES = range(SUBLANES * LANES)
VMEM_LIMIT = 16 * 1024 * 1024


def tile_of(ref, comp, at, place):
    z, y = divmod(place, LANES)
    return ref[comp, at, z * 8 : z * 8 + 8, y * 128 : y * 128 + 128]


def put(ref, comp, at, place, cells):
    z, y = divmod(place, LANES)
    ref[comp, at, z * 8 : z * 8 + 8, y * 128 : y * 128 + 128] = cells


def flat_of(ref, at, place):
    z, y = divmod(place, LANES)
    return ref[at, z * 8 : z * 8 + 8, y * 128 : y * 128 + 128]


def put_flat(ref, at, place, cells):
    z, y = divmod(place, LANES)
    ref[at, z * 8 : z * 8 + 8, y * 128 : y * 128 + 128] = cells


def vector(ref, at, place):
    return [tile_of(ref, comp, at, place) for comp in range(3)]


def around(line, axis):
    size = line[0].shape[axis]
    where = lax.broadcasted_iota(jnp.int32, line[0].shape, axis)
    first, last = where == 0, where == size - 1
    later = [pltpu.roll(cells, 1, axis) for cells in line]
    earlier = [pltpu.roll(cells, size - 1, axis) for cells in line]
    later, earlier = [0.0, *later], [*earlier, 0.0]
    return [
        jnp.where(first, later[i], later[i + 1]) + jnp.where(last, earlier[i + 1], earlier[i])
        for i in range(len(line))
    ]


def laplace(ref, comp, at):
    cells = [tile_of(ref, comp, at, place) for place in TILES]
    total = [
        tile_of(ref, comp, at - 1, place) + tile_of(ref, comp, at + 1, place)
        for place in TILES
    ]
    for z in range(SUBLANES):
        picked = range(z * LANES, z * LANES + LANES)
        for place, side in zip(picked, around([cells[i] for i in picked], 1)):
            total[place] = total[place] + side
    for y in range(LANES):
        picked = range(y, SUBLANES * LANES, LANES)
        for place, side in zip(picked, around([cells[i] for i in picked], 0)):
            total[place] = total[place] + side
    return cells, total


def dot(left, right):
    return left[0] * right[0] + left[1] * right[1] + left[2] * right[2]


def stiffness(square, coefs):
    plain = (0.5 - 6.0) - square
    return [plain, plain, plain + coefs]


def loop(low, high, body, carry=0):
    count = high - low
    exact = [u for u in (8, 7, 6, 5, 4) if count and count % u == 0]
    unroll = exact[0] if exact else (8 if count >= 20 else 4)
    return lax.fori_loop(low, high, body, carry, unroll=unroll)


def clear_outside(tile, last_tile, refs, own):
    rows = refs[0].shape[1]

    @pl.when(tile == 0)
    def _():
        for ref in refs:
            ref[:, 0:HALO] = jnp.zeros((3, HALO) + ref.shape[2:], jnp.float32)

    @pl.when(tile == last_tile)
    def _():
        for ref in refs:
            ref[:, HALO + own :] = jnp.zeros((3, rows - HALO - own) + ref.shape[2:], jnp.float32)


def block(phi_ref, m_ref, n_ref, lm_ref, ln_ref, q_ref, r_ref, coef_ref, offset, scratch, cuts, clear, sums):
    fa_ref, fb_ref, fs_ref, sm_ref, sn_ref = scratch
    rows = phi_ref.shape[1]

    def drive(at, carry):
        for ref, lap_ref, out, squares, before in (
            (m_ref, lm_ref, fa_ref, sm_ref, None),
            (n_ref, ln_ref, fb_ref, sn_ref, (fa_ref, fs_ref)),
        ):
            stiff = []
            for place in TILES:
                cells = vector(ref, at, place)
                square = 0.125 * dot(cells, cells)
                put_flat(squares, at, place, square)
                stiff.append(stiffness(square, flat_of(coef_ref, at + offset, place)))
            for comp in range(3):
                cells, bent = laplace(ref, comp, at)
                for place in TILES:
                    put(lap_ref, comp, at, place, bent[place])
                    total = bent[place] + stiff[place][comp] * cells[place]
                    put(out, comp, at, place, total)
                    if before is not None:
                        total = total + tile_of(fa_ref, comp, at, place)
                        put(fs_ref, comp, at, place, total)
        return carry

    loop(1, rows - 1, drive)
    clear((fa_ref, fb_ref, fs_ref))

    def fields(at, sums):
        adjoint = [laplace(fs_ref, comp, at)[1] for comp in range(3)]
        for place in TILES:
            phi, m, n = (vector(ref, at, place) for ref in (phi_ref, m_ref, n_ref))
            fa, fb = vector(fa_ref, at, place), vector(fb_ref, at, place)
            square_m, square_n = flat_of(sm_ref, at, place), flat_of(sn_ref, at, place)
            coefs = flat_of(coef_ref, at + offset, place)
            stiff_m, stiff_n = stiffness(square_m, coefs), stiffness(square_n, coefs)
            turn_m, turn_n = 0.25 * dot(m, fa), 0.25 * dot(n, fb)
            gap = square_m - square_n
            rise_m = 0.25 * dot(m, phi) - square_m
            rise_n = square_n - 0.25 * dot(n, phi)
            flat, bent = [], []
            for c in range(3):
                flat.append(phi[c] * gap + m[c] * rise_m + n[c] * rise_n)
                bent.append(
                    0.25
                    * (
                        adjoint[c][place]
                        + (stiff_m[c] * fa[c] + stiff_n[c] * fb[c])
                        - (m[c] * turn_m + n[c] * turn_n)
                    )
                )
                put(q_ref, c, at, place, flat[c])
                put(r_ref, c, at, place, bent[c])
            if sums:
                behind = [2.0 * one - other for one, other in zip(phi, m)]
                ahead = [other - 2.0 * one for one, other in zip(phi, n)]
                pairs = (
                    (behind, behind), (behind, ahead), (ahead, ahead),
                    (flat, behind), (flat, ahead), (bent, behind), (bent, ahead),
                    (flat, flat), (flat, bent), (bent, bent), (fb, fb),
                )
                sums = [total + dot(left, right) for total, (left, right) in zip(sums, pairs)]
        return sums

    def rim(at, carry):
        fields(at, None)
        return carry

    loop(2, cuts[0], rim)
    sums = loop(cuts[0], cuts[1], fields, sums)
    loop(cuts[1], rows - 2, rim)
    clear((q_ref, r_ref))
    return sums


def join(pieces, outs, low, high, shift):
    own_ref, a_ref, b_ref = pieces
    phi_ref, m_ref, n_ref = outs

    def one(at, carry):
        for comp in range(3):
            for place in TILES:
                phi = tile_of(own_ref, comp, at, place)
                put(phi_ref, comp, at + shift, place, phi)
                put(m_ref, comp, at + shift, place, phi + tile_of(a_ref, comp, at, place))
                put(n_ref, comp, at + shift, place, phi + tile_of(b_ref, comp, at, place))
        return carry

    loop(low, high, one)


def first_ends_kernel(
    where, own_edge, a_edge, b_edge, up_own, down_own, up_ref, down_ref, coef_ref, *refs
):
    own = coef_ref.shape[0]
    coef_out, refs = refs[8], refs[:8] + refs[9:]
    coef_out[0:HALO] = up_own[3]
    coef_out[HALO : HALO + own] = coef_ref[...]
    coef_out[HALO + own :] = down_own[3]
    ends_kernel(
        where, own_edge, a_edge, b_edge, up_own, down_own, up_ref, down_ref, coef_out, *refs
    )


def ends_kernel(
    where, own_edge, a_edge, b_edge, up_own, down_own, up_ref, down_ref, coef_ref,
    phi_ref, m_ref, n_ref, lm_ref, ln_ref, q_ref, r_ref, sums_ref,
    fa_ref, fb_ref, fs_ref, sm_ref, sn_ref
):
    tile, last_tile = where[1], where[2] - 1
    span = 2 * HALO
    fields = (phi_ref, m_ref, n_ref, lm_ref, ln_ref, q_ref, r_ref)
    scratch = (fa_ref, fb_ref, fs_ref, sm_ref, sn_ref)
    halos = [
        (first, ref.at[0:3], ref.at[3:6])
        for first, ref in ((up_own, up_ref), (down_own, down_ref))
    ]
    edges = (own_edge, a_edge, b_edge)
    sums = [jnp.zeros((8, 128), jnp.float32)] * PRODUCTS
    for top in (True, False):
        first = 0 if top else span
        here = [ref.at[:, first : first + span] for ref in fields]
        join(halos[0 if top else 1], here[:3], 0, HALO, 0 if top else HALO)
        if top:
            join(edges, here[:3], 0, HALO, HALO)
        else:
            join(edges, here[:3], HALO, span, -HALO)

        def clear(refs, top=top):
            outside = slice(0, HALO) if top else slice(HALO, span)

            @pl.when(tile == (0 if top else last_tile))
            def _():
                for ref in refs:
                    ref[:, outside] = jnp.zeros((3, HALO) + ref.shape[2:], jnp.float32)

        cuts = (HALO, span - 2) if top else (2, HALO)
        offset = 0 if top else coef_ref.shape[0] - span
        sums = block(*here, coef_ref, offset, scratch, cuts, clear, sums)
    for which in range(PRODUCTS):
        sums_ref[which] = sums[which]


def middle_kernel(
    where, own_mid, a_mid, b_mid, phi_end, m_end, n_end, part_ref, coef_ref,
    phi_ref, m_ref, n_ref, lm_ref, ln_ref, q_ref, r_ref, sums_ref,
    fa_ref, fb_ref, fs_ref, sm_ref, sn_ref
):
    span = 2 * HALO
    rows = phi_ref.shape[1]
    outs = (phi_ref, m_ref, n_ref)
    for end, ref in zip((phi_end, m_end, n_end), outs):
        ref[:, 0:4] = end[:, span - 4 : span]
        ref[:, rows - 4 :] = end[:, span : span + 4]
    join((own_mid, a_mid, b_mid), outs, 0, rows - 8, 4)
    sums = block(
        *outs, lm_ref, ln_ref, q_ref, r_ref, coef_ref, span - 4,
        (fa_ref, fb_ref, fs_ref, sm_ref, sn_ref), (2, rows - 2), lambda refs: None,
        [part_ref[which] for which in range(PRODUCTS)],
    )
    lane = lax.broadcasted_iota(jnp.int32, (1, 128), 1)
    result = jnp.zeros((1, 128), jnp.float32)
    for which in range(PRODUCTS):
        result = jnp.where(lane == which, jnp.sum(sums[which]), result)
    sums_ref[...] = jnp.broadcast_to(result, sums_ref.shape)


def path_scalars(where, all_ref, tiles, cells):
    devices = all_ref.shape[0]
    images = devices // tiles
    table = jnp.sum(all_ref[...].reshape(images, tiles, 128), axis=1)
    lane = lax.broadcasted_iota(jnp.int32, (images, 128), 1)
    image = lax.broadcasted_iota(jnp.int32, (images, 128), 0)
    one = image[:, :1]

    def column(which):
        return jnp.sum(jnp.where(lane == which, table, 0.0), axis=1, keepdims=True)

    live = one < images - 1
    seg = jnp.where(live, jnp.sqrt(column(2) + epsilon), 0.0)
    drv = jnp.where(live, jnp.sqrt(0.25 * column(10) + epsilon), 0.0)
    path_len = jnp.sum(seg, axis=0, keepdims=True)
    tau = path_len / jnp.sum(drv, axis=0, keepdims=True)
    before = jnp.sum(jnp.where(image < lane, seg, 0.0), axis=0, keepdims=True)
    before = jnp.sum(jnp.where(image == lane, before, 0.0), axis=1, keepdims=True)
    target = one.astype(jnp.float32) / (images - 1)
    pull = spring_coef * (before / path_len - target) * (images - 1) / (2.0 * path_len)
    inv = 1.0 / tau
    near, far = inv + pull, pull - inv
    norm = near * near * column(0) + far * far * column(2) + 2.0 * near * far * column(1)
    norm += 2.0 * (near * column(3) + far * column(4))
    norm += 2.0 * tau * (near * column(5) + far * column(6))
    norm += column(7) + tau * (2.0 * column(8) + tau * column(9))
    inner = (one > 0) & (one < images - 1)
    total = jnp.sum(jnp.where(inner, norm, 0.0), axis=0, keepdims=True)
    step = step_scale / jnp.sqrt(total / cells + epsilon)
    mine = jnp.sum(jnp.where(one == where[0], pull, 0.0), axis=0, keepdims=True)
    return tau[0, 0], mine[0, 0], step[0, 0]


def gradients(
    phi_ref, m_ref, n_ref, coef_ref, fa_ref, fb_ref, fs_ref, sm_ref, sn_ref, g_ref, tau, pull, out
):
    inv = 1.0 / tau
    turned = 0.25 * tau

    def grad(at, total):
        adjoint = [laplace(fs_ref, comp, at)[1] for comp in range(3)]
        for place in TILES:
            phi, m, n = (vector(ref, at, place) for ref in (phi_ref, m_ref, n_ref))
            fa, fb = vector(fa_ref, at, place), vector(fb_ref, at, place)
            square_m, square_n = flat_of(sm_ref, at, place), flat_of(sn_ref, at, place)
            coefs = flat_of(coef_ref, at, place)
            stiff_m, stiff_n = stiffness(square_m, coefs), stiffness(square_n, coefs)
            gap = (square_m - square_n) + 4.0 * inv
            lean_m = (
                0.25 * (dot(m, phi) - turned * dot(m, fa)) - square_m - (pull + inv)
            )
            lean_n = (
                square_n - 0.25 * (dot(n, phi) + turned * dot(n, fb)) + (pull - inv)
            )
            cells = [
                phi[c] * gap
                + (m[c] * lean_m + n[c] * lean_n)
                + turned * (adjoint[c][place] + (stiff_m[c] * fa[c] + stiff_n[c] * fb[c]))
                for c in range(3)
            ]
            for c in range(3):
                put(g_ref, c, at - out, place, cells[c])
            total = total + dot(cells, cells)
        return total

    def rim(at, carry):
        grad(at, 0.0)
        return carry

    return rim, grad


def interior(where):
    return jnp.where((where[0] > 0) & (where[0] < where[3] - 1), 1.0, 0.0)


def advance(
    step_ref, scale, old, old_shift, new, coef_ref, scratch, low, high, keep
):
    p_ref, m0_ref, n0_ref, lm0_ref, ln0_ref = old
    phi_ref, m_ref, n_ref, lm_ref, ln_ref = new
    fa_ref, fb_ref, fs_ref, sm_ref, sn_ref = scratch

    def body(at, carry):
        was = at + old_shift
        moves, bends = [], []
        for comp in range(3):
            cells, bent = laplace(step_ref, comp, at)
            if scale is not None:
                cells, bent = [scale * cell for cell in cells], [scale * cell for cell in bent]
            moves.append(cells)
            bends.append(bent)
            for place in TILES:
                put(phi_ref, comp, at, place, tile_of(p_ref, comp, was, place) + cells[place])
        for ref, lap_old, out, lap_new, drive_ref, squares, last in (
            (m0_ref, lm0_ref, m_ref, lm_ref, fa_ref, sm_ref, False),
            (n0_ref, ln0_ref, n_ref, ln_ref, fb_ref, sn_ref, True),
        ):
            for place in TILES:
                cells = [tile_of(ref, comp, was, place) + moves[comp][place] for comp in range(3)]
                square = 0.125 * dot(cells, cells)
                put_flat(squares, at, place, square)
                stiff = stiffness(square, flat_of(coef_ref, at, place))
                for comp in range(3):
                    put(out, comp, at, place, cells[comp])
                    bent = tile_of(lap_old, comp, was, place) + bends[comp][place]
                    if keep:
                        put(lap_new, comp, at, place, bent)
                    total = bent + stiff[comp] * cells[comp]
                    put(drive_ref, comp, at, place, total)
                    if last:
                        total = total + tile_of(fa_ref, comp, at, place)
                        put(fs_ref, comp, at, place, total)
        return carry

    loop(low, high, body)


def second_kernel(tiles, cells, where, all_ref, *refs):
    ends, mids, refs = refs[:7], refs[7:14], refs[14:]
    coef_ref, phi_ref, m_ref, n_ref, lm_ref, ln_ref, g_ref, scal_ref, sums_ref, d_ref = refs[:10]
    scratch = refs[10:]
    rows = phi_ref.shape[1]
    own = rows - 2 * HALO
    span = 2 * HALO
    tile, last_tile = where[1], where[2] - 1
    tau, pull, step = path_scalars(where, all_ref, tiles, cells)
    live = interior(where)
    step = step * live
    inv = 1.0 / tau
    first = lax.broadcasted_iota(jnp.int32, scal_ref.shape, 0) == 0
    scal_ref[...] = jnp.where(first, tau, pull)
    from_p, from_m, from_n = -4.0 * step * inv, step * (inv + pull), step * (inv - pull)
    bend = step * tau
    regions = (
        (ends, 2, span - 2, 0),
        (mids, span - 2, rows - span + 2, 4 - span),
        (ends, rows - span + 2, rows - 2, 2 * span - rows),
    )
    for here, low, high, shift in regions:

        def direction(at, carry, here=here, shift=shift):
            was = at + shift
            for comp in range(3):
                for place in TILES:
                    p, m, n, q, r = (
                        tile_of(here[i], comp, was, place) for i in (0, 1, 2, 5, 6)
                    )
                    move = (from_p * p + from_m * m) + (from_n * n - step * q) - bend * r
                    put(d_ref, comp, at, place, move)
            return carry

        loop(low, high, direction)
    new = (phi_ref, m_ref, n_ref, lm_ref, ln_ref)
    for here, low, high, shift in regions:
        low, high = max(low, 3), min(high, rows - 3)
        advance(d_ref, None, here[:5], shift, new, coef_ref, scratch, low, high, True)
    fa_ref, fb_ref, fs_ref, sm_ref, sn_ref = scratch
    clear_outside(tile, last_tile, (fa_ref, fb_ref, fs_ref), own)
    rim, inside = gradients(
        phi_ref, m_ref, n_ref, coef_ref, fa_ref, fb_ref, fs_ref, sm_ref, sn_ref, g_ref, tau, pull, 0
    )
    loop(4, HALO, rim)
    total = loop(HALO, HALO + own, inside, jnp.zeros((8, 128), jnp.float32))
    loop(HALO + own, rows - 4, rim)
    clear_outside(tile, last_tile, (g_ref,), own)
    sums = jnp.sum(total, axis=0, keepdims=True) * live
    sums_ref[...] = jnp.broadcast_to(sums, sums_ref.shape)


def step_of(all_ref, cells):
    return step_scale / jnp.sqrt(jnp.sum(all_ref[...]) / cells + epsilon)


def third_kernel(
    cells, where, scal_ref, all_ref, p_ref, m0_ref, n0_ref, lm0_ref, ln0_ref, h_ref, coef_ref,
    phi_ref, g_ref, sums_ref, m_ref, n_ref, fa_ref, fb_ref, fs_ref, sm_ref, sn_ref
):
    rows = p_ref.shape[1]
    own = rows - 2 * HALO
    tile, last_tile = where[1], where[2] - 1
    live = interior(where)
    kept = scal_ref[...]
    tau, pull = kept[0, 0], kept[1, 0]
    step = step_of(all_ref, cells) * live
    advance(
        h_ref, -step, (p_ref, m0_ref, n0_ref, lm0_ref, ln0_ref), 0,
        (phi_ref, m_ref, n_ref, None, None), coef_ref,
        (fa_ref, fb_ref, fs_ref, sm_ref, sn_ref), HALO - 1, HALO + own + 1, False,
    )
    clear_outside(tile, last_tile, (fa_ref, fb_ref, fs_ref), own)
    _, inside = gradients(
        phi_ref, m_ref, n_ref, coef_ref, fa_ref, fb_ref, fs_ref, sm_ref, sn_ref, g_ref, tau, pull,
        HALO,
    )
    total = loop(HALO, HALO + own, inside, jnp.zeros((8, 128), jnp.float32))
    sums = jnp.sum(total, axis=0, keepdims=True) * live
    sums_ref[...] = jnp.broadcast_to(sums, sums_ref.shape)


def last_kernel(cells, where, all_ref, p_ref, g_ref, edge_ref, mid_ref):
    own = g_ref.shape[1]
    step = step_of(all_ref, cells) * interior(where)
    for ref, low, high, shift in (
        (edge_ref, 0, HALO, 0),
        (mid_ref, HALO, own - HALO, HALO),
        (edge_ref, own - HALO, own, own - 2 * HALO),
    ):

        def move(at, carry, ref=ref, shift=shift):
            for comp in range(3):
                for place in TILES:
                    old = tile_of(p_ref, comp, at + HALO, place)
                    put(ref, comp, at - shift, place, old - step * tile_of(g_ref, comp, at, place))
            return carry

        loop(low, high, move)


def f32(*shape):
    return jax.ShapeDtypeStruct(shape, jnp.float32)


def position():
    found = []
    for axes in (IMG, TILE):
        index = 0
        for axis in axes:
            index = index * lax.axis_size(axis) + lax.axis_index(axis)
        found.append(index)
    return (*found, lax.axis_size(TILE), lax.axis_size(IMG))


def call(kernel, operands, outs, scratch):
    vmem = pl.BlockSpec(memory_space=pltpu.VMEM)
    return pl.pallas_call(
        lambda *refs: kernel(position(), *refs),
        out_shape=outs,
        in_specs=[vmem] * len(operands),
        out_specs=[vmem] * len(outs),
        scratch_shapes=[pltpu.VMEM(shape, jnp.float32) for shape in scratch],
        compiler_params=pltpu.CompilerParams(vmem_limit_bytes=VMEM_LIMIT),
    )(*operands)


def beside(cells, axis, forward):
    count = lax.axis_size(axis)
    pairs = [(i, i + 1) if forward else (i + 1, i) for i in range(count - 1)]
    return lax.ppermute(cells, axis, pairs)


def from_everyone(rows):
    return lax.all_to_all(rows, IMG_TILE, 0, 0, tiled=True)


def body(spins, aniso):
    _, comps, depth, own, width = spins.shape
    images, tiles = lax.axis_size(IMG), lax.axis_size(TILE)
    devices = images * tiles
    cells = float(images * comps * depth * own * tiles * width)
    rows = own + 2 * HALO
    start = jnp.swapaxes(spins[0], 1, 2)
    coefs = jnp.swapaxes(aniso, 0, 1)
    edge = jnp.concatenate([start[:, :HALO], start[:, own - HALO :]], axis=1)
    mid = start[:, HALO : own - HALO]
    ext = (3, rows, depth, width)
    ends, middle = (3, 4 * HALO, depth, width), (3, own - 4, depth, width)
    whole = f32(*ext)
    table = f32(devices, 128)
    coef_ext = None

    def scratch(count):
        return [(3, count, depth, width)] * 3 + [(count, depth, width)] * 2

    for _ in range(OUTER):
        a_edge, b_edge = beside(edge, IMG, True), beside(edge, IMG, False)
        a_mid, b_mid = beside(mid, IMG, True), beside(mid, IMG, False)
        bottom, top = edge[:, HALO:], edge[:, :HALO]
        if coef_ext is None:
            bottom = jnp.concatenate([bottom, coefs[None, own - HALO :]])
            top = jnp.concatenate([top, coefs[None, :HALO]])
        up_own, down_own = beside(bottom, TILE, True), beside(top, TILE, False)
        a_edge, b_edge, up_own, down_own = lax.optimization_barrier((a_edge, b_edge, up_own, down_own))
        up = beside(jnp.concatenate([a_edge[:, HALO:], b_edge[:, HALO:]]), TILE, True)
        down = beside(jnp.concatenate([a_edge[:, :HALO], b_edge[:, :HALO]]), TILE, False)
        shapes = [f32(*ends)] * 7 + [f32(PRODUCTS, 8, 128)]
        if coef_ext is None:
            *far, part, coef_ext = call(
                first_ends_kernel,
                [edge, a_edge, b_edge, up_own, down_own, up, down, coefs],
                [*shapes, f32(*ext[1:])],
                scratch(2 * HALO),
            )
        else:
            *far, part = call(
                ends_kernel,
                [edge, a_edge, b_edge, up_own, down_own, up, down, coef_ext],
                shapes,
                scratch(2 * HALO),
            )
        *near, sums = call(
            middle_kernel,
            [mid, a_mid, b_mid, *far[:3], part, coef_ext],
            [f32(*middle)] * 7 + [table],
            scratch(own - 4),
        )
        phi, m, n, lm, ln, g, scal, sums = call(
            lambda *refs: second_kernel(tiles, cells, *refs),
            [from_everyone(sums), *far, *near, coef_ext],
            [whole] * 6 + [f32(8, 128), table],
            [ext, *scratch(rows)],
        )
        phi, g, sums = call(
            lambda *refs: third_kernel(cells, *refs),
            [scal, from_everyone(sums), phi, m, n, lm, ln, g, coef_ext],
            [whole, f32(3, own, depth, width), table],
            [ext, ext, *scratch(rows)],
        )
        edge, mid = call(
            lambda *refs: last_kernel(cells, *refs),
            [from_everyone(sums), phi, g],
            [f32(3, 2 * HALO, depth, width), f32(3, own - 2 * HALO, depth, width)],
            [],
        )
    final = jnp.concatenate([edge[:, :HALO], mid, edge[:, HALO:]], axis=1)
    return jnp.swapaxes(final, 1, 2)[None]


def solution(mesh):
    split = Mesh(mesh.devices.reshape(4, 4, 4, 2), IMG_TILE)
    return jax.shard_map(
        body,
        mesh=split,
        in_specs=(P(IMG, None, None, TILE, None), P(None, TILE, None)),
        out_specs=P(IMG, None, None, TILE, None),
        check_vma=False,
    )
```

```python
import jax
import jax.numpy as jnp
from jax import lax
from jax.experimental import pallas as pl
from jax.experimental.pallas import tpu as pltpu
from jax.sharding import Mesh
from jax.sharding import PartitionSpec as P

OUTER = 2
INNER = 3
IMG = ("img_0", "img_1")
TILE = ("tile_0", "tile_1")
IMG_TILE = ("img_0", "img_1", "tile_0", "tile_1")

spring_coef = 20.0
step_scale = 0.25
epsilon = 1e-06

HALO = 2 * INNER
PRODUCTS = 11
SUBLANES = 2
LANES = 2
TILES = range(SUBLANES * LANES)
VMEM_LIMIT = 16 * 1024 * 1024


def tile_of(ref, comp, at, place):
    z, y = divmod(place, LANES)
    return ref[comp, at, z * 8 : z * 8 + 8, y * 128 : y * 128 + 128]


def put(ref, comp, at, place, cells):
    z, y = divmod(place, LANES)
    ref[comp, at, z * 8 : z * 8 + 8, y * 128 : y * 128 + 128] = cells


def flat_of(ref, at, place):
    z, y = divmod(place, LANES)
    return ref[at, z * 8 : z * 8 + 8, y * 128 : y * 128 + 128]


def put_flat(ref, at, place, cells):
    z, y = divmod(place, LANES)
    ref[at, z * 8 : z * 8 + 8, y * 128 : y * 128 + 128] = cells


def vector(ref, at, place):
    return [tile_of(ref, comp, at, place) for comp in range(3)]


def around(line, axis):
    size = line[0].shape[axis]
    where = lax.broadcasted_iota(jnp.int32, line[0].shape, axis)
    first, last = where == 0, where == size - 1
    later = [pltpu.roll(cells, 1, axis) for cells in line]
    earlier = [pltpu.roll(cells, size - 1, axis) for cells in line]
    later, earlier = [0.0, *later], [*earlier, 0.0]
    return [
        jnp.where(first, later[i], later[i + 1]) + jnp.where(last, earlier[i + 1], earlier[i])
        for i in range(len(line))
    ]


def laplace(ref, comp, at):
    cells = [tile_of(ref, comp, at, place) for place in TILES]
    total = [
        tile_of(ref, comp, at - 1, place) + tile_of(ref, comp, at + 1, place)
        for place in TILES
    ]
    for z in range(SUBLANES):
        picked = range(z * LANES, z * LANES + LANES)
        for place, side in zip(picked, around([cells[i] for i in picked], 1)):
            total[place] = total[place] + side
    for y in range(LANES):
        picked = range(y, SUBLANES * LANES, LANES)
        for place, side in zip(picked, around([cells[i] for i in picked], 0)):
            total[place] = total[place] + side
    return cells, total


def dot(left, right):
    return left[0] * right[0] + left[1] * right[1] + left[2] * right[2]


def stiffness(square, coefs):
    plain = (0.5 - 6.0) - square
    return [plain, plain, plain + coefs]


def loop(low, high, body, carry=0):
    count = high - low
    exact = [u for u in (8, 7, 6, 5, 4) if count and count % u == 0]
    unroll = exact[0] if exact else (8 if count >= 20 else 4)
    return lax.fori_loop(low, high, body, carry, unroll=unroll)


def clear_outside(tile, last_tile, refs, own):
    rows = refs[0].shape[1]

    @pl.when(tile == 0)
    def _():
        for ref in refs:
            ref[:, 0:HALO] = jnp.zeros((3, HALO) + ref.shape[2:], jnp.float32)

    @pl.when(tile == last_tile)
    def _():
        for ref in refs:
            ref[:, HALO + own :] = jnp.zeros((3, rows - HALO - own) + ref.shape[2:], jnp.float32)


def residual(ref, lap_ref, out, squares, coef_ref, offset, other_ref=None, sum_ref=None):
    def body(at, carry):
        stiff = []
        for place in TILES:
            cells = vector(ref, at, place)
            square = 0.125 * dot(cells, cells)
            put_flat(squares, at, place, square)
            stiff.append(stiffness(square, flat_of(coef_ref, at + offset, place)))
        for comp in range(3):
            cells, bent = laplace(ref, comp, at)
            for place in TILES:
                put(lap_ref, comp, at, place, bent[place])
                total = bent[place] + stiff[place][comp] * cells[place]
                put(out, comp, at, place, total)
                if sum_ref is not None:
                    total = total + tile_of(other_ref, comp, at, place)
                    put(sum_ref, comp, at, place, total)
        return carry

    loop(1, ref.shape[1] - 1, body)


def block(phi_ref, m_ref, n_ref, q_ref, r_ref, coef_ref, offset, scratch, cuts, clear, sums):
    fa_ref, fb_ref, fs_ref, sm_ref, sn_ref = scratch
    rows = phi_ref.shape[1]

    def fields(at, sums):
        adjoint = [laplace(fs_ref, comp, at)[1] for comp in range(3)]
        for place in TILES:
            phi, m, n = (vector(ref, at, place) for ref in (phi_ref, m_ref, n_ref))
            fa, fb = vector(fa_ref, at, place), vector(fb_ref, at, place)
            square_m, square_n = flat_of(sm_ref, at, place), flat_of(sn_ref, at, place)
            coefs = flat_of(coef_ref, at + offset, place)
            stiff_m, stiff_n = stiffness(square_m, coefs), stiffness(square_n, coefs)
            turn_m, turn_n = 0.25 * dot(m, fa), 0.25 * dot(n, fb)
            gap = square_m - square_n
            rise_m = 0.25 * dot(m, phi) - square_m
            rise_n = square_n - 0.25 * dot(n, phi)
            flat, bent = [], []
            for c in range(3):
                flat.append(phi[c] * gap + m[c] * rise_m + n[c] * rise_n)
                bent.append(
                    0.25
                    * (
                        adjoint[c][place]
                        + (stiff_m[c] * fa[c] + stiff_n[c] * fb[c])
                        - (m[c] * turn_m + n[c] * turn_n)
                    )
                )
                put(q_ref, c, at, place, flat[c])
                put(r_ref, c, at, place, bent[c])
            if sums:
                behind = [2.0 * one - other for one, other in zip(phi, m)]
                ahead = [other - 2.0 * one for one, other in zip(phi, n)]
                pairs = (
                    (behind, behind), (behind, ahead), (ahead, ahead),
                    (flat, behind), (flat, ahead), (bent, behind), (bent, ahead),
                    (flat, flat), (flat, bent), (bent, bent), (fb, fb),
                )
                sums = [total + dot(left, right) for total, (left, right) in zip(sums, pairs)]
        return sums

    def rim(at, carry):
        fields(at, None)
        return carry

    loop(2, cuts[0], rim)
    sums = loop(cuts[0], cuts[1], fields, sums)
    loop(cuts[1], rows - 2, rim)
    clear((q_ref, r_ref))
    return sums


def join(own_ref, beside_refs, phi_ref, sum_refs, low, high, shift):
    def one(at, carry):
        for comp in range(3):
            for place in TILES:
                phi = tile_of(own_ref, comp, at, place)
                if phi_ref is not None:
                    put(phi_ref, comp, at + shift, place, phi)
                for ref, sum_ref in zip(beside_refs, sum_refs):
                    put(sum_ref, comp, at + shift, place, phi + tile_of(ref, comp, at, place))
        return carry

    loop(low, high, one)


def first_ends_kernel(
    where, own_edge, a_edge, b_edge, up_own, down_own, up_ref, down_ref, coef_ref, *refs
):
    own = coef_ref.shape[0]
    coef_out, refs = refs[8], refs[:8] + refs[9:]
    coef_out[0:HALO] = up_own[3]
    coef_out[HALO : HALO + own] = coef_ref[...]
    coef_out[HALO + own :] = down_own[3]
    ends_kernel(
        where, own_edge, a_edge, b_edge, up_own, down_own, up_ref, down_ref, coef_out, *refs
    )


def ends_kernel(
    where, own_edge, a_edge, b_edge, up_own, down_own, up_ref, down_ref, coef_ref,
    phi_ref, m_ref, n_ref, lm_ref, ln_ref, q_ref, r_ref, sums_ref,
    fa_ref, fb_ref, fs_ref, sm_ref, sn_ref
):
    tile, last_tile = where[1], where[2] - 1
    span = 2 * HALO
    fields = (phi_ref, m_ref, n_ref, lm_ref, ln_ref, q_ref, r_ref)
    scratch = (fa_ref, fb_ref, fs_ref, sm_ref, sn_ref)
    halos = [
        (first, ref.at[0:3], ref.at[3:6])
        for first, ref in ((up_own, up_ref), (down_own, down_ref))
    ]
    sums = [jnp.zeros((8, 128), jnp.float32)] * PRODUCTS
    for top in (True, False):
        first = 0 if top else span
        here = [ref.at[:, first : first + span] for ref in fields]
        phi, m, n, lm, ln, q, r = here
        halo = halos[0 if top else 1]
        join(halo[0], halo[1:], phi, (m, n), 0, HALO, 0 if top else HALO)
        if top:
            join(own_edge, (a_edge, b_edge), phi, (m, n), 0, HALO, HALO)
        else:
            join(own_edge, (a_edge, b_edge), phi, (m, n), HALO, span, -HALO)

        def clear(refs, top=top):
            outside = slice(0, HALO) if top else slice(HALO, span)

            @pl.when(tile == (0 if top else last_tile))
            def _():
                for ref in refs:
                    ref[:, outside] = jnp.zeros((3, HALO) + ref.shape[2:], jnp.float32)

        cuts = (HALO, span - 2) if top else (2, HALO)
        offset = 0 if top else coef_ref.shape[0] - span
        residual(m, lm, fa_ref, sm_ref, coef_ref, offset)
        residual(n, ln, fb_ref, sn_ref, coef_ref, offset, fa_ref, fs_ref)
        clear((fa_ref, fb_ref, fs_ref))
        sums = block(phi, m, n, q, r, coef_ref, offset, scratch, cuts, clear, sums)
    for which in range(PRODUCTS):
        sums_ref[which] = sums[which]


def ends_into(ref, end, span):
    rows = ref.shape[1]
    ref[:, 0:4] = end[:, span - 4 : span]
    ref[:, rows - 4 :] = end[:, span : span + 4]


def ahead_kernel(
    where, own_mid, b_mid, phi_end, n_end, coef_ref, phi_ref, n_ref, ln_ref, fb_ref, sn_ref
):
    span = 2 * HALO
    ends_into(phi_ref, phi_end, span)
    ends_into(n_ref, n_end, span)
    join(own_mid, (b_mid,), phi_ref, (n_ref,), 0, phi_ref.shape[1] - 8, 4)
    residual(n_ref, ln_ref, fb_ref, sn_ref, coef_ref, span - 4)


def middle_kernel(
    where, own_mid, a_mid, m_end, phi_ref, n_ref, fb_ref, sn_ref, part_ref, coef_ref,
    m_ref, lm_ref, q_ref, r_ref, sums_ref, fa_ref, fs_ref, sm_ref
):
    span = 2 * HALO
    rows = phi_ref.shape[1]
    ends_into(m_ref, m_end, span)
    join(own_mid, (a_mid,), None, (m_ref,), 0, rows - 8, 4)
    residual(m_ref, lm_ref, fa_ref, sm_ref, coef_ref, span - 4, fb_ref, fs_ref)
    sums = block(
        phi_ref, m_ref, n_ref, q_ref, r_ref, coef_ref, span - 4,
        (fa_ref, fb_ref, fs_ref, sm_ref, sn_ref), (2, rows - 2), lambda refs: None,
        [part_ref[which] for which in range(PRODUCTS)],
    )
    lane = lax.broadcasted_iota(jnp.int32, (1, 128), 1)
    result = jnp.zeros((1, 128), jnp.float32)
    for which in range(PRODUCTS):
        result = jnp.where(lane == which, jnp.sum(sums[which]), result)
    sums_ref[...] = jnp.broadcast_to(result, sums_ref.shape)


def path_scalars(where, all_ref, tiles, cells):
    devices = all_ref.shape[0]
    images = devices // tiles
    table = jnp.sum(all_ref[...].reshape(images, tiles, 128), axis=1)
    lane = lax.broadcasted_iota(jnp.int32, (images, 128), 1)
    image = lax.broadcasted_iota(jnp.int32, (images, 128), 0)
    one = image[:, :1]

    def column(which):
        return jnp.sum(jnp.where(lane == which, table, 0.0), axis=1, keepdims=True)

    live = one < images - 1
    seg = jnp.where(live, jnp.sqrt(column(2) + epsilon), 0.0)
    drv = jnp.where(live, jnp.sqrt(0.25 * column(10) + epsilon), 0.0)
    path_len = jnp.sum(seg, axis=0, keepdims=True)
    tau = path_len / jnp.sum(drv, axis=0, keepdims=True)
    before = jnp.sum(jnp.where(image < lane, seg, 0.0), axis=0, keepdims=True)
    before = jnp.sum(jnp.where(image == lane, before, 0.0), axis=1, keepdims=True)
    target = one.astype(jnp.float32) / (images - 1)
    pull = spring_coef * (before / path_len - target) * (images - 1) / (2.0 * path_len)
    inv = 1.0 / tau
    near, far = inv + pull, pull - inv
    norm = near * near * column(0) + far * far * column(2) + 2.0 * near * far * column(1)
    norm += 2.0 * (near * column(3) + far * column(4))
    norm += 2.0 * tau * (near * column(5) + far * column(6))
    norm += column(7) + tau * (2.0 * column(8) + tau * column(9))
    inner = (one > 0) & (one < images - 1)
    total = jnp.sum(jnp.where(inner, norm, 0.0), axis=0, keepdims=True)
    step = step_scale / jnp.sqrt(total / cells + epsilon)
    mine = jnp.sum(jnp.where(one == where[0], pull, 0.0), axis=0, keepdims=True)
    return tau[0, 0], mine[0, 0], step[0, 0]


def gradients(
    phi_ref, m_ref, n_ref, coef_ref, fa_ref, fb_ref, fs_ref, sm_ref, sn_ref, g_ref, tau, pull, out
):
    inv = 1.0 / tau
    turned = 0.25 * tau

    def grad(at, total):
        adjoint = [laplace(fs_ref, comp, at)[1] for comp in range(3)]
        for place in TILES:
            phi, m, n = (vector(ref, at, place) for ref in (phi_ref, m_ref, n_ref))
            fa, fb = vector(fa_ref, at, place), vector(fb_ref, at, place)
            square_m, square_n = flat_of(sm_ref, at, place), flat_of(sn_ref, at, place)
            coefs = flat_of(coef_ref, at, place)
            stiff_m, stiff_n = stiffness(square_m, coefs), stiffness(square_n, coefs)
            gap = (square_m - square_n) + 4.0 * inv
            lean_m = (
                0.25 * (dot(m, phi) - turned * dot(m, fa)) - square_m - (pull + inv)
            )
            lean_n = (
                square_n - 0.25 * (dot(n, phi) + turned * dot(n, fb)) + (pull - inv)
            )
            cells = [
                phi[c] * gap
                + (m[c] * lean_m + n[c] * lean_n)
                + turned * (adjoint[c][place] + (stiff_m[c] * fa[c] + stiff_n[c] * fb[c]))
                for c in range(3)
            ]
            for c in range(3):
                put(g_ref, c, at - out, place, cells[c])
            total = total + dot(cells, cells)
        return total

    def rim(at, carry):
        grad(at, 0.0)
        return carry

    return rim, grad


def interior(where):
    return jnp.where((where[0] > 0) & (where[0] < where[3] - 1), 1.0, 0.0)


def advance(
    step_ref, scale, old, old_shift, new, coef_ref, scratch, low, high, keep
):
    p_ref, m0_ref, n0_ref, lm0_ref, ln0_ref = old
    phi_ref, m_ref, n_ref, lm_ref, ln_ref = new
    fa_ref, fb_ref, fs_ref, sm_ref, sn_ref = scratch

    def body(at, carry):
        was = at + old_shift
        moves, bends = [], []
        for comp in range(3):
            cells, bent = laplace(step_ref, comp, at)
            if scale is not None:
                cells, bent = [scale * cell for cell in cells], [scale * cell for cell in bent]
            moves.append(cells)
            bends.append(bent)
            for place in TILES:
                put(phi_ref, comp, at, place, tile_of(p_ref, comp, was, place) + cells[place])
        for ref, lap_old, out, lap_new, drive_ref, squares, last in (
            (m0_ref, lm0_ref, m_ref, lm_ref, fa_ref, sm_ref, False),
            (n0_ref, ln0_ref, n_ref, ln_ref, fb_ref, sn_ref, True),
        ):
            for place in TILES:
                cells = [tile_of(ref, comp, was, place) + moves[comp][place] for comp in range(3)]
                square = 0.125 * dot(cells, cells)
                put_flat(squares, at, place, square)
                stiff = stiffness(square, flat_of(coef_ref, at, place))
                for comp in range(3):
                    put(out, comp, at, place, cells[comp])
                    bent = tile_of(lap_old, comp, was, place) + bends[comp][place]
                    if keep:
                        put(lap_new, comp, at, place, bent)
                    total = bent + stiff[comp] * cells[comp]
                    put(drive_ref, comp, at, place, total)
                    if last:
                        total = total + tile_of(fa_ref, comp, at, place)
                        put(fs_ref, comp, at, place, total)
        return carry

    loop(low, high, body)


def second_kernel(tiles, cells, where, all_ref, *refs):
    ends, mids, refs = refs[:7], refs[7:14], refs[14:]
    coef_ref, phi_ref, m_ref, n_ref, lm_ref, ln_ref, g_ref, scal_ref, sums_ref, d_ref = refs[:10]
    scratch = refs[10:]
    rows = phi_ref.shape[1]
    own = rows - 2 * HALO
    span = 2 * HALO
    tile, last_tile = where[1], where[2] - 1
    tau, pull, step = path_scalars(where, all_ref, tiles, cells)
    live = interior(where)
    step = step * live
    inv = 1.0 / tau
    first = lax.broadcasted_iota(jnp.int32, scal_ref.shape, 0) == 0
    scal_ref[...] = jnp.where(first, tau, pull)
    from_p, from_m, from_n = -4.0 * step * inv, step * (inv + pull), step * (inv - pull)
    bend = step * tau
    regions = (
        (ends, 2, span - 2, 0),
        (mids, span - 2, rows - span + 2, 4 - span),
        (ends, rows - span + 2, rows - 2, 2 * span - rows),
    )
    for here, low, high, shift in regions:

        def direction(at, carry, here=here, shift=shift):
            was = at + shift
            for comp in range(3):
                for place in TILES:
                    p, m, n, q, r = (
                        tile_of(here[i], comp, was, place) for i in (0, 1, 2, 5, 6)
                    )
                    move = (from_p * p + from_m * m) + (from_n * n - step * q) - bend * r
                    put(d_ref, comp, at, place, move)
            return carry

        loop(low, high, direction)
    new = (phi_ref, m_ref, n_ref, lm_ref, ln_ref)
    for here, low, high, shift in regions:
        low, high = max(low, 3), min(high, rows - 3)
        advance(d_ref, None, here[:5], shift, new, coef_ref, scratch, low, high, True)
    fa_ref, fb_ref, fs_ref, sm_ref, sn_ref = scratch
    clear_outside(tile, last_tile, (fa_ref, fb_ref, fs_ref), own)
    rim, inside = gradients(
        phi_ref, m_ref, n_ref, coef_ref, fa_ref, fb_ref, fs_ref, sm_ref, sn_ref, g_ref, tau, pull, 0
    )
    loop(4, HALO, rim)
    total = loop(HALO, HALO + own, inside, jnp.zeros((8, 128), jnp.float32))
    loop(HALO + own, rows - 4, rim)
    clear_outside(tile, last_tile, (g_ref,), own)
    sums = jnp.sum(total, axis=0, keepdims=True) * live
    sums_ref[...] = jnp.broadcast_to(sums, sums_ref.shape)


def step_of(all_ref, cells):
    return step_scale / jnp.sqrt(jnp.sum(all_ref[...]) / cells + epsilon)


def third_kernel(
    cells, where, scal_ref, all_ref, p_ref, m0_ref, n0_ref, lm0_ref, ln0_ref, h_ref, coef_ref,
    phi_ref, g_ref, sums_ref, m_ref, n_ref, fa_ref, fb_ref, fs_ref, sm_ref, sn_ref
):
    rows = p_ref.shape[1]
    own = rows - 2 * HALO
    tile, last_tile = where[1], where[2] - 1
    live = interior(where)
    kept = scal_ref[...]
    tau, pull = kept[0, 0], kept[1, 0]
    step = step_of(all_ref, cells) * live
    advance(
        h_ref, -step, (p_ref, m0_ref, n0_ref, lm0_ref, ln0_ref), 0,
        (phi_ref, m_ref, n_ref, None, None), coef_ref,
        (fa_ref, fb_ref, fs_ref, sm_ref, sn_ref), HALO - 1, HALO + own + 1, False,
    )
    clear_outside(tile, last_tile, (fa_ref, fb_ref, fs_ref), own)
    _, inside = gradients(
        phi_ref, m_ref, n_ref, coef_ref, fa_ref, fb_ref, fs_ref, sm_ref, sn_ref, g_ref, tau, pull,
        HALO,
    )
    total = loop(HALO, HALO + own, inside, jnp.zeros((8, 128), jnp.float32))
    sums = jnp.sum(total, axis=0, keepdims=True) * live
    sums_ref[...] = jnp.broadcast_to(sums, sums_ref.shape)


def last_kernel(cells, where, all_ref, p_ref, g_ref, edge_ref, mid_ref):
    own = g_ref.shape[1]
    step = step_of(all_ref, cells) * interior(where)
    for ref, low, high, shift in (
        (edge_ref, 0, HALO, 0),
        (mid_ref, HALO, own - HALO, HALO),
        (edge_ref, own - HALO, own, own - 2 * HALO),
    ):

        def move(at, carry, ref=ref, shift=shift):
            for comp in range(3):
                for place in TILES:
                    old = tile_of(p_ref, comp, at + HALO, place)
                    put(ref, comp, at - shift, place, old - step * tile_of(g_ref, comp, at, place))
            return carry

        loop(low, high, move)


def f32(*shape):
    return jax.ShapeDtypeStruct(shape, jnp.float32)


def position():
    found = []
    for axes in (IMG, TILE):
        index = 0
        for axis in axes:
            index = index * lax.axis_size(axis) + lax.axis_index(axis)
        found.append(index)
    return (*found, lax.axis_size(TILE), lax.axis_size(IMG))


def call(kernel, operands, outs, scratch):
    vmem = pl.BlockSpec(memory_space=pltpu.VMEM)
    return pl.pallas_call(
        lambda *refs: kernel(position(), *refs),
        out_shape=outs,
        in_specs=[vmem] * len(operands),
        out_specs=[vmem] * len(outs),
        scratch_shapes=[pltpu.VMEM(shape, jnp.float32) for shape in scratch],
        compiler_params=pltpu.CompilerParams(vmem_limit_bytes=VMEM_LIMIT),
    )(*operands)


def beside(cells, axis, forward):
    count = lax.axis_size(axis)
    pairs = [(i, i + 1) if forward else (i + 1, i) for i in range(count - 1)]
    return lax.ppermute(cells, axis, pairs)


def from_everyone(rows):
    return lax.all_to_all(rows, IMG_TILE, 0, 0, tiled=True)


def body(spins, aniso):
    _, comps, depth, own, width = spins.shape
    images, tiles = lax.axis_size(IMG), lax.axis_size(TILE)
    devices = images * tiles
    cells = float(images * comps * depth * own * tiles * width)
    rows = own + 2 * HALO
    start = jnp.swapaxes(spins[0], 1, 2)
    coefs = jnp.swapaxes(aniso, 0, 1)
    edge = jnp.concatenate([start[:, :HALO], start[:, own - HALO :]], axis=1)
    mid = start[:, HALO : own - HALO]
    ext = (3, rows, depth, width)
    ends, middle = (3, 4 * HALO, depth, width), (3, own - 4, depth, width)
    whole = f32(*ext)
    table = f32(devices, 128)
    coef_ext = None

    def scratch(count):
        return [(3, count, depth, width)] * 3 + [(count, depth, width)] * 2

    for _ in range(OUTER):
        a_edge, b_edge = beside(edge, IMG, True), beside(edge, IMG, False)
        a_mid, b_mid = beside(mid, IMG, True), beside(mid, IMG, False)
        bottom, top = edge[:, HALO:], edge[:, :HALO]
        if coef_ext is None:
            bottom = jnp.concatenate([bottom, coefs[None, own - HALO :]])
            top = jnp.concatenate([top, coefs[None, :HALO]])
        up_own, down_own = beside(bottom, TILE, True), beside(top, TILE, False)
        a_edge, b_edge, up_own, down_own = lax.optimization_barrier((a_edge, b_edge, up_own, down_own))
        up = beside(jnp.concatenate([a_edge[:, HALO:], b_edge[:, HALO:]]), TILE, True)
        down = beside(jnp.concatenate([a_edge[:, :HALO], b_edge[:, :HALO]]), TILE, False)
        shapes = [f32(*ends)] * 7 + [f32(PRODUCTS, 8, 128)]
        if coef_ext is None:
            *far, part, coef_ext = call(
                first_ends_kernel,
                [edge, a_edge, b_edge, up_own, down_own, up, down, coefs],
                [*shapes, f32(*ext[1:])],
                scratch(2 * HALO),
            )
        else:
            *far, part = call(
                ends_kernel,
                [edge, a_edge, b_edge, up_own, down_own, up, down, coef_ext],
                shapes,
                scratch(2 * HALO),
            )
        phi, n, ln, fb, sn = call(
            ahead_kernel,
            [mid, b_mid, far[0], far[2], coef_ext],
            [f32(*middle)] * 4 + [f32(*middle[1:])],
            [],
        )
        m, lm, q, r, sums = call(
            middle_kernel,
            [mid, a_mid, far[1], phi, n, fb, sn, part, coef_ext],
            [f32(*middle)] * 4 + [table],
            [middle, middle, middle[1:]],
        )
        near = phi, m, n, lm, ln, q, r
        phi, m, n, lm, ln, g, scal, sums = call(
            lambda *refs: second_kernel(tiles, cells, *refs),
            [from_everyone(sums), *far, *near, coef_ext],
            [whole] * 6 + [f32(8, 128), table],
            [ext, *scratch(rows)],
        )
        phi, g, sums = call(
            lambda *refs: third_kernel(cells, *refs),
            [scal, from_everyone(sums), phi, m, n, lm, ln, g, coef_ext],
            [whole, f32(3, own, depth, width), table],
            [ext, ext, *scratch(rows)],
        )
        edge, mid = call(
            lambda *refs: last_kernel(cells, *refs),
            [from_everyone(sums), phi, g],
            [f32(3, 2 * HALO, depth, width), f32(3, own - 2 * HALO, depth, width)],
            [],
        )
    final = jnp.concatenate([edge[:, :HALO], mid, edge[:, HALO:]], axis=1)
    return jnp.swapaxes(final, 1, 2)[None]


def solution(mesh):
    split = Mesh(mesh.devices.reshape(4, 4, 4, 2), IMG_TILE)
    return jax.shard_map(
        body,
        mesh=split,
        in_specs=(P(IMG, None, None, TILE, None), P(None, TILE, None)),
        out_specs=P(IMG, None, None, TILE, None),
        check_vma=False,
    )
```

```python
import jax
import jax.numpy as jnp
from jax import lax
from jax.experimental import pallas as pl
from jax.experimental.pallas import tpu as pltpu
from jax.sharding import Mesh
from jax.sharding import PartitionSpec as P

OUTER = 2
INNER = 3
IMG = ("img_0", "img_1")
TILE = ("tile_0", "tile_1")
IMG_TILE = ("img_0", "img_1", "tile_0", "tile_1")

spring_coef = 20.0
step_scale = 0.25
epsilon = 1e-06

HALO = 2 * INNER
PRODUCTS = 11
SUBLANES = 2
LANES = 2
TILES = range(SUBLANES * LANES)
VMEM_LIMIT = 16 * 1024 * 1024


def tile_of(ref, comp, at, place):
    z, y = divmod(place, LANES)
    return ref[comp, at, z * 8 : z * 8 + 8, y * 128 : y * 128 + 128]


def put(ref, comp, at, place, cells):
    z, y = divmod(place, LANES)
    ref[comp, at, z * 8 : z * 8 + 8, y * 128 : y * 128 + 128] = cells


def flat_of(ref, at, place):
    z, y = divmod(place, LANES)
    return ref[at, z * 8 : z * 8 + 8, y * 128 : y * 128 + 128]


def put_flat(ref, at, place, cells):
    z, y = divmod(place, LANES)
    ref[at, z * 8 : z * 8 + 8, y * 128 : y * 128 + 128] = cells


def vector(ref, at, place):
    return [tile_of(ref, comp, at, place) for comp in range(3)]


def around(line, axis):
    size = line[0].shape[axis]
    where = lax.broadcasted_iota(jnp.int32, line[0].shape, axis)
    first, last = where == 0, where == size - 1
    later = [pltpu.roll(cells, 1, axis) for cells in line]
    earlier = [pltpu.roll(cells, size - 1, axis) for cells in line]
    later, earlier = [0.0, *later], [*earlier, 0.0]
    return [
        jnp.where(first, later[i], later[i + 1]) + jnp.where(last, earlier[i + 1], earlier[i])
        for i in range(len(line))
    ]


def laplace(ref, comp, at):
    cells = [tile_of(ref, comp, at, place) for place in TILES]
    total = [
        tile_of(ref, comp, at - 1, place) + tile_of(ref, comp, at + 1, place)
        for place in TILES
    ]
    for z in range(SUBLANES):
        picked = range(z * LANES, z * LANES + LANES)
        for place, side in zip(picked, around([cells[i] for i in picked], 1)):
            total[place] = total[place] + side
    for y in range(LANES):
        picked = range(y, SUBLANES * LANES, LANES)
        for place, side in zip(picked, around([cells[i] for i in picked], 0)):
            total[place] = total[place] + side
    return cells, total


def dot(left, right):
    return left[0] * right[0] + left[1] * right[1] + left[2] * right[2]


def stiffness(square, coefs):
    plain = (0.5 - 6.0) - square
    return [plain, plain, plain + coefs]


def loop(low, high, body, carry=0):
    count = high - low
    exact = [u for u in (8, 7, 6, 5, 4) if count and count % u == 0]
    unroll = exact[0] if exact else (8 if count >= 20 else 4)
    return lax.fori_loop(low, high, body, carry, unroll=unroll)


def clear_outside(tile, last_tile, refs, own):
    rows = refs[0].shape[1]

    @pl.when(tile == 0)
    def _():
        for ref in refs:
            ref[:, 0:HALO] = jnp.zeros((3, HALO) + ref.shape[2:], jnp.float32)

    @pl.when(tile == last_tile)
    def _():
        for ref in refs:
            ref[:, HALO + own :] = jnp.zeros((3, rows - HALO - own) + ref.shape[2:], jnp.float32)


def residual(ref, lap_ref, out, squares, coef_ref, offset, other_ref=None, sum_ref=None):
    def body(at, carry):
        stiff = []
        for place in TILES:
            cells = vector(ref, at, place)
            square = 0.125 * dot(cells, cells)
            put_flat(squares, at, place, square)
            stiff.append(stiffness(square, flat_of(coef_ref, at + offset, place)))
        for comp in range(3):
            cells, bent = laplace(ref, comp, at)
            for place in TILES:
                put(lap_ref, comp, at, place, bent[place])
                total = bent[place] + stiff[place][comp] * cells[place]
                put(out, comp, at, place, total)
                if sum_ref is not None:
                    total = total + tile_of(other_ref, comp, at, place)
                    put(sum_ref, comp, at, place, total)
        return carry

    loop(1, ref.shape[1] - 1, body)


def block(phi_ref, m_ref, n_ref, q_ref, r_ref, coef_ref, offset, scratch, cuts, clear, sums):
    fa_ref, fb_ref, fs_ref, sm_ref, sn_ref = scratch
    rows = phi_ref.shape[1]

    def fields(at, sums):
        adjoint = [laplace(fs_ref, comp, at)[1] for comp in range(3)]
        for place in TILES:
            phi, m, n = (vector(ref, at, place) for ref in (phi_ref, m_ref, n_ref))
            fa, fb = vector(fa_ref, at, place), vector(fb_ref, at, place)
            square_m, square_n = flat_of(sm_ref, at, place), flat_of(sn_ref, at, place)
            coefs = flat_of(coef_ref, at + offset, place)
            stiff_m, stiff_n = stiffness(square_m, coefs), stiffness(square_n, coefs)
            turn_m, turn_n = 0.25 * dot(m, fa), 0.25 * dot(n, fb)
            gap = square_m - square_n
            rise_m = 0.25 * dot(m, phi) - square_m
            rise_n = square_n - 0.25 * dot(n, phi)
            flat, bent = [], []
            for c in range(3):
                flat.append(phi[c] * gap + m[c] * rise_m + n[c] * rise_n)
                bent.append(
                    0.25
                    * (
                        adjoint[c][place]
                        + (stiff_m[c] * fa[c] + stiff_n[c] * fb[c])
                        - (m[c] * turn_m + n[c] * turn_n)
                    )
                )
                put(q_ref, c, at, place, flat[c])
                put(r_ref, c, at, place, bent[c])
            if sums:
                behind = [2.0 * one - other for one, other in zip(phi, m)]
                ahead = [other - 2.0 * one for one, other in zip(phi, n)]
                pairs = (
                    (behind, behind), (behind, ahead), (ahead, ahead),
                    (flat, behind), (flat, ahead), (bent, behind), (bent, ahead),
                    (flat, flat), (flat, bent), (bent, bent), (fb, fb),
                )
                sums = [total + dot(left, right) for total, (left, right) in zip(sums, pairs)]
        return sums

    def rim(at, carry):
        fields(at, None)
        return carry

    loop(2, cuts[0], rim)
    sums = loop(cuts[0], cuts[1], fields, sums)
    loop(cuts[1], rows - 2, rim)
    clear((q_ref, r_ref))
    return sums


def join(own_ref, beside_refs, phi_ref, sum_refs, low, high, shift):
    def one(at, carry):
        for comp in range(3):
            for place in TILES:
                phi = tile_of(own_ref, comp, at, place)
                if phi_ref is not None:
                    put(phi_ref, comp, at + shift, place, phi)
                for ref, sum_ref in zip(beside_refs, sum_refs):
                    put(sum_ref, comp, at + shift, place, phi + tile_of(ref, comp, at, place))
        return carry

    loop(low, high, one)


def first_ends_kernel(
    where, own_edge, a_edge, b_edge, up_own, down_own, up_ref, down_ref, coef_ref, *refs
):
    own = coef_ref.shape[0]
    coef_out, refs = refs[8], refs[:8] + refs[9:]
    coef_out[0:HALO] = up_own[3]
    coef_out[HALO : HALO + own] = coef_ref[...]
    coef_out[HALO + own :] = down_own[3]
    ends_kernel(
        where, own_edge, a_edge, b_edge, up_own, down_own, up_ref, down_ref, coef_out, *refs
    )


def ends_kernel(
    where, own_edge, a_edge, b_edge, up_own, down_own, up_ref, down_ref, coef_ref,
    phi_ref, m_ref, n_ref, lm_ref, ln_ref, q_ref, r_ref, sums_ref,
    fa_ref, fb_ref, fs_ref, sm_ref, sn_ref
):
    tile, last_tile = where[1], where[2] - 1
    span = 2 * HALO
    fields = (phi_ref, m_ref, n_ref, lm_ref, ln_ref, q_ref, r_ref)
    scratch = (fa_ref, fb_ref, fs_ref, sm_ref, sn_ref)
    halos = [
        (first, ref.at[0:3], ref.at[3:6])
        for first, ref in ((up_own, up_ref), (down_own, down_ref))
    ]
    sums = [jnp.zeros((8, 128), jnp.float32)] * PRODUCTS
    for top in (True, False):
        first = 0 if top else span
        here = [ref.at[:, first : first + span] for ref in fields]
        phi, m, n, lm, ln, q, r = here
        halo = halos[0 if top else 1]
        join(halo[0], halo[1:], phi, (m, n), 0, HALO, 0 if top else HALO)
        if top:
            join(own_edge, (a_edge, b_edge), phi, (m, n), 0, HALO, HALO)
        else:
            join(own_edge, (a_edge, b_edge), phi, (m, n), HALO, span, -HALO)

        def clear(refs, top=top):
            outside = slice(0, HALO) if top else slice(HALO, span)

            @pl.when(tile == (0 if top else last_tile))
            def _():
                for ref in refs:
                    ref[:, outside] = jnp.zeros((3, HALO) + ref.shape[2:], jnp.float32)

        cuts = (HALO, span - 2) if top else (2, HALO)
        offset = 0 if top else coef_ref.shape[0] - span
        residual(m, lm, fa_ref, sm_ref, coef_ref, offset)
        residual(n, ln, fb_ref, sn_ref, coef_ref, offset, fa_ref, fs_ref)
        clear((fa_ref, fb_ref, fs_ref))
        sums = block(phi, m, n, q, r, coef_ref, offset, scratch, cuts, clear, sums)
    for which in range(PRODUCTS):
        sums_ref[which] = sums[which]


def ends_into(ref, end, span):
    rows = ref.shape[1]
    ref[:, 0:4] = end[:, span - 4 : span]
    ref[:, rows - 4 :] = end[:, span : span + 4]


def ahead_kernel(
    where, own_mid, b_mid, phi_end, n_end, coef_ref, phi_ref, n_ref, ln_ref, fb_ref, sn_ref
):
    span = 2 * HALO
    ends_into(phi_ref, phi_end, span)
    ends_into(n_ref, n_end, span)
    join(own_mid, (b_mid,), phi_ref, (n_ref,), 0, phi_ref.shape[1] - 8, 4)
    residual(n_ref, ln_ref, fb_ref, sn_ref, coef_ref, span - 4)


def middle_kernel(
    where, own_mid, a_mid, m_end, phi_ref, n_ref, fb_ref, sn_ref, part_ref, coef_ref,
    m_ref, lm_ref, q_ref, r_ref, sums_ref, fa_ref, fs_ref, sm_ref
):
    span = 2 * HALO
    rows = phi_ref.shape[1]
    ends_into(m_ref, m_end, span)
    join(own_mid, (a_mid,), None, (m_ref,), 0, rows - 8, 4)
    residual(m_ref, lm_ref, fa_ref, sm_ref, coef_ref, span - 4, fb_ref, fs_ref)
    sums = block(
        phi_ref, m_ref, n_ref, q_ref, r_ref, coef_ref, span - 4,
        (fa_ref, fb_ref, fs_ref, sm_ref, sn_ref), (2, rows - 2), lambda refs: None,
        [part_ref[which] for which in range(PRODUCTS)],
    )
    lane = lax.broadcasted_iota(jnp.int32, (1, 128), 1)
    result = jnp.zeros((1, 128), jnp.float32)
    for which in range(PRODUCTS):
        result = jnp.where(lane == which, jnp.sum(sums[which]), result)
    sums_ref[...] = jnp.broadcast_to(result, sums_ref.shape)


def path_scalars(where, all_ref, tiles, cells):
    devices = all_ref.shape[0]
    images = devices // tiles
    table = jnp.sum(all_ref[...].reshape(images, tiles, 128), axis=1)
    lane = lax.broadcasted_iota(jnp.int32, (images, 128), 1)
    image = lax.broadcasted_iota(jnp.int32, (images, 128), 0)
    one = image[:, :1]

    def column(which):
        return jnp.sum(jnp.where(lane == which, table, 0.0), axis=1, keepdims=True)

    live = one < images - 1
    seg = jnp.where(live, jnp.sqrt(column(2) + epsilon), 0.0)
    drv = jnp.where(live, jnp.sqrt(0.25 * column(10) + epsilon), 0.0)
    path_len = jnp.sum(seg, axis=0, keepdims=True)
    tau = path_len / jnp.sum(drv, axis=0, keepdims=True)
    before = jnp.sum(jnp.where(image < lane, seg, 0.0), axis=0, keepdims=True)
    before = jnp.sum(jnp.where(image == lane, before, 0.0), axis=1, keepdims=True)
    target = one.astype(jnp.float32) / (images - 1)
    pull = spring_coef * (before / path_len - target) * (images - 1) / (2.0 * path_len)
    inv = 1.0 / tau
    near, far = inv + pull, pull - inv
    norm = near * near * column(0) + far * far * column(2) + 2.0 * near * far * column(1)
    norm += 2.0 * (near * column(3) + far * column(4))
    norm += 2.0 * tau * (near * column(5) + far * column(6))
    norm += column(7) + tau * (2.0 * column(8) + tau * column(9))
    inner = (one > 0) & (one < images - 1)
    total = jnp.sum(jnp.where(inner, norm, 0.0), axis=0, keepdims=True)
    step = step_scale / jnp.sqrt(total / cells + epsilon)
    mine = jnp.sum(jnp.where(one == where[0], pull, 0.0), axis=0, keepdims=True)
    return tau[0, 0], mine[0, 0], step[0, 0]


def gradients(
    phi_ref, m_ref, n_ref, coef_ref, fa_ref, fb_ref, fs_ref, sm_ref, sn_ref, g_ref, tau, pull, out
):
    inv = 1.0 / tau
    turned = 0.25 * tau

    def grad(at, total):
        adjoint = [laplace(fs_ref, comp, at)[1] for comp in range(3)]
        for place in TILES:
            phi, m, n = (vector(ref, at, place) for ref in (phi_ref, m_ref, n_ref))
            fa, fb = vector(fa_ref, at, place), vector(fb_ref, at, place)
            square_m, square_n = flat_of(sm_ref, at, place), flat_of(sn_ref, at, place)
            coefs = flat_of(coef_ref, at, place)
            stiff_m, stiff_n = stiffness(square_m, coefs), stiffness(square_n, coefs)
            gap = (square_m - square_n) + 4.0 * inv
            lean_m = (
                0.25 * (dot(m, phi) - turned * dot(m, fa)) - square_m - (pull + inv)
            )
            lean_n = (
                square_n - 0.25 * (dot(n, phi) + turned * dot(n, fb)) + (pull - inv)
            )
            cells = [
                phi[c] * gap
                + (m[c] * lean_m + n[c] * lean_n)
                + turned * (adjoint[c][place] + (stiff_m[c] * fa[c] + stiff_n[c] * fb[c]))
                for c in range(3)
            ]
            for c in range(3):
                put(g_ref, c, at - out, place, cells[c])
            total = total + dot(cells, cells)
        return total

    def rim(at, carry):
        grad(at, 0.0)
        return carry

    return rim, grad


def interior(where):
    return jnp.where((where[0] > 0) & (where[0] < where[3] - 1), 1.0, 0.0)


def advance(
    step_ref, scale, old, old_shift, new, coef_ref, scratch, low, high, keep
):
    p_ref, m0_ref, n0_ref, lm0_ref, ln0_ref = old
    phi_ref, m_ref, n_ref, lm_ref, ln_ref = new
    fa_ref, fb_ref, fs_ref, sm_ref, sn_ref = scratch

    def body(at, carry):
        was = at + old_shift
        moves, bends = [], []
        for comp in range(3):
            cells, bent = laplace(step_ref, comp, at)
            if scale is not None:
                cells, bent = [scale * cell for cell in cells], [scale * cell for cell in bent]
            moves.append(cells)
            bends.append(bent)
            for place in TILES:
                put(phi_ref, comp, at, place, tile_of(p_ref, comp, was, place) + cells[place])
        for ref, lap_old, out, lap_new, drive_ref, squares, last in (
            (m0_ref, lm0_ref, m_ref, lm_ref, fa_ref, sm_ref, False),
            (n0_ref, ln0_ref, n_ref, ln_ref, fb_ref, sn_ref, True),
        ):
            for place in TILES:
                cells = [tile_of(ref, comp, was, place) + moves[comp][place] for comp in range(3)]
                square = 0.125 * dot(cells, cells)
                put_flat(squares, at, place, square)
                stiff = stiffness(square, flat_of(coef_ref, at, place))
                for comp in range(3):
                    put(out, comp, at, place, cells[comp])
                    bent = tile_of(lap_old, comp, was, place) + bends[comp][place]
                    if keep:
                        put(lap_new, comp, at, place, bent)
                    total = bent + stiff[comp] * cells[comp]
                    put(drive_ref, comp, at, place, total)
                    if last:
                        total = total + tile_of(fa_ref, comp, at, place)
                        put(fs_ref, comp, at, place, total)
        return carry

    loop(low, high, body)


def second_kernel(tiles, cells, where, all_ref, *refs):
    ends, mids, refs = refs[:7], refs[7:14], refs[14:]
    coef_ref, phi_ref, m_ref, n_ref, lm_ref, ln_ref, g_ref, scal_ref, sums_ref, d_ref = refs[:10]
    scratch = refs[10:]
    rows = phi_ref.shape[1]
    own = rows - 2 * HALO
    span = 2 * HALO
    tile, last_tile = where[1], where[2] - 1
    tau, pull, step = path_scalars(where, all_ref, tiles, cells)
    live = interior(where)
    step = step * live
    inv = 1.0 / tau
    first = lax.broadcasted_iota(jnp.int32, scal_ref.shape, 0) == 0
    scal_ref[...] = jnp.where(first, tau, pull)
    from_p, from_m, from_n = -4.0 * step * inv, step * (inv + pull), step * (inv - pull)
    bend = step * tau
    regions = (
        (ends, 2, span - 2, 0),
        (mids, span - 2, rows - span + 2, 4 - span),
        (ends, rows - span + 2, rows - 2, 2 * span - rows),
    )
    for here, low, high, shift in regions:

        def direction(at, carry, here=here, shift=shift):
            was = at + shift
            for comp in range(3):
                for place in TILES:
                    p, m, n, q, r = (
                        tile_of(here[i], comp, was, place) for i in (0, 1, 2, 5, 6)
                    )
                    move = (from_p * p + from_m * m) + (from_n * n - step * q) - bend * r
                    put(d_ref, comp, at, place, move)
            return carry

        loop(low, high, direction)
    new = (phi_ref, m_ref, n_ref, lm_ref, ln_ref)
    for here, low, high, shift in regions:
        low, high = max(low, 3), min(high, rows - 3)
        advance(d_ref, None, here[:5], shift, new, coef_ref, scratch, low, high, True)
    fa_ref, fb_ref, fs_ref, sm_ref, sn_ref = scratch
    clear_outside(tile, last_tile, (fa_ref, fb_ref, fs_ref), own)
    rim, inside = gradients(
        phi_ref, m_ref, n_ref, coef_ref, fa_ref, fb_ref, fs_ref, sm_ref, sn_ref, g_ref, tau, pull, 0
    )
    loop(4, HALO, rim)
    total = loop(HALO, HALO + own, inside, jnp.zeros((8, 128), jnp.float32))
    loop(HALO + own, rows - 4, rim)
    clear_outside(tile, last_tile, (g_ref,), own)
    sums = jnp.sum(total, axis=0, keepdims=True) * live
    sums_ref[...] = jnp.broadcast_to(sums, sums_ref.shape)


def step_of(all_ref, cells):
    return step_scale / jnp.sqrt(jnp.sum(all_ref[...]) / cells + epsilon)


def third_kernel(
    cells, where, scal_ref, all_ref, p_ref, m0_ref, n0_ref, lm0_ref, ln0_ref, h_ref, coef_ref,
    phi_ref, g_ref, sums_ref, m_ref, n_ref, fa_ref, fb_ref, fs_ref, sm_ref, sn_ref
):
    rows = p_ref.shape[1]
    own = rows - 2 * HALO
    tile, last_tile = where[1], where[2] - 1
    live = interior(where)
    kept = scal_ref[...]
    tau, pull = kept[0, 0], kept[1, 0]
    step = step_of(all_ref, cells) * live
    advance(
        h_ref, -step, (p_ref, m0_ref, n0_ref, lm0_ref, ln0_ref), 0,
        (phi_ref, m_ref, n_ref, None, None), coef_ref,
        (fa_ref, fb_ref, fs_ref, sm_ref, sn_ref), HALO - 1, HALO + own + 1, False,
    )
    clear_outside(tile, last_tile, (fa_ref, fb_ref, fs_ref), own)
    _, inside = gradients(
        phi_ref, m_ref, n_ref, coef_ref, fa_ref, fb_ref, fs_ref, sm_ref, sn_ref, g_ref, tau, pull,
        HALO,
    )
    total = loop(HALO, HALO + own, inside, jnp.zeros((8, 128), jnp.float32))
    sums = jnp.sum(total, axis=0, keepdims=True) * live
    sums_ref[...] = jnp.broadcast_to(sums, sums_ref.shape)


def last_kernel(cells, where, all_ref, p_ref, g_ref, edge_ref, mid_ref):
    own = g_ref.shape[1]
    step = step_of(all_ref, cells) * interior(where)
    for ref, low, high, shift in (
        (edge_ref, 0, HALO, 0),
        (mid_ref, HALO, own - HALO, HALO),
        (edge_ref, own - HALO, own, own - 2 * HALO),
    ):

        def move(at, carry, ref=ref, shift=shift):
            for comp in range(3):
                for place in TILES:
                    old = tile_of(p_ref, comp, at + HALO, place)
                    put(ref, comp, at - shift, place, old - step * tile_of(g_ref, comp, at, place))
            return carry

        loop(low, high, move)


def blocks(shape):
    depth, own, width = shape
    return [
        (z, x, slice(z, z + 8), slice(x, x + 8), slice(y, y + 128))
        for z in range(0, depth, 8)
        for x in range(0, own, 8)
        for y in range(0, width, 128)
    ]


def prep_kernel(where, raw_ref, edge_ref, mid_ref):
    own = raw_ref.shape[2]
    for comp in range(3):
        for _, x, zs, xs, ys in blocks(raw_ref.shape[1:]):
            cells = jnp.swapaxes(raw_ref[comp, zs, xs, ys], 0, 1)
            for i in range(8):
                ref, at = edge_ref, x + i
                if HALO <= at < own - HALO:
                    ref, at = mid_ref, at - HALO
                elif at >= own - HALO:
                    at = at - (own - 2 * HALO)
                ref[comp, at, zs, ys] = cells[i]


def final_kernel(cells, where, all_ref, p_ref, g_ref, out_ref):
    step = step_of(all_ref, cells) * interior(where)
    for comp in range(3):
        for _, x, zs, xs, ys in blocks(out_ref.shape[1:]):
            old = p_ref[comp, HALO + x : HALO + x + 8, zs, ys]
            new = old - step * g_ref[comp, xs, zs, ys]
            out_ref[comp, zs, xs, ys] = jnp.swapaxes(new, 0, 1)


def f32(*shape):
    return jax.ShapeDtypeStruct(shape, jnp.float32)


def position():
    found = []
    for axes in (IMG, TILE):
        index = 0
        for axis in axes:
            index = index * lax.axis_size(axis) + lax.axis_index(axis)
        found.append(index)
    return (*found, lax.axis_size(TILE), lax.axis_size(IMG))


def call(kernel, operands, outs, scratch):
    vmem = pl.BlockSpec(memory_space=pltpu.VMEM)
    return pl.pallas_call(
        lambda *refs: kernel(position(), *refs),
        out_shape=outs,
        in_specs=[vmem] * len(operands),
        out_specs=[vmem] * len(outs),
        scratch_shapes=[pltpu.VMEM(shape, jnp.float32) for shape in scratch],
        compiler_params=pltpu.CompilerParams(vmem_limit_bytes=VMEM_LIMIT),
    )(*operands)


def beside(cells, axis, forward):
    count = lax.axis_size(axis)
    pairs = [(i, i + 1) if forward else (i + 1, i) for i in range(count - 1)]
    return lax.ppermute(cells, axis, pairs)


def from_everyone(rows):
    return lax.all_to_all(rows, IMG_TILE, 0, 0, tiled=True)


def body(spins, aniso):
    _, comps, depth, own, width = spins.shape
    images, tiles = lax.axis_size(IMG), lax.axis_size(TILE)
    devices = images * tiles
    cells = float(images * comps * depth * own * tiles * width)
    rows = own + 2 * HALO
    coefs = jnp.swapaxes(aniso, 0, 1)
    edge, mid = call(
        prep_kernel,
        [spins[0]],
        [f32(3, 2 * HALO, depth, width), f32(3, own - 2 * HALO, depth, width)],
        [],
    )
    ext = (3, rows, depth, width)
    ends, middle = (3, 4 * HALO, depth, width), (3, own - 4, depth, width)
    whole = f32(*ext)
    table = f32(devices, 128)
    coef_ext = None

    def scratch(count):
        return [(3, count, depth, width)] * 3 + [(count, depth, width)] * 2

    for outer in range(OUTER):
        a_edge, b_edge = beside(edge, IMG, True), beside(edge, IMG, False)
        a_mid, b_mid = beside(mid, IMG, True), beside(mid, IMG, False)
        bottom, top = edge[:, HALO:], edge[:, :HALO]
        if coef_ext is None:
            bottom = jnp.concatenate([bottom, coefs[None, own - HALO :]])
            top = jnp.concatenate([top, coefs[None, :HALO]])
        up_own, down_own = beside(bottom, TILE, True), beside(top, TILE, False)
        a_edge, b_edge, up_own, down_own = lax.optimization_barrier((a_edge, b_edge, up_own, down_own))
        up = beside(jnp.concatenate([a_edge[:, HALO:], b_edge[:, HALO:]]), TILE, True)
        down = beside(jnp.concatenate([a_edge[:, :HALO], b_edge[:, :HALO]]), TILE, False)
        shapes = [f32(*ends)] * 7 + [f32(PRODUCTS, 8, 128)]
        if coef_ext is None:
            *far, part, coef_ext = call(
                first_ends_kernel,
                [edge, a_edge, b_edge, up_own, down_own, up, down, coefs],
                [*shapes, f32(*ext[1:])],
                scratch(2 * HALO),
            )
        else:
            *far, part = call(
                ends_kernel,
                [edge, a_edge, b_edge, up_own, down_own, up, down, coef_ext],
                shapes,
                scratch(2 * HALO),
            )
        phi, n, ln, fb, sn = call(
            ahead_kernel,
            [mid, b_mid, far[0], far[2], coef_ext],
            [f32(*middle)] * 4 + [f32(*middle[1:])],
            [],
        )
        m, lm, q, r, sums = call(
            middle_kernel,
            [mid, a_mid, far[1], phi, n, fb, sn, part, coef_ext],
            [f32(*middle)] * 4 + [table],
            [middle, middle, middle[1:]],
        )
        near = phi, m, n, lm, ln, q, r
        phi, m, n, lm, ln, g, scal, sums = call(
            lambda *refs: second_kernel(tiles, cells, *refs),
            [from_everyone(sums), *far, *near, coef_ext],
            [whole] * 6 + [f32(8, 128), table],
            [ext, *scratch(rows)],
        )
        phi, g, sums = call(
            lambda *refs: third_kernel(cells, *refs),
            [scal, from_everyone(sums), phi, m, n, lm, ln, g, coef_ext],
            [whole, f32(3, own, depth, width), table],
            [ext, ext, *scratch(rows)],
        )
        sums = from_everyone(sums)
        if outer == OUTER - 1:
            (path,) = call(
                lambda *refs: final_kernel(cells, *refs), [sums, phi, g], [f32(*spins.shape[1:])], []
            )
            return path[None]
        edge, mid = call(
            lambda *refs: last_kernel(cells, *refs),
            [sums, phi, g],
            [f32(3, 2 * HALO, depth, width), f32(3, own - 2 * HALO, depth, width)],
            [],
        )


def solution(mesh):
    split = Mesh(mesh.devices.reshape(4, 4, 4, 2), IMG_TILE)
    return jax.shard_map(
        body,
        mesh=split,
        in_specs=(P(IMG, None, None, TILE, None), P(None, TILE, None)),
        out_specs=P(IMG, None, None, TILE, None),
        check_vma=False,
    )
```

```python
import jax
import jax.numpy as jnp
from jax import lax
from jax.experimental import pallas as pl
from jax.experimental.pallas import tpu as pltpu
from jax.sharding import Mesh
from jax.sharding import PartitionSpec as P

OUTER = 2
INNER = 3
IMG = ("img_0", "img_1")
TILE = ("tile_0", "tile_1")
IMG_TILE = ("img_0", "img_1", "tile_0", "tile_1")

spring_coef = 20.0
step_scale = 0.25
epsilon = 1e-06

HALO = 2 * INNER
PRODUCTS = 11
SUBLANES = 2
LANES = 2
TILES = range(SUBLANES * LANES)
VMEM_LIMIT = 16 * 1024 * 1024


def tile_of(ref, comp, at, place):
    z, y = divmod(place, LANES)
    return ref[comp, at, z * 8 : z * 8 + 8, y * 128 : y * 128 + 128]


def put(ref, comp, at, place, cells):
    z, y = divmod(place, LANES)
    ref[comp, at, z * 8 : z * 8 + 8, y * 128 : y * 128 + 128] = cells


def flat_of(ref, at, place):
    z, y = divmod(place, LANES)
    return ref[at, z * 8 : z * 8 + 8, y * 128 : y * 128 + 128]


def put_flat(ref, at, place, cells):
    z, y = divmod(place, LANES)
    ref[at, z * 8 : z * 8 + 8, y * 128 : y * 128 + 128] = cells


def vector(ref, at, place):
    return [tile_of(ref, comp, at, place) for comp in range(3)]


def around(line, axis):
    size = line[0].shape[axis]
    where = lax.broadcasted_iota(jnp.int32, line[0].shape, axis)
    first, last = where == 0, where == size - 1
    later = [pltpu.roll(cells, 1, axis) for cells in line]
    earlier = [pltpu.roll(cells, size - 1, axis) for cells in line]
    later, earlier = [0.0, *later], [*earlier, 0.0]
    return [
        jnp.where(first, later[i], later[i + 1]) + jnp.where(last, earlier[i + 1], earlier[i])
        for i in range(len(line))
    ]


def laplace(ref, comp, at):
    cells = [tile_of(ref, comp, at, place) for place in TILES]
    total = [
        tile_of(ref, comp, at - 1, place) + tile_of(ref, comp, at + 1, place)
        for place in TILES
    ]
    for z in range(SUBLANES):
        picked = range(z * LANES, z * LANES + LANES)
        for place, side in zip(picked, around([cells[i] for i in picked], 1)):
            total[place] = total[place] + side
    for y in range(LANES):
        picked = range(y, SUBLANES * LANES, LANES)
        for place, side in zip(picked, around([cells[i] for i in picked], 0)):
            total[place] = total[place] + side
    return cells, total


def dot(left, right):
    return left[0] * right[0] + left[1] * right[1] + left[2] * right[2]


def stiffness(square, coefs):
    plain = (0.5 - 6.0) - square
    return [plain, plain, plain + coefs]


def loop(low, high, body, carry=0):
    count = high - low
    exact = [u for u in (8, 7, 6, 5, 4) if count and count % u == 0]
    unroll = exact[0] if exact else (8 if count >= 20 else 4)
    return lax.fori_loop(low, high, body, carry, unroll=unroll)


def clear_outside(tile, last_tile, refs, own):
    rows = refs[0].shape[1]

    @pl.when(tile == 0)
    def _():
        for ref in refs:
            ref[:, 0:HALO] = jnp.zeros((3, HALO) + ref.shape[2:], jnp.float32)

    @pl.when(tile == last_tile)
    def _():
        for ref in refs:
            ref[:, HALO + own :] = jnp.zeros((3, rows - HALO - own) + ref.shape[2:], jnp.float32)


def residual(ref, lap_ref, out, squares, coef_ref, offset, other_ref=None, sum_ref=None):
    def body(at, carry):
        stiff = []
        for place in TILES:
            cells = vector(ref, at, place)
            square = 0.125 * dot(cells, cells)
            put_flat(squares, at, place, square)
            stiff.append(stiffness(square, flat_of(coef_ref, at + offset, place)))
        for comp in range(3):
            cells, bent = laplace(ref, comp, at)
            for place in TILES:
                put(lap_ref, comp, at, place, bent[place])
                total = bent[place] + stiff[place][comp] * cells[place]
                put(out, comp, at, place, total)
                if sum_ref is not None:
                    total = total + tile_of(other_ref, comp, at, place)
                    put(sum_ref, comp, at, place, total)
        return carry

    loop(1, ref.shape[1] - 1, body)


def block(phi_ref, m_ref, n_ref, q_ref, r_ref, coef_ref, offset, scratch, cuts, clear, sums):
    fa_ref, fb_ref, fs_ref, sm_ref, sn_ref = scratch
    rows = phi_ref.shape[1]

    def fields(at, sums):
        adjoint = [laplace(fs_ref, comp, at)[1] for comp in range(3)]
        for place in TILES:
            phi, m, n = (vector(ref, at, place) for ref in (phi_ref, m_ref, n_ref))
            fa, fb = vector(fa_ref, at, place), vector(fb_ref, at, place)
            square_m, square_n = flat_of(sm_ref, at, place), flat_of(sn_ref, at, place)
            coefs = flat_of(coef_ref, at + offset, place)
            stiff_m, stiff_n = stiffness(square_m, coefs), stiffness(square_n, coefs)
            turn_m, turn_n = 0.25 * dot(m, fa), 0.25 * dot(n, fb)
            gap = square_m - square_n
            rise_m = 0.25 * dot(m, phi) - square_m
            rise_n = square_n - 0.25 * dot(n, phi)
            flat, bent = [], []
            for c in range(3):
                flat.append(phi[c] * gap + m[c] * rise_m + n[c] * rise_n)
                bent.append(
                    0.25
                    * (
                        adjoint[c][place]
                        + (stiff_m[c] * fa[c] + stiff_n[c] * fb[c])
                        - (m[c] * turn_m + n[c] * turn_n)
                    )
                )
                put(q_ref, c, at, place, flat[c])
                put(r_ref, c, at, place, bent[c])
            if sums:
                behind = [2.0 * one - other for one, other in zip(phi, m)]
                ahead = [other - 2.0 * one for one, other in zip(phi, n)]
                pairs = (
                    (behind, behind), (behind, ahead), (ahead, ahead),
                    (flat, behind), (flat, ahead), (bent, behind), (bent, ahead),
                    (flat, flat), (flat, bent), (bent, bent), (fb, fb),
                )
                sums = [total + dot(left, right) for total, (left, right) in zip(sums, pairs)]
        return sums

    def rim(at, carry):
        fields(at, None)
        return carry

    loop(2, cuts[0], rim)
    sums = loop(cuts[0], cuts[1], fields, sums)
    loop(cuts[1], rows - 2, rim)
    clear((q_ref, r_ref))
    return sums


def join(own_ref, beside_refs, phi_ref, sum_refs, low, high, shift):
    def one(at, carry):
        for comp in range(3):
            for place in TILES:
                phi = tile_of(own_ref, comp, at, place)
                if phi_ref is not None:
                    put(phi_ref, comp, at + shift, place, phi)
                for ref, sum_ref in zip(beside_refs, sum_refs):
                    put(sum_ref, comp, at + shift, place, phi + tile_of(ref, comp, at, place))
        return carry

    loop(low, high, one)


def first_ends_kernel(
    where, own_edge, a_edge, b_edge, up_own, down_own, up_ref, down_ref, coef_ref, *refs
):
    own = coef_ref.shape[0]
    coef_out, refs = refs[8], refs[:8] + refs[9:]
    coef_out[0:HALO] = up_own[3]
    coef_out[HALO : HALO + own] = coef_ref[...]
    coef_out[HALO + own :] = down_own[3]
    ends_kernel(
        where, own_edge, a_edge, b_edge, up_own, down_own, up_ref, down_ref, coef_out, *refs
    )


def ends_kernel(
    where, own_edge, a_edge, b_edge, up_own, down_own, up_ref, down_ref, coef_ref,
    phi_ref, m_ref, n_ref, lm_ref, ln_ref, q_ref, r_ref, sums_ref,
    fa_ref, fb_ref, fs_ref, sm_ref, sn_ref
):
    tile, last_tile = where[1], where[2] - 1
    span = 2 * HALO
    fields = (phi_ref, m_ref, n_ref, lm_ref, ln_ref, q_ref, r_ref)
    scratch = (fa_ref, fb_ref, fs_ref, sm_ref, sn_ref)
    halos = [
        (first, ref.at[0:3], ref.at[3:6])
        for first, ref in ((up_own, up_ref), (down_own, down_ref))
    ]
    sums = [jnp.zeros((8, 128), jnp.float32)] * PRODUCTS
    for top in (True, False):
        first = 0 if top else span
        here = [ref.at[:, first : first + span] for ref in fields]
        phi, m, n, lm, ln, q, r = here
        halo = halos[0 if top else 1]
        join(halo[0], halo[1:], phi, (m, n), 0, HALO, 0 if top else HALO)
        if top:
            join(own_edge, (a_edge, b_edge), phi, (m, n), 0, HALO, HALO)
        else:
            join(own_edge, (a_edge, b_edge), phi, (m, n), HALO, span, -HALO)

        def clear(refs, top=top):
            outside = slice(0, HALO) if top else slice(HALO, span)

            @pl.when(tile == (0 if top else last_tile))
            def _():
                for ref in refs:
                    ref[:, outside] = jnp.zeros((3, HALO) + ref.shape[2:], jnp.float32)

        cuts = (HALO, span - 2) if top else (2, HALO)
        offset = 0 if top else coef_ref.shape[0] - span
        residual(m, lm, fa_ref, sm_ref, coef_ref, offset)
        residual(n, ln, fb_ref, sn_ref, coef_ref, offset, fa_ref, fs_ref)
        clear((fa_ref, fb_ref, fs_ref))
        sums = block(phi, m, n, q, r, coef_ref, offset, scratch, cuts, clear, sums)
    for which in range(PRODUCTS):
        sums_ref[which] = sums[which]


def ends_into(ref, end, span):
    rows = ref.shape[1]
    ref[:, 0:4] = end[:, span - 4 : span]
    ref[:, rows - 4 :] = end[:, span : span + 4]


def ahead_kernel(
    where, own_mid, b_mid, phi_end, n_end, coef_ref, phi_ref, n_ref, ln_ref, fb_ref, sn_ref
):
    span = 2 * HALO
    ends_into(phi_ref, phi_end, span)
    ends_into(n_ref, n_end, span)
    join(own_mid, (b_mid,), phi_ref, (n_ref,), 0, phi_ref.shape[1] - 8, 4)
    residual(n_ref, ln_ref, fb_ref, sn_ref, coef_ref, span - 4)


def middle_kernel(
    where, own_mid, a_mid, m_end, phi_ref, n_ref, fb_ref, sn_ref, part_ref, coef_ref,
    m_ref, lm_ref, q_ref, r_ref, sums_ref, fa_ref, fs_ref, sm_ref
):
    span = 2 * HALO
    rows = phi_ref.shape[1]
    ends_into(m_ref, m_end, span)
    join(own_mid, (a_mid,), None, (m_ref,), 0, rows - 8, 4)
    residual(m_ref, lm_ref, fa_ref, sm_ref, coef_ref, span - 4, fb_ref, fs_ref)
    sums = block(
        phi_ref, m_ref, n_ref, q_ref, r_ref, coef_ref, span - 4,
        (fa_ref, fb_ref, fs_ref, sm_ref, sn_ref), (2, rows - 2), lambda refs: None,
        [part_ref[which] for which in range(PRODUCTS)],
    )
    lane = lax.broadcasted_iota(jnp.int32, (1, 128), 1)
    result = jnp.zeros((1, 128), jnp.float32)
    for which in range(PRODUCTS):
        result = jnp.where(lane == which, jnp.sum(sums[which]), result)
    sums_ref[...] = jnp.broadcast_to(result, sums_ref.shape)


def path_scalars(where, all_ref, tiles, cells):
    devices = all_ref.shape[0]
    images = devices // tiles
    table = jnp.sum(all_ref[...].reshape(images, tiles, 128), axis=1)
    lane = lax.broadcasted_iota(jnp.int32, (images, 128), 1)
    image = lax.broadcasted_iota(jnp.int32, (images, 128), 0)
    one = image[:, :1]

    def column(which):
        return jnp.sum(jnp.where(lane == which, table, 0.0), axis=1, keepdims=True)

    live = one < images - 1
    seg = jnp.where(live, jnp.sqrt(column(2) + epsilon), 0.0)
    drv = jnp.where(live, jnp.sqrt(0.25 * column(10) + epsilon), 0.0)
    path_len = jnp.sum(seg, axis=0, keepdims=True)
    tau = path_len / jnp.sum(drv, axis=0, keepdims=True)
    before = jnp.sum(jnp.where(image < lane, seg, 0.0), axis=0, keepdims=True)
    before = jnp.sum(jnp.where(image == lane, before, 0.0), axis=1, keepdims=True)
    target = one.astype(jnp.float32) / (images - 1)
    pull = spring_coef * (before / path_len - target) * (images - 1) / (2.0 * path_len)
    inv = 1.0 / tau
    near, far = inv + pull, pull - inv
    norm = near * near * column(0) + far * far * column(2) + 2.0 * near * far * column(1)
    norm += 2.0 * (near * column(3) + far * column(4))
    norm += 2.0 * tau * (near * column(5) + far * column(6))
    norm += column(7) + tau * (2.0 * column(8) + tau * column(9))
    inner = (one > 0) & (one < images - 1)
    total = jnp.sum(jnp.where(inner, norm, 0.0), axis=0, keepdims=True)
    step = step_scale / jnp.sqrt(total / cells + epsilon)
    mine = jnp.sum(jnp.where(one == where[0], pull, 0.0), axis=0, keepdims=True)
    return tau[0, 0], mine[0, 0], step[0, 0]


def gradients(
    phi_ref, m_ref, n_ref, coef_ref, fa_ref, fb_ref, fs_ref, sm_ref, sn_ref, g_ref, tau, pull, out
):
    inv = 1.0 / tau
    turned = 0.25 * tau

    def grad(at, total):
        adjoint = [laplace(fs_ref, comp, at)[1] for comp in range(3)]
        for place in TILES:
            phi, m, n = (vector(ref, at, place) for ref in (phi_ref, m_ref, n_ref))
            fa, fb = vector(fa_ref, at, place), vector(fb_ref, at, place)
            square_m, square_n = flat_of(sm_ref, at, place), flat_of(sn_ref, at, place)
            coefs = flat_of(coef_ref, at, place)
            stiff_m, stiff_n = stiffness(square_m, coefs), stiffness(square_n, coefs)
            gap = (square_m - square_n) + 4.0 * inv
            lean_m = (
                0.25 * (dot(m, phi) - turned * dot(m, fa)) - square_m - (pull + inv)
            )
            lean_n = (
                square_n - 0.25 * (dot(n, phi) + turned * dot(n, fb)) + (pull - inv)
            )
            cells = [
                phi[c] * gap
                + (m[c] * lean_m + n[c] * lean_n)
                + turned * (adjoint[c][place] + (stiff_m[c] * fa[c] + stiff_n[c] * fb[c]))
                for c in range(3)
            ]
            for c in range(3):
                put(g_ref, c, at - out, place, cells[c])
            total = total + dot(cells, cells)
        return total

    def rim(at, carry):
        grad(at, 0.0)
        return carry

    return rim, grad


def interior(where):
    return jnp.where((where[0] > 0) & (where[0] < where[3] - 1), 1.0, 0.0)


def advance(
    step_ref, scale, old, old_shift, new, coef_ref, scratch, low, high, keep
):
    p_ref, m0_ref, n0_ref, lm0_ref, ln0_ref = old
    phi_ref, m_ref, n_ref, lm_ref, ln_ref = new
    fa_ref, fb_ref, fs_ref, sm_ref, sn_ref = scratch

    def body(at, carry):
        was = at + old_shift
        moves, bends = [], []
        for comp in range(3):
            cells, bent = laplace(step_ref, comp, at)
            if scale is not None:
                cells, bent = [scale * cell for cell in cells], [scale * cell for cell in bent]
            moves.append(cells)
            bends.append(bent)
            for place in TILES:
                put(phi_ref, comp, at, place, tile_of(p_ref, comp, was, place) + cells[place])
        for ref, lap_old, out, lap_new, drive_ref, squares, last in (
            (m0_ref, lm0_ref, m_ref, lm_ref, fa_ref, sm_ref, False),
            (n0_ref, ln0_ref, n_ref, ln_ref, fb_ref, sn_ref, True),
        ):
            for place in TILES:
                cells = [tile_of(ref, comp, was, place) + moves[comp][place] for comp in range(3)]
                square = 0.125 * dot(cells, cells)
                put_flat(squares, at, place, square)
                stiff = stiffness(square, flat_of(coef_ref, at, place))
                for comp in range(3):
                    put(out, comp, at, place, cells[comp])
                    bent = tile_of(lap_old, comp, was, place) + bends[comp][place]
                    if keep:
                        put(lap_new, comp, at, place, bent)
                    total = bent + stiff[comp] * cells[comp]
                    put(drive_ref, comp, at, place, total)
                    if last:
                        total = total + tile_of(fa_ref, comp, at, place)
                        put(fs_ref, comp, at, place, total)
        return carry

    loop(low, high, body)


def second_kernel(tiles, cells, where, all_ref, *refs):
    ends, mids, refs = refs[:7], refs[7:14], refs[14:]
    coef_ref, phi_ref, m_ref, n_ref, lm_ref, ln_ref, g_ref, scal_ref, sums_ref, d_ref = refs[:10]
    scratch = refs[10:]
    rows = phi_ref.shape[1]
    own = rows - 2 * HALO
    span = 2 * HALO
    tile, last_tile = where[1], where[2] - 1
    tau, pull, step = path_scalars(where, all_ref, tiles, cells)
    live = interior(where)
    step = step * live
    inv = 1.0 / tau
    first = lax.broadcasted_iota(jnp.int32, scal_ref.shape, 0) == 0
    scal_ref[...] = jnp.where(first, tau, pull)
    from_p, from_m, from_n = -4.0 * step * inv, step * (inv + pull), step * (inv - pull)
    bend = step * tau
    regions = (
        (ends, 2, span - 2, 0),
        (mids, span - 2, rows - span + 2, 4 - span),
        (ends, rows - span + 2, rows - 2, 2 * span - rows),
    )
    for here, low, high, shift in regions:

        def direction(at, carry, here=here, shift=shift):
            was = at + shift
            for comp in range(3):
                for place in TILES:
                    p, m, n, q, r = (
                        tile_of(here[i], comp, was, place) for i in (0, 1, 2, 5, 6)
                    )
                    move = (from_p * p + from_m * m) + (from_n * n - step * q) - bend * r
                    put(d_ref, comp, at, place, move)
            return carry

        loop(low, high, direction)
    new = (phi_ref, m_ref, n_ref, lm_ref, ln_ref)
    for here, low, high, shift in regions:
        low, high = max(low, 3), min(high, rows - 3)
        advance(d_ref, None, here[:5], shift, new, coef_ref, scratch, low, high, True)
    fa_ref, fb_ref, fs_ref, sm_ref, sn_ref = scratch
    clear_outside(tile, last_tile, (fa_ref, fb_ref, fs_ref), own)
    rim, inside = gradients(
        phi_ref, m_ref, n_ref, coef_ref, fa_ref, fb_ref, fs_ref, sm_ref, sn_ref, g_ref, tau, pull, 0
    )
    loop(4, HALO, rim)
    total = loop(HALO, HALO + own, inside, jnp.zeros((8, 128), jnp.float32))
    loop(HALO + own, rows - 4, rim)
    clear_outside(tile, last_tile, (g_ref,), own)
    sums = jnp.sum(total, axis=0, keepdims=True) * live
    sums_ref[...] = jnp.broadcast_to(sums, sums_ref.shape)


def step_of(all_ref, cells):
    return step_scale / jnp.sqrt(jnp.sum(all_ref[...]) / cells + epsilon)


def third_kernel(
    cells, where, scal_ref, all_ref, p_ref, m0_ref, n0_ref, lm0_ref, ln0_ref, h_ref, coef_ref,
    phi_ref, g_ref, sums_ref, m_ref, n_ref, fa_ref, fb_ref, fs_ref, sm_ref, sn_ref
):
    rows = p_ref.shape[1]
    own = rows - 2 * HALO
    tile, last_tile = where[1], where[2] - 1
    live = interior(where)
    kept = scal_ref[...]
    tau, pull = kept[0, 0], kept[1, 0]
    step = step_of(all_ref, cells) * live
    advance(
        h_ref, -step, (p_ref, m0_ref, n0_ref, lm0_ref, ln0_ref), 0,
        (phi_ref, m_ref, n_ref, None, None), coef_ref,
        (fa_ref, fb_ref, fs_ref, sm_ref, sn_ref), HALO - 1, HALO + own + 1, False,
    )
    clear_outside(tile, last_tile, (fa_ref, fb_ref, fs_ref), own)
    _, inside = gradients(
        phi_ref, m_ref, n_ref, coef_ref, fa_ref, fb_ref, fs_ref, sm_ref, sn_ref, g_ref, tau, pull,
        HALO,
    )
    total = loop(HALO, HALO + own, inside, jnp.zeros((8, 128), jnp.float32))
    sums = jnp.sum(total, axis=0, keepdims=True) * live
    sums_ref[...] = jnp.broadcast_to(sums, sums_ref.shape)


def last_kernel(cells, where, all_ref, p_ref, g_ref, edge_ref, mid_ref):
    own = g_ref.shape[1]
    step = step_of(all_ref, cells) * interior(where)
    for ref, low, high, shift in (
        (edge_ref, 0, HALO, 0),
        (mid_ref, HALO, own - HALO, HALO),
        (edge_ref, own - HALO, own, own - 2 * HALO),
    ):

        def move(at, carry, ref=ref, shift=shift):
            for comp in range(3):
                for place in TILES:
                    old = tile_of(p_ref, comp, at + HALO, place)
                    put(ref, comp, at - shift, place, old - step * tile_of(g_ref, comp, at, place))
            return carry

        loop(low, high, move)


def blocks(shape):
    depth, own, width = shape
    return [
        (z, x, slice(z, z + 8), slice(x, x + 8), slice(y, y + 128))
        for z in range(0, depth, 8)
        for x in range(0, own, 8)
        for y in range(0, width, 128)
    ]


def slabs(source, target, sems):
    found = {}
    for comp in range(3):
        for z in range(0, source.shape[1], 8):
            part = comp, pl.ds(z, 8)
            found[comp, z] = pltpu.make_async_copy(
                source.at[part], target.at[part], sems.at[comp, z // 8]
            )
    return found


def prep_kernel(where, raw_ref, edge_ref, mid_ref):
    own = raw_ref.shape[2]
    for comp in range(3):
        for _, x, zs, xs, ys in blocks(raw_ref.shape[1:]):
            cells = jnp.swapaxes(raw_ref[comp, zs, xs, ys], 0, 1)
            for i in range(8):
                ref, at = edge_ref, x + i
                if HALO <= at < own - HALO:
                    ref, at = mid_ref, at - HALO
                elif at >= own - HALO:
                    at = at - (own - 2 * HALO)
                ref[comp, at, zs, ys] = cells[i]


def final_kernel(cells, where, all_ref, p_ref, g_ref, output_ref, out_ref, sems):
    step = step_of(all_ref, cells) * interior(where)
    copies = slabs(out_ref, output_ref, sems)
    own, width = out_ref.shape[2:]
    for comp in range(3):
        for z, x, zs, xs, ys in blocks(out_ref.shape[1:]):
            old = p_ref[comp, HALO + x : HALO + x + 8, zs, ys]
            new = old - step * g_ref[comp, xs, zs, ys]
            out_ref[comp, zs, xs, ys] = jnp.swapaxes(new, 0, 1)
            if x == own - 8 and ys.stop == width:
                copies[comp, z].start()
    for copy in copies.values():
        copy.wait()


def f32(*shape):
    return jax.ShapeDtypeStruct(shape, jnp.float32)


def position():
    found = []
    for axes in (IMG, TILE):
        index = 0
        for axis in axes:
            index = index * lax.axis_size(axis) + lax.axis_index(axis)
        found.append(index)
    return (*found, lax.axis_size(TILE), lax.axis_size(IMG))


def call(kernel, operands, outs, scratch, hbm_out=False):
    vmem, hbm = pl.BlockSpec(memory_space=pltpu.VMEM), pl.BlockSpec(memory_space=pltpu.HBM)
    return pl.pallas_call(
        lambda *refs: kernel(position(), *refs),
        out_shape=outs,
        in_specs=[vmem] * len(operands),
        out_specs=[hbm if hbm_out else vmem] * len(outs),
        scratch_shapes=[
            pltpu.VMEM(shape, jnp.float32) if isinstance(shape, tuple) else shape
            for shape in scratch
        ],
        compiler_params=pltpu.CompilerParams(vmem_limit_bytes=VMEM_LIMIT),
    )(*operands)


def beside(cells, axis, forward):
    count = lax.axis_size(axis)
    pairs = [(i, i + 1) if forward else (i + 1, i) for i in range(count - 1)]
    return lax.ppermute(cells, axis, pairs)


def from_everyone(rows):
    return lax.all_to_all(rows, IMG_TILE, 0, 0, tiled=True)


def body(spins, aniso):
    _, comps, depth, own, width = spins.shape
    images, tiles = lax.axis_size(IMG), lax.axis_size(TILE)
    devices = images * tiles
    cells = float(images * comps * depth * own * tiles * width)
    rows = own + 2 * HALO
    coefs = jnp.swapaxes(aniso, 0, 1)
    moved = [spins.shape[1:], pltpu.SemaphoreType.DMA((3, depth // 8))]
    edge, mid = call(
        prep_kernel,
        [spins[0]],
        [f32(3, 2 * HALO, depth, width), f32(3, own - 2 * HALO, depth, width)],
        [],
    )
    ext = (3, rows, depth, width)
    ends, middle = (3, 4 * HALO, depth, width), (3, own - 4, depth, width)
    whole = f32(*ext)
    table = f32(devices, 128)
    coef_ext = None

    def scratch(count):
        return [(3, count, depth, width)] * 3 + [(count, depth, width)] * 2

    for outer in range(OUTER):
        a_edge, b_edge = beside(edge, IMG, True), beside(edge, IMG, False)
        a_mid, b_mid = beside(mid, IMG, True), beside(mid, IMG, False)
        bottom, top = edge[:, HALO:], edge[:, :HALO]
        if coef_ext is None:
            bottom = jnp.concatenate([bottom, coefs[None, own - HALO :]])
            top = jnp.concatenate([top, coefs[None, :HALO]])
        up_own, down_own = beside(bottom, TILE, True), beside(top, TILE, False)
        a_edge, b_edge, up_own, down_own = lax.optimization_barrier((a_edge, b_edge, up_own, down_own))
        up = beside(jnp.concatenate([a_edge[:, HALO:], b_edge[:, HALO:]]), TILE, True)
        down = beside(jnp.concatenate([a_edge[:, :HALO], b_edge[:, :HALO]]), TILE, False)
        shapes = [f32(*ends)] * 7 + [f32(PRODUCTS, 8, 128)]
        if coef_ext is None:
            *far, part, coef_ext = call(
                first_ends_kernel,
                [edge, a_edge, b_edge, up_own, down_own, up, down, coefs],
                [*shapes, f32(*ext[1:])],
                scratch(2 * HALO),
            )
        else:
            *far, part = call(
                ends_kernel,
                [edge, a_edge, b_edge, up_own, down_own, up, down, coef_ext],
                shapes,
                scratch(2 * HALO),
            )
        phi, n, ln, fb, sn = call(
            ahead_kernel,
            [mid, b_mid, far[0], far[2], coef_ext],
            [f32(*middle)] * 4 + [f32(*middle[1:])],
            [],
        )
        m, lm, q, r, sums = call(
            middle_kernel,
            [mid, a_mid, far[1], phi, n, fb, sn, part, coef_ext],
            [f32(*middle)] * 4 + [table],
            [middle, middle, middle[1:]],
        )
        near = phi, m, n, lm, ln, q, r
        phi, m, n, lm, ln, g, scal, sums = call(
            lambda *refs: second_kernel(tiles, cells, *refs),
            [from_everyone(sums), *far, *near, coef_ext],
            [whole] * 6 + [f32(8, 128), table],
            [ext, *scratch(rows)],
        )
        phi, g, sums = call(
            lambda *refs: third_kernel(cells, *refs),
            [scal, from_everyone(sums), phi, m, n, lm, ln, g, coef_ext],
            [whole, f32(3, own, depth, width), table],
            [ext, ext, *scratch(rows)],
        )
        sums = from_everyone(sums)
        if outer == OUTER - 1:
            (path,) = call(
                lambda *refs: final_kernel(cells, *refs),
                [sums, phi, g],
                [f32(*spins.shape[1:])],
                moved,
                hbm_out=True,
            )
            return path[None]
        edge, mid = call(
            lambda *refs: last_kernel(cells, *refs),
            [sums, phi, g],
            [f32(3, 2 * HALO, depth, width), f32(3, own - 2 * HALO, depth, width)],
            [],
        )


def solution(mesh):
    split = Mesh(mesh.devices.reshape(4, 4, 4, 2), IMG_TILE)
    return jax.shard_map(
        body,
        mesh=split,
        in_specs=(P(IMG, None, None, TILE, None), P(None, TILE, None)),
        out_specs=P(IMG, None, None, TILE, None),
        check_vma=False,
    )
```

```python
import jax
import jax.numpy as jnp
from jax import lax
from jax.experimental import pallas as pl
from jax.experimental.pallas import tpu as pltpu
from jax.sharding import Mesh
from jax.sharding import PartitionSpec as P

OUTER = 2
INNER = 3
IMG = ("img_0", "img_1")
TILE = ("tile_0", "tile_1")
IMG_TILE = ("img_0", "img_1", "tile_0", "tile_1")

spring_coef = 20.0
step_scale = 0.25
epsilon = 1e-06

HALO = 2 * INNER
PRODUCTS = 11
SUBLANES = 2
LANES = 2
TILES = range(SUBLANES * LANES)
VMEM_LIMIT = 16 * 1024 * 1024


def tile_of(ref, comp, at, place):
    z, y = divmod(place, LANES)
    return ref[comp, at, z * 8 : z * 8 + 8, y * 128 : y * 128 + 128]


def put(ref, comp, at, place, cells):
    z, y = divmod(place, LANES)
    ref[comp, at, z * 8 : z * 8 + 8, y * 128 : y * 128 + 128] = cells


def flat_of(ref, at, place):
    z, y = divmod(place, LANES)
    return ref[at, z * 8 : z * 8 + 8, y * 128 : y * 128 + 128]


def put_flat(ref, at, place, cells):
    z, y = divmod(place, LANES)
    ref[at, z * 8 : z * 8 + 8, y * 128 : y * 128 + 128] = cells


def vector(ref, at, place):
    return [tile_of(ref, comp, at, place) for comp in range(3)]


def around(line, axis):
    size = line[0].shape[axis]
    where = lax.broadcasted_iota(jnp.int32, line[0].shape, axis)
    first, last = where == 0, where == size - 1
    later = [pltpu.roll(cells, 1, axis) for cells in line]
    earlier = [pltpu.roll(cells, size - 1, axis) for cells in line]
    later, earlier = [0.0, *later], [*earlier, 0.0]
    return [
        jnp.where(first, later[i], later[i + 1]) + jnp.where(last, earlier[i + 1], earlier[i])
        for i in range(len(line))
    ]


def laplace(ref, comp, at):
    cells = [tile_of(ref, comp, at, place) for place in TILES]
    total = [
        tile_of(ref, comp, at - 1, place) + tile_of(ref, comp, at + 1, place)
        for place in TILES
    ]
    for z in range(SUBLANES):
        picked = range(z * LANES, z * LANES + LANES)
        for place, side in zip(picked, around([cells[i] for i in picked], 1)):
            total[place] = total[place] + side
    for y in range(LANES):
        picked = range(y, SUBLANES * LANES, LANES)
        for place, side in zip(picked, around([cells[i] for i in picked], 0)):
            total[place] = total[place] + side
    return cells, total


def dot(left, right):
    return left[0] * right[0] + left[1] * right[1] + left[2] * right[2]


def stiffness(square, coefs):
    plain = (0.5 - 6.0) - square
    return [plain, plain, plain + coefs]


def loop(low, high, body, carry=0):
    count = high - low
    exact = [u for u in (8, 7, 6, 5, 4) if count and count % u == 0]
    unroll = exact[0] if exact else (8 if count >= 20 else 4)
    return lax.fori_loop(low, high, body, carry, unroll=unroll)


def clear_outside(tile, last_tile, refs, own):
    rows = refs[0].shape[1]

    @pl.when(tile == 0)
    def _():
        for ref in refs:
            ref[:, 0:HALO] = jnp.zeros((3, HALO) + ref.shape[2:], jnp.float32)

    @pl.when(tile == last_tile)
    def _():
        for ref in refs:
            ref[:, HALO + own :] = jnp.zeros((3, rows - HALO - own) + ref.shape[2:], jnp.float32)


def residual(sides, coef_ref, offset):
    def body(at, carry):
        for ref, lap_ref, out, squares, other_ref, sum_ref in sides:
            stiff = []
            for place in TILES:
                cells = vector(ref, at, place)
                square = 0.125 * dot(cells, cells)
                put_flat(squares, at, place, square)
                stiff.append(stiffness(square, flat_of(coef_ref, at + offset, place)))
            for comp in range(3):
                cells, bent = laplace(ref, comp, at)
                for place in TILES:
                    put(lap_ref, comp, at, place, bent[place])
                    total = bent[place] + stiff[place][comp] * cells[place]
                    put(out, comp, at, place, total)
                    if sum_ref is not None:
                        total = total + tile_of(other_ref, comp, at, place)
                        put(sum_ref, comp, at, place, total)
        return carry

    loop(1, sides[0][0].shape[1] - 1, body)


def block(phi_ref, m_ref, n_ref, q_ref, r_ref, coef_ref, offset, scratch, cuts, clear, sums):
    fa_ref, fb_ref, fs_ref, sm_ref, sn_ref = scratch
    rows = phi_ref.shape[1]

    def fields(at, sums):
        adjoint = [laplace(fs_ref, comp, at)[1] for comp in range(3)]
        for place in TILES:
            phi, m, n = (vector(ref, at, place) for ref in (phi_ref, m_ref, n_ref))
            fa, fb = vector(fa_ref, at, place), vector(fb_ref, at, place)
            square_m, square_n = flat_of(sm_ref, at, place), flat_of(sn_ref, at, place)
            coefs = flat_of(coef_ref, at + offset, place)
            stiff_m, stiff_n = stiffness(square_m, coefs), stiffness(square_n, coefs)
            turn_m, turn_n = 0.25 * dot(m, fa), 0.25 * dot(n, fb)
            gap = square_m - square_n
            rise_m = 0.25 * dot(m, phi) - square_m
            rise_n = square_n - 0.25 * dot(n, phi)
            flat, bent = [], []
            for c in range(3):
                flat.append(phi[c] * gap + m[c] * rise_m + n[c] * rise_n)
                bent.append(
                    0.25
                    * (
                        adjoint[c][place]
                        + (stiff_m[c] * fa[c] + stiff_n[c] * fb[c])
                        - (m[c] * turn_m + n[c] * turn_n)
                    )
                )
                put(q_ref, c, at, place, flat[c])
                put(r_ref, c, at, place, bent[c])
            if sums:
                behind = [2.0 * one - other for one, other in zip(phi, m)]
                ahead = [other - 2.0 * one for one, other in zip(phi, n)]
                pairs = (
                    (behind, behind), (behind, ahead), (ahead, ahead),
                    (flat, behind), (flat, ahead), (bent, behind), (bent, ahead),
                    (flat, flat), (flat, bent), (bent, bent), (fb, fb),
                )
                sums = [total + dot(left, right) for total, (left, right) in zip(sums, pairs)]
        return sums

    def rim(at, carry):
        fields(at, None)
        return carry

    loop(2, cuts[0], rim)
    sums = loop(cuts[0], cuts[1], fields, sums)
    loop(cuts[1], rows - 2, rim)
    clear((q_ref, r_ref))
    return sums


def join(own_ref, beside_refs, phi_ref, sum_refs, low, high, shift):
    def one(at, carry):
        for comp in range(3):
            for place in TILES:
                phi = tile_of(own_ref, comp, at, place)
                if phi_ref is not None:
                    put(phi_ref, comp, at + shift, place, phi)
                for ref, sum_ref in zip(beside_refs, sum_refs):
                    put(sum_ref, comp, at + shift, place, phi + tile_of(ref, comp, at, place))
        return carry

    loop(low, high, one)


def first_ends_kernel(
    where, own_edge, a_edge, b_edge, up_own, down_own, up_ref, down_ref, coef_ref, *refs
):
    own = coef_ref.shape[0]
    coef_out, refs = refs[8], refs[:8] + refs[9:]
    coef_out[0:HALO] = up_own[3]
    coef_out[HALO : HALO + own] = coef_ref[...]
    coef_out[HALO + own :] = down_own[3]
    ends_kernel(
        where, own_edge, a_edge, b_edge, up_own, down_own, up_ref, down_ref, coef_out, *refs
    )


def ends_kernel(
    where, own_edge, a_edge, b_edge, up_own, down_own, up_ref, down_ref, coef_ref,
    phi_ref, m_ref, n_ref, lm_ref, ln_ref, q_ref, r_ref, sums_ref,
    fa_ref, fb_ref, fs_ref, sm_ref, sn_ref
):
    tile, last_tile = where[1], where[2] - 1
    span = 2 * HALO
    fields = (phi_ref, m_ref, n_ref, lm_ref, ln_ref, q_ref, r_ref)
    scratch = (fa_ref, fb_ref, fs_ref, sm_ref, sn_ref)
    halos = [
        (first, ref.at[0:3], ref.at[3:6])
        for first, ref in ((up_own, up_ref), (down_own, down_ref))
    ]
    sums = [jnp.zeros((8, 128), jnp.float32)] * PRODUCTS
    for top in (True, False):
        first = 0 if top else span
        here = [ref.at[:, first : first + span] for ref in fields]
        phi, m, n, lm, ln, q, r = here
        halo = halos[0 if top else 1]
        join(halo[0], halo[1:], phi, (m, n), 0, HALO, 0 if top else HALO)
        if top:
            join(own_edge, (a_edge, b_edge), phi, (m, n), 0, HALO, HALO)
        else:
            join(own_edge, (a_edge, b_edge), phi, (m, n), HALO, span, -HALO)

        def clear(refs, top=top):
            outside = slice(0, HALO) if top else slice(HALO, span)

            @pl.when(tile == (0 if top else last_tile))
            def _():
                for ref in refs:
                    ref[:, outside] = jnp.zeros((3, HALO) + ref.shape[2:], jnp.float32)

        cuts = (HALO, span - 2) if top else (2, HALO)
        offset = 0 if top else coef_ref.shape[0] - span
        residual(
            [
                (m, lm, fa_ref, sm_ref, None, None),
                (n, ln, fb_ref, sn_ref, fa_ref, fs_ref),
            ],
            coef_ref,
            offset,
        )
        clear((fa_ref, fb_ref, fs_ref))
        sums = block(phi, m, n, q, r, coef_ref, offset, scratch, cuts, clear, sums)
    for which in range(PRODUCTS):
        sums_ref[which] = sums[which]


def ends_into(ref, end, span):
    rows = ref.shape[1]
    ref[:, 0:4] = end[:, span - 4 : span]
    ref[:, rows - 4 :] = end[:, span : span + 4]


def ahead_kernel(
    where, own_mid, b_mid, phi_end, n_end, coef_ref, phi_ref, n_ref, ln_ref, fb_ref, sn_ref
):
    span = 2 * HALO
    ends_into(phi_ref, phi_end, span)
    ends_into(n_ref, n_end, span)
    join(own_mid, (b_mid,), phi_ref, (n_ref,), 0, phi_ref.shape[1] - 8, 4)
    residual([(n_ref, ln_ref, fb_ref, sn_ref, None, None)], coef_ref, span - 4)


def middle_kernel(
    where, own_mid, a_mid, m_end, phi_ref, n_ref, fb_ref, sn_ref, part_ref, coef_ref,
    m_ref, lm_ref, q_ref, r_ref, sums_ref, fa_ref, fs_ref, sm_ref
):
    span = 2 * HALO
    rows = phi_ref.shape[1]
    ends_into(m_ref, m_end, span)
    join(own_mid, (a_mid,), None, (m_ref,), 0, rows - 8, 4)
    residual([(m_ref, lm_ref, fa_ref, sm_ref, fb_ref, fs_ref)], coef_ref, span - 4)
    sums = block(
        phi_ref, m_ref, n_ref, q_ref, r_ref, coef_ref, span - 4,
        (fa_ref, fb_ref, fs_ref, sm_ref, sn_ref), (2, rows - 2), lambda refs: None,
        [part_ref[which] for which in range(PRODUCTS)],
    )
    lane = lax.broadcasted_iota(jnp.int32, (1, 128), 1)
    result = jnp.zeros((1, 128), jnp.float32)
    for which in range(PRODUCTS):
        result = jnp.where(lane == which, jnp.sum(sums[which]), result)
    sums_ref[...] = jnp.broadcast_to(result, sums_ref.shape)


def path_scalars(where, all_ref, tiles, cells):
    devices = all_ref.shape[0]
    images = devices // tiles
    table = jnp.sum(all_ref[...].reshape(images, tiles, 128), axis=1)
    lane = lax.broadcasted_iota(jnp.int32, (images, 128), 1)
    image = lax.broadcasted_iota(jnp.int32, (images, 128), 0)
    one = image[:, :1]

    def column(which):
        return jnp.sum(jnp.where(lane == which, table, 0.0), axis=1, keepdims=True)

    live = one < images - 1
    seg = jnp.where(live, jnp.sqrt(column(2) + epsilon), 0.0)
    drv = jnp.where(live, jnp.sqrt(0.25 * column(10) + epsilon), 0.0)
    path_len = jnp.sum(seg, axis=0, keepdims=True)
    tau = path_len / jnp.sum(drv, axis=0, keepdims=True)
    before = jnp.sum(jnp.where(image < lane, seg, 0.0), axis=0, keepdims=True)
    before = jnp.sum(jnp.where(image == lane, before, 0.0), axis=1, keepdims=True)
    target = one.astype(jnp.float32) / (images - 1)
    pull = spring_coef * (before / path_len - target) * (images - 1) / (2.0 * path_len)
    inv = 1.0 / tau
    near, far = inv + pull, pull - inv
    norm = near * near * column(0) + far * far * column(2) + 2.0 * near * far * column(1)
    norm += 2.0 * (near * column(3) + far * column(4))
    norm += 2.0 * tau * (near * column(5) + far * column(6))
    norm += column(7) + tau * (2.0 * column(8) + tau * column(9))
    inner = (one > 0) & (one < images - 1)
    total = jnp.sum(jnp.where(inner, norm, 0.0), axis=0, keepdims=True)
    step = step_scale / jnp.sqrt(total / cells + epsilon)
    mine = jnp.sum(jnp.where(one == where[0], pull, 0.0), axis=0, keepdims=True)
    return tau[0, 0], mine[0, 0], step[0, 0]


def gradients(
    phi_ref, m_ref, n_ref, coef_ref, fa_ref, fb_ref, fs_ref, sm_ref, sn_ref, g_ref, tau, pull, out
):
    inv = 1.0 / tau
    turned = 0.25 * tau

    def grad(at, total):
        adjoint = [laplace(fs_ref, comp, at)[1] for comp in range(3)]
        for place in TILES:
            phi, m, n = (vector(ref, at, place) for ref in (phi_ref, m_ref, n_ref))
            fa, fb = vector(fa_ref, at, place), vector(fb_ref, at, place)
            square_m, square_n = flat_of(sm_ref, at, place), flat_of(sn_ref, at, place)
            coefs = flat_of(coef_ref, at, place)
            stiff_m, stiff_n = stiffness(square_m, coefs), stiffness(square_n, coefs)
            gap = (square_m - square_n) + 4.0 * inv
            lean_m = (
                0.25 * (dot(m, phi) - turned * dot(m, fa)) - square_m - (pull + inv)
            )
            lean_n = (
                square_n - 0.25 * (dot(n, phi) + turned * dot(n, fb)) + (pull - inv)
            )
            cells = [
                phi[c] * gap
                + (m[c] * lean_m + n[c] * lean_n)
                + turned * (adjoint[c][place] + (stiff_m[c] * fa[c] + stiff_n[c] * fb[c]))
                for c in range(3)
            ]
            for c in range(3):
                put(g_ref, c, at - out, place, cells[c])
            total = total + dot(cells, cells)
        return total

    def rim(at, carry):
        grad(at, 0.0)
        return carry

    return rim, grad


def interior(where):
    return jnp.where((where[0] > 0) & (where[0] < where[3] - 1), 1.0, 0.0)


def advance(
    step_ref, scale, old, old_shift, new, coef_ref, scratch, low, high, keep
):
    p_ref, m0_ref, n0_ref, lm0_ref, ln0_ref = old
    phi_ref, m_ref, n_ref, lm_ref, ln_ref = new
    fa_ref, fb_ref, fs_ref, sm_ref, sn_ref = scratch

    def body(at, carry):
        was = at + old_shift
        moves, bends = [], []
        for comp in range(3):
            cells, bent = laplace(step_ref, comp, at)
            if scale is not None:
                cells, bent = [scale * cell for cell in cells], [scale * cell for cell in bent]
            moves.append(cells)
            bends.append(bent)
            for place in TILES:
                put(phi_ref, comp, at, place, tile_of(p_ref, comp, was, place) + cells[place])
        for ref, lap_old, out, lap_new, drive_ref, squares, last in (
            (m0_ref, lm0_ref, m_ref, lm_ref, fa_ref, sm_ref, False),
            (n0_ref, ln0_ref, n_ref, ln_ref, fb_ref, sn_ref, True),
        ):
            for place in TILES:
                cells = [tile_of(ref, comp, was, place) + moves[comp][place] for comp in range(3)]
                square = 0.125 * dot(cells, cells)
                put_flat(squares, at, place, square)
                stiff = stiffness(square, flat_of(coef_ref, at, place))
                for comp in range(3):
                    put(out, comp, at, place, cells[comp])
                    bent = tile_of(lap_old, comp, was, place) + bends[comp][place]
                    if keep:
                        put(lap_new, comp, at, place, bent)
                    total = bent + stiff[comp] * cells[comp]
                    put(drive_ref, comp, at, place, total)
                    if last:
                        total = total + tile_of(fa_ref, comp, at, place)
                        put(fs_ref, comp, at, place, total)
        return carry

    loop(low, high, body)


def second_kernel(tiles, cells, where, all_ref, *refs):
    ends, mids, refs = refs[:7], refs[7:14], refs[14:]
    coef_ref, phi_ref, m_ref, n_ref, lm_ref, ln_ref, g_ref, scal_ref, sums_ref, d_ref = refs[:10]
    scratch = refs[10:]
    rows = phi_ref.shape[1]
    own = rows - 2 * HALO
    span = 2 * HALO
    tile, last_tile = where[1], where[2] - 1
    tau, pull, step = path_scalars(where, all_ref, tiles, cells)
    live = interior(where)
    step = step * live
    inv = 1.0 / tau
    first = lax.broadcasted_iota(jnp.int32, scal_ref.shape, 0) == 0
    scal_ref[...] = jnp.where(first, tau, pull)
    from_p, from_m, from_n = -4.0 * step * inv, step * (inv + pull), step * (inv - pull)
    bend = step * tau
    regions = (
        (ends, 2, span - 2, 0),
        (mids, span - 2, rows - span + 2, 4 - span),
        (ends, rows - span + 2, rows - 2, 2 * span - rows),
    )
    for here, low, high, shift in regions:

        def direction(at, carry, here=here, shift=shift):
            was = at + shift
            for comp in range(3):
                for place in TILES:
                    p, m, n, q, r = (
                        tile_of(here[i], comp, was, place) for i in (0, 1, 2, 5, 6)
                    )
                    move = (from_p * p + from_m * m) + (from_n * n - step * q) - bend * r
                    put(d_ref, comp, at, place, move)
            return carry

        loop(low, high, direction)
    new = (phi_ref, m_ref, n_ref, lm_ref, ln_ref)
    for here, low, high, shift in regions:
        low, high = max(low, 3), min(high, rows - 3)
        advance(d_ref, None, here[:5], shift, new, coef_ref, scratch, low, high, True)
    fa_ref, fb_ref, fs_ref, sm_ref, sn_ref = scratch
    clear_outside(tile, last_tile, (fa_ref, fb_ref, fs_ref), own)
    rim, inside = gradients(
        phi_ref, m_ref, n_ref, coef_ref, fa_ref, fb_ref, fs_ref, sm_ref, sn_ref, g_ref, tau, pull, 0
    )
    loop(4, HALO, rim)
    total = loop(HALO, HALO + own, inside, jnp.zeros((8, 128), jnp.float32))
    loop(HALO + own, rows - 4, rim)
    clear_outside(tile, last_tile, (g_ref,), own)
    sums = jnp.sum(total, axis=0, keepdims=True) * live
    sums_ref[...] = jnp.broadcast_to(sums, sums_ref.shape)


def step_of(all_ref, cells):
    return step_scale / jnp.sqrt(jnp.sum(all_ref[...]) / cells + epsilon)


def third_kernel(
    cells, where, scal_ref, all_ref, p_ref, m0_ref, n0_ref, lm0_ref, ln0_ref, h_ref, coef_ref,
    phi_ref, g_ref, sums_ref, m_ref, n_ref, fa_ref, fb_ref, fs_ref, sm_ref, sn_ref
):
    rows = p_ref.shape[1]
    own = rows - 2 * HALO
    tile, last_tile = where[1], where[2] - 1
    live = interior(where)
    kept = scal_ref[...]
    tau, pull = kept[0, 0], kept[1, 0]
    step = step_of(all_ref, cells) * live
    advance(
        h_ref, -step, (p_ref, m0_ref, n0_ref, lm0_ref, ln0_ref), 0,
        (phi_ref, m_ref, n_ref, None, None), coef_ref,
        (fa_ref, fb_ref, fs_ref, sm_ref, sn_ref), HALO - 1, HALO + own + 1, False,
    )
    clear_outside(tile, last_tile, (fa_ref, fb_ref, fs_ref), own)
    _, inside = gradients(
        phi_ref, m_ref, n_ref, coef_ref, fa_ref, fb_ref, fs_ref, sm_ref, sn_ref, g_ref, tau, pull,
        HALO,
    )
    total = loop(HALO, HALO + own, inside, jnp.zeros((8, 128), jnp.float32))
    sums = jnp.sum(total, axis=0, keepdims=True) * live
    sums_ref[...] = jnp.broadcast_to(sums, sums_ref.shape)


def last_kernel(cells, where, all_ref, p_ref, g_ref, edge_ref, mid_ref):
    own = g_ref.shape[1]
    step = step_of(all_ref, cells) * interior(where)
    for ref, low, high, shift in (
        (edge_ref, 0, HALO, 0),
        (mid_ref, HALO, own - HALO, HALO),
        (edge_ref, own - HALO, own, own - 2 * HALO),
    ):

        def move(at, carry, ref=ref, shift=shift):
            for comp in range(3):
                for place in TILES:
                    old = tile_of(p_ref, comp, at + HALO, place)
                    put(ref, comp, at - shift, place, old - step * tile_of(g_ref, comp, at, place))
            return carry

        loop(low, high, move)


def blocks(shape):
    depth, own, width = shape
    return [
        (z, x, slice(z, z + 8), slice(x, x + 8), slice(y, y + 128))
        for z in range(0, depth, 8)
        for x in range(0, own, 8)
        for y in range(0, width, 128)
    ]


def prep_kernel(where, raw_ref, edge_ref, mid_ref):
    own = raw_ref.shape[2]
    for comp in range(3):
        for _, x, zs, xs, ys in blocks(raw_ref.shape[1:]):
            cells = jnp.swapaxes(raw_ref[comp, zs, xs, ys], 0, 1)
            for i in range(8):
                ref, at = edge_ref, x + i
                if HALO <= at < own - HALO:
                    ref, at = mid_ref, at - HALO
                elif at >= own - HALO:
                    at = at - (own - 2 * HALO)
                ref[comp, at, zs, ys] = cells[i]


def final_kernel(cells, where, all_ref, p_ref, g_ref, out_ref):
    step = step_of(all_ref, cells) * interior(where)
    for comp in range(3):
        for _, x, zs, xs, ys in blocks(out_ref.shape[1:]):
            old = p_ref[comp, HALO + x : HALO + x + 8, zs, ys]
            new = old - step * g_ref[comp, xs, zs, ys]
            out_ref[comp, zs, xs, ys] = jnp.swapaxes(new, 0, 1)


def f32(*shape):
    return jax.ShapeDtypeStruct(shape, jnp.float32)


def position():
    found = []
    for axes in (IMG, TILE):
        index = 0
        for axis in axes:
            index = index * lax.axis_size(axis) + lax.axis_index(axis)
        found.append(index)
    return (*found, lax.axis_size(TILE), lax.axis_size(IMG))


def call(kernel, operands, outs, scratch):
    vmem = pl.BlockSpec(memory_space=pltpu.VMEM)
    return pl.pallas_call(
        lambda *refs: kernel(position(), *refs),
        out_shape=outs,
        in_specs=[vmem] * len(operands),
        out_specs=[vmem] * len(outs),
        scratch_shapes=[pltpu.VMEM(shape, jnp.float32) for shape in scratch],
        compiler_params=pltpu.CompilerParams(vmem_limit_bytes=VMEM_LIMIT),
    )(*operands)


def beside(cells, axis, forward):
    count = lax.axis_size(axis)
    pairs = [(i, i + 1) if forward else (i + 1, i) for i in range(count - 1)]
    return lax.ppermute(cells, axis, pairs)


def from_everyone(rows):
    return lax.all_to_all(rows, IMG_TILE, 0, 0, tiled=True)


def body(spins, aniso):
    _, comps, depth, own, width = spins.shape
    images, tiles = lax.axis_size(IMG), lax.axis_size(TILE)
    devices = images * tiles
    cells = float(images * comps * depth * own * tiles * width)
    rows = own + 2 * HALO
    coefs = jnp.swapaxes(aniso, 0, 1)
    edge, mid = call(
        prep_kernel,
        [spins[0]],
        [f32(3, 2 * HALO, depth, width), f32(3, own - 2 * HALO, depth, width)],
        [],
    )
    ext = (3, rows, depth, width)
    ends, middle = (3, 4 * HALO, depth, width), (3, own - 4, depth, width)
    whole = f32(*ext)
    table = f32(devices, 128)
    coef_ext = None

    def scratch(count):
        return [(3, count, depth, width)] * 3 + [(count, depth, width)] * 2

    for outer in range(OUTER):
        a_edge, b_edge = beside(edge, IMG, True), beside(edge, IMG, False)
        a_mid, b_mid = beside(mid, IMG, True), beside(mid, IMG, False)
        bottom, top = edge[:, HALO:], edge[:, :HALO]
        if coef_ext is None:
            bottom = jnp.concatenate([bottom, coefs[None, own - HALO :]])
            top = jnp.concatenate([top, coefs[None, :HALO]])
        up_own, down_own = beside(bottom, TILE, True), beside(top, TILE, False)
        a_edge, b_edge, up_own, down_own = lax.optimization_barrier((a_edge, b_edge, up_own, down_own))
        up = beside(jnp.concatenate([a_edge[:, HALO:], b_edge[:, HALO:]]), TILE, True)
        down = beside(jnp.concatenate([a_edge[:, :HALO], b_edge[:, :HALO]]), TILE, False)
        shapes = [f32(*ends)] * 7 + [f32(PRODUCTS, 8, 128)]
        if coef_ext is None:
            *far, part, coef_ext = call(
                first_ends_kernel,
                [edge, a_edge, b_edge, up_own, down_own, up, down, coefs],
                [*shapes, f32(*ext[1:])],
                scratch(2 * HALO),
            )
        else:
            *far, part = call(
                ends_kernel,
                [edge, a_edge, b_edge, up_own, down_own, up, down, coef_ext],
                shapes,
                scratch(2 * HALO),
            )
        phi, n, ln, fb, sn = call(
            ahead_kernel,
            [mid, b_mid, far[0], far[2], coef_ext],
            [f32(*middle)] * 4 + [f32(*middle[1:])],
            [],
        )
        m, lm, q, r, sums = call(
            middle_kernel,
            [mid, a_mid, far[1], phi, n, fb, sn, part, coef_ext],
            [f32(*middle)] * 4 + [table],
            [middle, middle, middle[1:]],
        )
        near = phi, m, n, lm, ln, q, r
        phi, m, n, lm, ln, g, scal, sums = call(
            lambda *refs: second_kernel(tiles, cells, *refs),
            [from_everyone(sums), *far, *near, coef_ext],
            [whole] * 6 + [f32(8, 128), table],
            [ext, *scratch(rows)],
        )
        phi, g, sums = call(
            lambda *refs: third_kernel(cells, *refs),
            [scal, from_everyone(sums), phi, m, n, lm, ln, g, coef_ext],
            [whole, f32(3, own, depth, width), table],
            [ext, ext, *scratch(rows)],
        )
        sums = from_everyone(sums)
        if outer == OUTER - 1:
            (path,) = call(
                lambda *refs: final_kernel(cells, *refs), [sums, phi, g], [f32(*spins.shape[1:])], []
            )
            return path[None]
        edge, mid = call(
            lambda *refs: last_kernel(cells, *refs),
            [sums, phi, g],
            [f32(3, 2 * HALO, depth, width), f32(3, own - 2 * HALO, depth, width)],
            [],
        )


def solution(mesh):
    split = Mesh(mesh.devices.reshape(4, 4, 4, 2), IMG_TILE)
    return jax.shard_map(
        body,
        mesh=split,
        in_specs=(P(IMG, None, None, TILE, None), P(None, TILE, None)),
        out_specs=P(IMG, None, None, TILE, None),
        check_vma=False,
    )
```

```python
import jax
import jax.numpy as jnp
from jax import lax
from jax.experimental import pallas as pl
from jax.experimental.pallas import tpu as pltpu
from jax.sharding import Mesh
from jax.sharding import PartitionSpec as P

OUTER = 2
INNER = 3
IMG = ("img_0", "img_1")
TILE = ("tile_0", "tile_1")
IMG_TILE = ("img_0", "img_1", "tile_0", "tile_1")

spring_coef = 20.0
step_scale = 0.25
epsilon = 1e-06

HALO = 2 * INNER
PRODUCTS = 11
SUBLANES = 2
LANES = 2
TILES = range(SUBLANES * LANES)
VMEM_LIMIT = 16 * 1024 * 1024


def tile_of(ref, comp, at, place):
    z, y = divmod(place, LANES)
    return ref[comp, at, z * 8 : z * 8 + 8, y * 128 : y * 128 + 128]


def put(ref, comp, at, place, cells):
    z, y = divmod(place, LANES)
    ref[comp, at, z * 8 : z * 8 + 8, y * 128 : y * 128 + 128] = cells


def flat_of(ref, at, place):
    z, y = divmod(place, LANES)
    return ref[at, z * 8 : z * 8 + 8, y * 128 : y * 128 + 128]


def put_flat(ref, at, place, cells):
    z, y = divmod(place, LANES)
    ref[at, z * 8 : z * 8 + 8, y * 128 : y * 128 + 128] = cells


def vector(ref, at, place):
    return [tile_of(ref, comp, at, place) for comp in range(3)]


def around(line, axis):
    size = line[0].shape[axis]
    where = lax.broadcasted_iota(jnp.int32, line[0].shape, axis)
    first, last = where == 0, where == size - 1
    later = [pltpu.roll(cells, 1, axis) for cells in line]
    earlier = [pltpu.roll(cells, size - 1, axis) for cells in line]
    later, earlier = [0.0, *later], [*earlier, 0.0]
    return [
        jnp.where(first, later[i], later[i + 1]) + jnp.where(last, earlier[i + 1], earlier[i])
        for i in range(len(line))
    ]


def laplace(ref, comp, at):
    cells = [tile_of(ref, comp, at, place) for place in TILES]
    total = [
        tile_of(ref, comp, at - 1, place) + tile_of(ref, comp, at + 1, place)
        for place in TILES
    ]
    for z in range(SUBLANES):
        picked = range(z * LANES, z * LANES + LANES)
        for place, side in zip(picked, around([cells[i] for i in picked], 1)):
            total[place] = total[place] + side
    for y in range(LANES):
        picked = range(y, SUBLANES * LANES, LANES)
        for place, side in zip(picked, around([cells[i] for i in picked], 0)):
            total[place] = total[place] + side
    return cells, total


def dot(left, right):
    return left[0] * right[0] + left[1] * right[1] + left[2] * right[2]


def stiffness(square, coefs):
    plain = (0.5 - 6.0) - square
    return [plain, plain, plain + coefs]


def loop(low, high, body, carry=0):
    count = high - low
    exact = [u for u in (8, 7, 6, 5, 4) if count and count % u == 0]
    unroll = exact[0] if exact else (8 if count >= 20 else 4)
    return lax.fori_loop(low, high, body, carry, unroll=unroll)


def clear_outside(tile, last_tile, refs, own):
    rows = refs[0].shape[1]

    @pl.when(tile == 0)
    def _():
        for ref in refs:
            ref[:, 0:HALO] = jnp.zeros((3, HALO) + ref.shape[2:], jnp.float32)

    @pl.when(tile == last_tile)
    def _():
        for ref in refs:
            ref[:, HALO + own :] = jnp.zeros((3, rows - HALO - own) + ref.shape[2:], jnp.float32)


def residual(sides, coef_ref, offset):
    def body(at, carry):
        for ref, lap_ref, out, squares, other_ref, sum_ref in sides:
            stiff = []
            for place in TILES:
                cells = vector(ref, at, place)
                square = 0.125 * dot(cells, cells)
                put_flat(squares, at, place, square)
                stiff.append(stiffness(square, flat_of(coef_ref, at + offset, place)))
            for comp in range(3):
                cells, bent = laplace(ref, comp, at)
                for place in TILES:
                    put(lap_ref, comp, at, place, bent[place])
                    total = bent[place] + stiff[place][comp] * cells[place]
                    put(out, comp, at, place, total)
                    if sum_ref is not None:
                        total = total + tile_of(other_ref, comp, at, place)
                        put(sum_ref, comp, at, place, total)
        return carry

    loop(1, sides[0][0].shape[1] - 1, body)


def block(phi_ref, m_ref, n_ref, q_ref, r_ref, coef_ref, offset, scratch, cuts, clear, sums):
    fa_ref, fb_ref, fs_ref, sm_ref, sn_ref = scratch
    rows = phi_ref.shape[1]

    def fields(at, sums):
        adjoint = [laplace(fs_ref, comp, at)[1] for comp in range(3)]
        for place in TILES:
            phi, m, n = (vector(ref, at, place) for ref in (phi_ref, m_ref, n_ref))
            fa, fb = vector(fa_ref, at, place), vector(fb_ref, at, place)
            square_m, square_n = flat_of(sm_ref, at, place), flat_of(sn_ref, at, place)
            coefs = flat_of(coef_ref, at + offset, place)
            stiff_m, stiff_n = stiffness(square_m, coefs), stiffness(square_n, coefs)
            turn_m, turn_n = 0.25 * dot(m, fa), 0.25 * dot(n, fb)
            gap = square_m - square_n
            rise_m = 0.25 * dot(m, phi) - square_m
            rise_n = square_n - 0.25 * dot(n, phi)
            flat, bent = [], []
            for c in range(3):
                flat.append(phi[c] * gap + m[c] * rise_m + n[c] * rise_n)
                bent.append(
                    0.25
                    * (
                        adjoint[c][place]
                        + (stiff_m[c] * fa[c] + stiff_n[c] * fb[c])
                        - (m[c] * turn_m + n[c] * turn_n)
                    )
                )
                put(q_ref, c, at, place, flat[c])
                put(r_ref, c, at, place, bent[c])
            if sums:
                behind = [2.0 * one - other for one, other in zip(phi, m)]
                ahead = [other - 2.0 * one for one, other in zip(phi, n)]
                pairs = (
                    (behind, behind), (behind, ahead), (ahead, ahead),
                    (flat, behind), (flat, ahead), (bent, behind), (bent, ahead),
                    (flat, flat), (flat, bent), (bent, bent), (fb, fb),
                )
                sums = [total + dot(left, right) for total, (left, right) in zip(sums, pairs)]
        return sums

    def rim(at, carry):
        fields(at, None)
        return carry

    loop(2, cuts[0], rim)
    sums = loop(cuts[0], cuts[1], fields, sums)
    loop(cuts[1], rows - 2, rim)
    clear((q_ref, r_ref))
    return sums


def join(own_ref, beside_refs, phi_ref, sum_refs, low, high, shift):
    def one(at, carry):
        for comp in range(3):
            for place in TILES:
                phi = tile_of(own_ref, comp, at, place)
                if phi_ref is not None:
                    put(phi_ref, comp, at + shift, place, phi)
                for ref, sum_ref in zip(beside_refs, sum_refs):
                    put(sum_ref, comp, at + shift, place, phi + tile_of(ref, comp, at, place))
        return carry

    loop(low, high, one)


def first_ends_kernel(
    where, own_edge, a_edge, b_edge, up_own, down_own, up_ref, down_ref, coef_ref, *refs
):
    own = coef_ref.shape[0]
    coef_out, refs = refs[8], refs[:8] + refs[9:]
    coef_out[0:HALO] = up_own[3]
    coef_out[HALO : HALO + own] = coef_ref[...]
    coef_out[HALO + own :] = down_own[3]
    ends_kernel(
        where, own_edge, a_edge, b_edge, up_own, down_own, up_ref, down_ref, coef_out, *refs
    )


def ends_kernel(
    where, own_edge, a_edge, b_edge, up_own, down_own, up_ref, down_ref, coef_ref,
    phi_ref, m_ref, n_ref, lm_ref, ln_ref, q_ref, r_ref, sums_ref,
    fa_ref, fb_ref, fs_ref, sm_ref, sn_ref
):
    tile, last_tile = where[1], where[2] - 1
    span = 2 * HALO
    fields = (phi_ref, m_ref, n_ref, lm_ref, ln_ref, q_ref, r_ref)
    scratch = (fa_ref, fb_ref, fs_ref, sm_ref, sn_ref)
    halos = [
        (first, ref.at[0:3], ref.at[3:6])
        for first, ref in ((up_own, up_ref), (down_own, down_ref))
    ]
    sums = [jnp.zeros((8, 128), jnp.float32)] * PRODUCTS
    for top in (True, False):
        first = 0 if top else span
        here = [ref.at[:, first : first + span] for ref in fields]
        phi, m, n, lm, ln, q, r = here
        halo = halos[0 if top else 1]
        join(halo[0], halo[1:], phi, (m, n), 0, HALO, 0 if top else HALO)
        if top:
            join(own_edge, (a_edge, b_edge), phi, (m, n), 0, HALO, HALO)
        else:
            join(own_edge, (a_edge, b_edge), phi, (m, n), HALO, span, -HALO)

        def clear(refs, top=top):
            outside = slice(0, HALO) if top else slice(HALO, span)

            @pl.when(tile == (0 if top else last_tile))
            def _():
                for ref in refs:
                    ref[:, outside] = jnp.zeros((3, HALO) + ref.shape[2:], jnp.float32)

        cuts = (HALO, span - 2) if top else (2, HALO)
        offset = 0 if top else coef_ref.shape[0] - span
        residual(
            [
                (m, lm, fa_ref, sm_ref, None, None),
                (n, ln, fb_ref, sn_ref, fa_ref, fs_ref),
            ],
            coef_ref,
            offset,
        )
        clear((fa_ref, fb_ref, fs_ref))
        sums = block(phi, m, n, q, r, coef_ref, offset, scratch, cuts, clear, sums)
    for which in range(PRODUCTS):
        sums_ref[which] = sums[which]


def ends_into(ref, end, span):
    rows = ref.shape[1]
    ref[:, 0:4] = end[:, span - 4 : span]
    ref[:, rows - 4 :] = end[:, span : span + 4]


def ahead_kernel(
    where, own_mid, b_mid, phi_end, n_end, coef_ref, phi_ref, n_ref, ln_ref, fb_ref, sn_ref
):
    span = 2 * HALO
    ends_into(phi_ref, phi_end, span)
    ends_into(n_ref, n_end, span)
    join(own_mid, (b_mid,), phi_ref, (n_ref,), 0, phi_ref.shape[1] - 8, 4)
    residual([(n_ref, ln_ref, fb_ref, sn_ref, None, None)], coef_ref, span - 4)


def middle_kernel(
    where, own_mid, a_mid, m_end, phi_ref, n_ref, fb_ref, sn_ref, part_ref, coef_ref,
    m_ref, lm_ref, q_ref, r_ref, sums_ref, fa_ref, fs_ref, sm_ref
):
    span = 2 * HALO
    rows = phi_ref.shape[1]
    ends_into(m_ref, m_end, span)
    join(own_mid, (a_mid,), None, (m_ref,), 0, rows - 8, 4)
    residual([(m_ref, lm_ref, fa_ref, sm_ref, fb_ref, fs_ref)], coef_ref, span - 4)
    sums = block(
        phi_ref, m_ref, n_ref, q_ref, r_ref, coef_ref, span - 4,
        (fa_ref, fb_ref, fs_ref, sm_ref, sn_ref), (2, rows - 2), lambda refs: None,
        [part_ref[which] for which in range(PRODUCTS)],
    )
    lane = lax.broadcasted_iota(jnp.int32, (1, 128), 1)
    result = jnp.zeros((1, 128), jnp.float32)
    for which in range(PRODUCTS):
        result = jnp.where(lane == which, jnp.sum(sums[which]), result)
    sums_ref[...] = jnp.broadcast_to(result, sums_ref.shape)


def path_scalars(where, all_ref, tiles, cells):
    devices = all_ref.shape[0]
    images = devices // tiles
    table = jnp.sum(all_ref[...].reshape(images, tiles, 128), axis=1)
    lane = lax.broadcasted_iota(jnp.int32, (images, 128), 1)
    image = lax.broadcasted_iota(jnp.int32, (images, 128), 0)
    one = image[:, :1]

    def column(which):
        return jnp.sum(jnp.where(lane == which, table, 0.0), axis=1, keepdims=True)

    live = one < images - 1
    seg = jnp.where(live, jnp.sqrt(column(2) + epsilon), 0.0)
    drv = jnp.where(live, jnp.sqrt(0.25 * column(10) + epsilon), 0.0)
    path_len = jnp.sum(seg, axis=0, keepdims=True)
    tau = path_len / jnp.sum(drv, axis=0, keepdims=True)
    before = jnp.sum(jnp.where(image < lane, seg, 0.0), axis=0, keepdims=True)
    before = jnp.sum(jnp.where(image == lane, before, 0.0), axis=1, keepdims=True)
    target = one.astype(jnp.float32) / (images - 1)
    pull = spring_coef * (before / path_len - target) * (images - 1) / (2.0 * path_len)
    inv = 1.0 / tau
    near, far = inv + pull, pull - inv
    norm = near * near * column(0) + far * far * column(2) + 2.0 * near * far * column(1)
    norm += 2.0 * (near * column(3) + far * column(4))
    norm += 2.0 * tau * (near * column(5) + far * column(6))
    norm += column(7) + tau * (2.0 * column(8) + tau * column(9))
    inner = (one > 0) & (one < images - 1)
    total = jnp.sum(jnp.where(inner, norm, 0.0), axis=0, keepdims=True)
    step = step_scale / jnp.sqrt(total / cells + epsilon)
    mine = jnp.sum(jnp.where(one == where[0], pull, 0.0), axis=0, keepdims=True)
    return tau[0, 0], mine[0, 0], step[0, 0]


def gradients(
    phi_ref, m_ref, n_ref, coef_ref, fa_ref, fb_ref, fs_ref, sm_ref, sn_ref, g_ref, tau, pull, out
):
    inv = 1.0 / tau
    turned = 0.25 * tau

    def grad(at, total):
        adjoint = [laplace(fs_ref, comp, at)[1] for comp in range(3)]
        for place in TILES:
            phi, m, n = (vector(ref, at, place) for ref in (phi_ref, m_ref, n_ref))
            fa, fb = vector(fa_ref, at, place), vector(fb_ref, at, place)
            square_m, square_n = flat_of(sm_ref, at, place), flat_of(sn_ref, at, place)
            coefs = flat_of(coef_ref, at, place)
            stiff_m, stiff_n = stiffness(square_m, coefs), stiffness(square_n, coefs)
            gap = (square_m - square_n) + 4.0 * inv
            lean_m = (
                0.25 * (dot(m, phi) - turned * dot(m, fa)) - square_m - (pull + inv)
            )
            lean_n = (
                square_n - 0.25 * (dot(n, phi) + turned * dot(n, fb)) + (pull - inv)
            )
            cells = [
                phi[c] * gap
                + (m[c] * lean_m + n[c] * lean_n)
                + turned * (adjoint[c][place] + (stiff_m[c] * fa[c] + stiff_n[c] * fb[c]))
                for c in range(3)
            ]
            for c in range(3):
                put(g_ref, c, at - out, place, cells[c])
            total = total + dot(cells, cells)
        return total

    def rim(at, carry):
        grad(at, 0.0)
        return carry

    return rim, grad


def interior(where):
    return jnp.where((where[0] > 0) & (where[0] < where[3] - 1), 1.0, 0.0)


def advance(
    step_ref, scale, old, old_shift, new, coef_ref, scratch, low, high, keep
):
    p_ref, m0_ref, n0_ref, lm0_ref, ln0_ref = old
    phi_ref, m_ref, n_ref, lm_ref, ln_ref = new
    fa_ref, fb_ref, fs_ref, sm_ref, sn_ref = scratch

    def body(at, carry):
        was = at + old_shift
        moves, bends = [], []
        for comp in range(3):
            cells, bent = laplace(step_ref, comp, at)
            if scale is not None:
                cells, bent = [scale * cell for cell in cells], [scale * cell for cell in bent]
            moves.append(cells)
            bends.append(bent)
            for place in TILES:
                put(phi_ref, comp, at, place, tile_of(p_ref, comp, was, place) + cells[place])
        for ref, lap_old, out, lap_new, drive_ref, squares, last in (
            (m0_ref, lm0_ref, m_ref, lm_ref, fa_ref, sm_ref, False),
            (n0_ref, ln0_ref, n_ref, ln_ref, fb_ref, sn_ref, True),
        ):
            for place in TILES:
                cells = [tile_of(ref, comp, was, place) + moves[comp][place] for comp in range(3)]
                square = 0.125 * dot(cells, cells)
                put_flat(squares, at, place, square)
                stiff = stiffness(square, flat_of(coef_ref, at, place))
                for comp in range(3):
                    put(out, comp, at, place, cells[comp])
                    bent = tile_of(lap_old, comp, was, place) + bends[comp][place]
                    if keep:
                        put(lap_new, comp, at, place, bent)
                    total = bent + stiff[comp] * cells[comp]
                    put(drive_ref, comp, at, place, total)
                    if last:
                        total = total + tile_of(fa_ref, comp, at, place)
                        put(fs_ref, comp, at, place, total)
        return carry

    loop(low, high, body)


def second_kernel(tiles, cells, where, all_ref, *refs):
    ends, mids, refs = refs[:7], refs[7:14], refs[14:]
    coef_ref, phi_ref, m_ref, n_ref, lm_ref, ln_ref, g_ref, scal_ref, sums_ref, d_ref = refs[:10]
    scratch = refs[10:]
    rows = phi_ref.shape[1]
    own = rows - 2 * HALO
    span = 2 * HALO
    tile, last_tile = where[1], where[2] - 1
    tau, pull, step = path_scalars(where, all_ref, tiles, cells)
    live = interior(where)
    step = step * live
    inv = 1.0 / tau
    first = lax.broadcasted_iota(jnp.int32, scal_ref.shape, 0) == 0
    scal_ref[...] = jnp.where(first, tau, pull)
    from_p, from_m, from_n = -4.0 * step * inv, step * (inv + pull), step * (inv - pull)
    bend = step * tau
    regions = (
        (ends, 2, span - 2, 0),
        (mids, span - 2, rows - span + 2, 4 - span),
        (ends, rows - span + 2, rows - 2, 2 * span - rows),
    )
    for here, low, high, shift in regions:

        def direction(at, carry, here=here, shift=shift):
            was = at + shift
            for comp in range(3):
                for place in TILES:
                    p, m, n, q, r = (
                        tile_of(here[i], comp, was, place) for i in (0, 1, 2, 5, 6)
                    )
                    move = (from_p * p + from_m * m) + (from_n * n - step * q) - bend * r
                    put(d_ref, comp, at, place, move)
            return carry

        loop(low, high, direction)
    new = (phi_ref, m_ref, n_ref, lm_ref, ln_ref)
    for here, low, high, shift in regions:
        low, high = max(low, 3), min(high, rows - 3)
        advance(d_ref, None, here[:5], shift, new, coef_ref, scratch, low, high, True)
    fa_ref, fb_ref, fs_ref, sm_ref, sn_ref = scratch
    clear_outside(tile, last_tile, (fa_ref, fb_ref, fs_ref), own)
    rim, inside = gradients(
        phi_ref, m_ref, n_ref, coef_ref, fa_ref, fb_ref, fs_ref, sm_ref, sn_ref, g_ref, tau, pull, 0
    )
    loop(4, HALO, rim)
    total = loop(HALO, HALO + own, inside, jnp.zeros((8, 128), jnp.float32))
    loop(HALO + own, rows - 4, rim)
    clear_outside(tile, last_tile, (g_ref,), own)
    sums = jnp.sum(total, axis=0, keepdims=True) * live
    sums_ref[...] = jnp.broadcast_to(sums, sums_ref.shape)


def step_of(all_ref, cells):
    return step_scale / jnp.sqrt(jnp.sum(all_ref[...]) / cells + epsilon)


def third_kernel(
    cells, where, scal_ref, all_ref, p_ref, m0_ref, n0_ref, lm0_ref, ln0_ref, h_ref, coef_ref,
    phi_ref, g_ref, sums_ref, m_ref, n_ref, fa_ref, fb_ref, fs_ref, sm_ref, sn_ref
):
    rows = p_ref.shape[1]
    own = rows - 2 * HALO
    tile, last_tile = where[1], where[2] - 1
    live = interior(where)
    kept = scal_ref[...]
    tau, pull = kept[0, 0], kept[1, 0]
    step = step_of(all_ref, cells) * live
    advance(
        h_ref, -step, (p_ref, m0_ref, n0_ref, lm0_ref, ln0_ref), 0,
        (phi_ref, m_ref, n_ref, None, None), coef_ref,
        (fa_ref, fb_ref, fs_ref, sm_ref, sn_ref), HALO - 1, HALO + own + 1, False,
    )
    clear_outside(tile, last_tile, (fa_ref, fb_ref, fs_ref), own)
    _, inside = gradients(
        phi_ref, m_ref, n_ref, coef_ref, fa_ref, fb_ref, fs_ref, sm_ref, sn_ref, g_ref, tau, pull,
        HALO,
    )
    total = loop(HALO, HALO + own, inside, jnp.zeros((8, 128), jnp.float32))
    sums = jnp.sum(total, axis=0, keepdims=True) * live
    sums_ref[...] = jnp.broadcast_to(sums, sums_ref.shape)


def last_kernel(cells, where, all_ref, p_ref, g_ref, edge_ref, mid_ref):
    own = g_ref.shape[1]
    step = step_of(all_ref, cells) * interior(where)
    for ref, low, high, shift in (
        (edge_ref, 0, HALO, 0),
        (mid_ref, HALO, own - HALO, HALO),
        (edge_ref, own - HALO, own, own - 2 * HALO),
    ):

        def move(at, carry, ref=ref, shift=shift):
            for comp in range(3):
                for place in TILES:
                    old = tile_of(p_ref, comp, at + HALO, place)
                    put(ref, comp, at - shift, place, old - step * tile_of(g_ref, comp, at, place))
            return carry

        loop(low, high, move)


def blocks(shape):
    depth, own, width = shape
    return [
        (z, x, slice(z, z + 8), slice(x, x + 8), slice(y, y + 128))
        for z in range(0, depth, 8)
        for x in range(0, own, 8)
        for y in range(0, width, 128)
    ]


def slabs(source, target, sems):
    found = {}
    for comp in range(3):
        for z in range(0, source.shape[1], 8):
            part = comp, pl.ds(z, 8)
            found[comp, z] = pltpu.make_async_copy(
                source.at[part], target.at[part], sems.at[comp, z // 8]
            )
    return found


def prep_kernel(where, raw_ref, edge_ref, mid_ref):
    own = raw_ref.shape[2]
    for comp in range(3):
        for _, x, zs, xs, ys in blocks(raw_ref.shape[1:]):
            cells = jnp.swapaxes(raw_ref[comp, zs, xs, ys], 0, 1)
            for i in range(8):
                ref, at = edge_ref, x + i
                if HALO <= at < own - HALO:
                    ref, at = mid_ref, at - HALO
                elif at >= own - HALO:
                    at = at - (own - 2 * HALO)
                ref[comp, at, zs, ys] = cells[i]


def final_kernel(cells, where, all_ref, p_ref, g_ref, output_ref, out_ref, sems):
    step = step_of(all_ref, cells) * interior(where)
    copies = slabs(out_ref, output_ref, sems)
    own, width = out_ref.shape[2:]
    for comp in range(3):
        for z, x, zs, xs, ys in blocks(out_ref.shape[1:]):
            old = p_ref[comp, HALO + x : HALO + x + 8, zs, ys]
            new = old - step * g_ref[comp, xs, zs, ys]
            out_ref[comp, zs, xs, ys] = jnp.swapaxes(new, 0, 1)
            if x == own - 8 and ys.stop == width:
                copies[comp, z].start()
    for copy in copies.values():
        copy.wait()


def f32(*shape):
    return jax.ShapeDtypeStruct(shape, jnp.float32)


def position():
    found = []
    for axes in (IMG, TILE):
        index = 0
        for axis in axes:
            index = index * lax.axis_size(axis) + lax.axis_index(axis)
        found.append(index)
    return (*found, lax.axis_size(TILE), lax.axis_size(IMG))


def call(kernel, operands, outs, scratch, hbm_out=False):
    vmem, hbm = pl.BlockSpec(memory_space=pltpu.VMEM), pl.BlockSpec(memory_space=pltpu.HBM)
    return pl.pallas_call(
        lambda *refs: kernel(position(), *refs),
        out_shape=outs,
        in_specs=[vmem] * len(operands),
        out_specs=[hbm if hbm_out else vmem] * len(outs),
        scratch_shapes=[
            pltpu.VMEM(shape, jnp.float32) if isinstance(shape, tuple) else shape
            for shape in scratch
        ],
        compiler_params=pltpu.CompilerParams(vmem_limit_bytes=VMEM_LIMIT),
    )(*operands)


def beside(cells, axis, forward):
    count = lax.axis_size(axis)
    pairs = [(i, i + 1) if forward else (i + 1, i) for i in range(count - 1)]
    return lax.ppermute(cells, axis, pairs)


def from_everyone(rows):
    return lax.all_to_all(rows, IMG_TILE, 0, 0, tiled=True)


def body(spins, aniso):
    _, comps, depth, own, width = spins.shape
    images, tiles = lax.axis_size(IMG), lax.axis_size(TILE)
    devices = images * tiles
    cells = float(images * comps * depth * own * tiles * width)
    rows = own + 2 * HALO
    coefs = jnp.swapaxes(aniso, 0, 1)
    moved = [spins.shape[1:], pltpu.SemaphoreType.DMA((3, depth // 8))]
    edge, mid = call(
        prep_kernel,
        [spins[0]],
        [f32(3, 2 * HALO, depth, width), f32(3, own - 2 * HALO, depth, width)],
        [],
    )
    ext = (3, rows, depth, width)
    ends, middle = (3, 4 * HALO, depth, width), (3, own - 4, depth, width)
    whole = f32(*ext)
    table = f32(devices, 128)
    coef_ext = None

    def scratch(count):
        return [(3, count, depth, width)] * 3 + [(count, depth, width)] * 2

    for outer in range(OUTER):
        a_edge, b_edge = beside(edge, IMG, True), beside(edge, IMG, False)
        a_mid, b_mid = beside(mid, IMG, True), beside(mid, IMG, False)
        bottom, top = edge[:, HALO:], edge[:, :HALO]
        if coef_ext is None:
            bottom = jnp.concatenate([bottom, coefs[None, own - HALO :]])
            top = jnp.concatenate([top, coefs[None, :HALO]])
        up_own, down_own = beside(bottom, TILE, True), beside(top, TILE, False)
        a_edge, b_edge, up_own, down_own = lax.optimization_barrier((a_edge, b_edge, up_own, down_own))
        up = beside(jnp.concatenate([a_edge[:, HALO:], b_edge[:, HALO:]]), TILE, True)
        down = beside(jnp.concatenate([a_edge[:, :HALO], b_edge[:, :HALO]]), TILE, False)
        shapes = [f32(*ends)] * 7 + [f32(PRODUCTS, 8, 128)]
        if coef_ext is None:
            *far, part, coef_ext = call(
                first_ends_kernel,
                [edge, a_edge, b_edge, up_own, down_own, up, down, coefs],
                [*shapes, f32(*ext[1:])],
                scratch(2 * HALO),
            )
        else:
            *far, part = call(
                ends_kernel,
                [edge, a_edge, b_edge, up_own, down_own, up, down, coef_ext],
                shapes,
                scratch(2 * HALO),
            )
        phi, n, ln, fb, sn = call(
            ahead_kernel,
            [mid, b_mid, far[0], far[2], coef_ext],
            [f32(*middle)] * 4 + [f32(*middle[1:])],
            [],
        )
        m, lm, q, r, sums = call(
            middle_kernel,
            [mid, a_mid, far[1], phi, n, fb, sn, part, coef_ext],
            [f32(*middle)] * 4 + [table],
            [middle, middle, middle[1:]],
        )
        near = phi, m, n, lm, ln, q, r
        phi, m, n, lm, ln, g, scal, sums = call(
            lambda *refs: second_kernel(tiles, cells, *refs),
            [from_everyone(sums), *far, *near, coef_ext],
            [whole] * 6 + [f32(8, 128), table],
            [ext, *scratch(rows)],
        )
        phi, g, sums = call(
            lambda *refs: third_kernel(cells, *refs),
            [scal, from_everyone(sums), phi, m, n, lm, ln, g, coef_ext],
            [whole, f32(3, own, depth, width), table],
            [ext, ext, *scratch(rows)],
        )
        sums = from_everyone(sums)
        if outer == OUTER - 1:
            (path,) = call(
                lambda *refs: final_kernel(cells, *refs),
                [sums, phi, g],
                [f32(*spins.shape[1:])],
                moved,
                hbm_out=True,
            )
            return path[None]
        edge, mid = call(
            lambda *refs: last_kernel(cells, *refs),
            [sums, phi, g],
            [f32(3, 2 * HALO, depth, width), f32(3, own - 2 * HALO, depth, width)],
            [],
        )


def solution(mesh):
    split = Mesh(mesh.devices.reshape(4, 4, 4, 2), IMG_TILE)
    return jax.shard_map(
        body,
        mesh=split,
        in_specs=(P(IMG, None, None, TILE, None), P(None, TILE, None)),
        out_specs=P(IMG, None, None, TILE, None),
        check_vma=False,
    )
```
